32 devices in a mesh: dp: 4 (over z), sp: 8 (over y, x, core).
Axes of the slice: x: 2, y: 2, z: 4, core: 2. Of those that a mesh axis runs over, the one named last changes fastest.
Arguments:
- tokens: bfloat16 [4096, 2048], P(('dp', 'sp')), may hold values from -6 to 6
- doc_lengths: int32 [4, 4], P('dp'), may hold values from 1 to 1020, as said below
- w_query: bfloat16 [2048, 2048], P('sp'), may hold values from -0.15625 to 0.15625
- w_key: bfloat16 [2048, 512], P('sp'), may hold values from -0.15625 to 0.15625
- w_value: bfloat16 [2048, 512], P('sp'), may hold values from -0.125 to 0.125
- w_out: bfloat16 [2048, 2048], P('sp'), may hold values from -0.75 to 0.75
- gain_attn: bfloat16 [2048], P('sp'), may hold values from 0.5 to 1.5
- gain_mlp: bfloat16 [2048], P('sp'), may hold values from 0.5 to 1.5
- w_gate: bfloat16 [2048, 8192], P(None, 'sp'), may hold values from -0.125 to 0.125
- w_up: bfloat16 [2048, 8192], P(None, 'sp'), may hold values from -0.125 to 0.125
- w_down: bfloat16 [8192, 2048], P('sp'), may hold values from -0.0625 to 0.0625
- cotangent: bfloat16 [4096, 2048], P(('dp', 'sp')), may hold values from -6 to 6
Outputs:
- layer_out: bfloat16 [4096, 2048], P(('dp', 'sp'))
- grad_tokens: float32 [4096, 2048], P(('dp', 'sp'))
- grad_query: float32 [2048, 2048], P('sp')
- grad_key: float32 [2048, 512], P('sp')
- grad_value: float32 [2048, 512], P('sp')
- grad_out: float32 [2048, 2048], P('sp')
- grad_gain_attn: float32 [2048], P('sp')
- grad_gain_mlp: float32 [2048], P('sp')
- grad_gate: float32 [2048, 8192], P(None, 'sp')
- grad_up: float32 [2048, 8192], P(None, 'sp')
- grad_down: float32 [8192, 2048], P('sp')
The draws below stay inside these ranges and needn't reach their ends.
Inputs may be any that keep to these rules, and one draw needn't show every extreme that they name: `doc_lengths`: each row gives the lengths of the 4 documents packed in order into one micro-batch of 1024 tokens; a row sums to 1024.
All inputs are finite; a program needn't handle non-finite values.
Results may differ from the reference program's by a relative error of at most 0.022.
Values may be sent and summed in bfloat16 or wider, within the bound.
No kernel may reach another device: no remote copies, remote signals or barrier semaphores. Data moves between devices by JAX's collectives and lax.ppermute only.
A program may use at most 192 MiB of HBM per device.

```python
import jax
import jax.numpy as jnp
from jax import lax

D = 2048
H = 32
KV = 8
HD = 64
FF = 8192
TOK_DEV = 128
BLOCK = 512
GROUPS = 4
GROUP_TOK = 1024
TOKENS = 4096
N_SP = 8


def draw_doc_lengths(key, part):
    key = jax.random.fold_in(key, 7)
    subkeys = jax.random.split(key, 6)
    front_count = jax.random.randint(subkeys[0], (GROUPS,), 1, 3)
    front_total = jax.random.randint(subkeys[1], (GROUPS,), 2, TOK_DEV)
    back_total = jax.random.randint(subkeys[2], (GROUPS,), 2, TOK_DEV)
    picked = jax.random.randint(subkeys[5], (), 0, GROUPS)
    forced = jnp.arange(GROUPS, dtype=jnp.int32) == picked
    front_total = jnp.where(forced, 2, front_total)
    back_total = jnp.where(forced, 2, back_total)
    front_cut = jax.random.randint(subkeys[3], (GROUPS,), 1, front_total)
    back_cut = jax.random.randint(subkeys[4], (GROUPS,), 1, back_total)
    longest = GROUP_TOK - front_total - back_total
    one_front = jnp.stack([front_total, longest, back_cut, back_total - back_cut], axis=1)
    two_front = jnp.stack([front_cut, front_total - front_cut, longest, back_total], axis=1)
    return jnp.where((front_count == 1)[:, None], one_front, two_front).astype(jnp.int32)


def block_scale(rng, extent, cuts, smallest, largest):
    level, own = 1.0, jax.random.fold_in(rng, 6)
    for dim, parts in cuts:
        steps = jnp.exp(jax.random.uniform(jax.random.fold_in(own, dim), (parts,), jnp.float32, smallest / len(cuts), largest / len(cuts)))
        level = level * jnp.repeat(steps, extent[dim] // parts).reshape([-1 if axis == dim else 1 for axis in range(len(extent))])
    return level


def normal_values(stream_key, dims, spread, most, cuts=(), kind=jnp.bfloat16):
    array = jax.random.normal(stream_key, dims, jnp.float32) * spread
    if len(cuts) > 0:
        array = block_scale(stream_key, dims, cuts, -0.22, 0.18) * array
    return jnp.clip(array, min=-most, max=most).astype(kind)


def setup_inputs(seed: int = 0) -> dict:
    key_of = jax.random.split(jax.random.key(seed), 13)
    return {
        "tokens": normal_values(key_of[0], (TOKENS, D), 1.0, 6.0, ((0, 32),)),
        "doc_lengths": draw_doc_lengths(jax.random.fold_in(key_of[12], 71), 0),
        "w_query": normal_values(key_of[2], (D, H * HD), (D * 2 // 3) ** -0.5, 0.15625, ((0, 8),)),
        "w_key": normal_values(key_of[3], (D, KV * HD), (D * 2 // 3) ** -0.5, 0.15625, ((0, 8),)),
        "w_value": normal_values(key_of[4], (D, KV * HD), D ** -0.5, 0.125, ((0, 8),)),
        "w_out": normal_values(key_of[5], (H * HD, D), HD ** -0.5, 0.75, ((0, 8),)),
        "gain_attn": jnp.clip(1.0 + 0.1 * jax.random.normal(key_of[6], (D,), jnp.float32), 0.5, 1.5).astype(jnp.bfloat16),
        "gain_mlp": jnp.clip(1.0 + 0.1 * jax.random.normal(key_of[7], (D,), jnp.float32), 0.5, 1.5).astype(jnp.bfloat16),
        "w_gate": normal_values(key_of[8], (D, FF), D ** -0.5, 0.125, ((1, 8),)),
        "w_up": normal_values(key_of[9], (D, FF), D ** -0.5, 0.125, ((1, 8),)),
        "w_down": normal_values(key_of[10], (FF, D), FF ** -0.5, 0.0625, ((0, 8),)),
        "cotangent": normal_values(key_of[11], (TOKENS, D), 1.0, 6.0, ((0, 32),)),
    }


EPS = 1e-05
THETA = 500000.0
FACTOR = 32.0
LOW_FACTOR = 1.0
HIGH_FACTOR = 4.0
BASE_CONTEXT = 8192.0
MASKED = -1e+30

@jax.custom_vjp
def low(v):
    return lax.optimization_barrier(v.astype(jnp.bfloat16)).astype(jnp.float32)

@jax.custom_vjp
def low_back(v):
    return v

def low_keep(v):
    return (low(v), None)

def low_pass(kept, grad):
    return (grad,)

def back_keep(v):
    return (v, None)

def back_low(kept, grad):
    return (low(grad),)
low.defvjp(low_keep, low_pass)
low_back.defvjp(back_keep, back_low)

def frequencies():
    half_index = jnp.arange(HD // 2).astype(jnp.float32)
    inverse = THETA ** (-2.0 * half_index / HD)
    wavelength = 2.0 * jnp.pi / inverse
    smooth = (BASE_CONTEXT / wavelength - LOW_FACTOR) / (HIGH_FACTOR - LOW_FACTOR)
    middle = (1.0 - smooth) * inverse / FACTOR + smooth * inverse
    slow_band = jnp.where(wavelength > BASE_CONTEXT / LOW_FACTOR, inverse / FACTOR, middle)
    return jnp.where(wavelength < BASE_CONTEXT / HIGH_FACTOR, inverse, slow_band)

def doc_layout(lengths, first_row, row_total):
    ends_at = jnp.cumsum(lengths).astype(jnp.int32)
    starts_at = (ends_at - lengths).astype(jnp.int32)
    places = first_row + jnp.arange(row_total, dtype=jnp.int32)
    documents = lax.optimization_barrier(jnp.sum((places[:, None] >= ends_at[None, :]).astype(jnp.int32), axis=1)).astype(jnp.int32)
    begins = lax.optimization_barrier(jnp.max(jnp.where(starts_at[None, :] <= places[:, None], starts_at[None, :], 0), axis=1)).astype(jnp.int32)
    return (documents, places, places - begins)

def rotation(positions):
    angles = positions.astype(jnp.float32)[:, None] * frequencies()[None, :]
    cosine_table = jnp.concatenate([jnp.cos(angles), jnp.cos(angles)], axis=1)
    sine_table = jnp.concatenate([jnp.sin(angles), jnp.sin(angles)], axis=1)
    return (cosine_table, sine_table)

def rotate_half(values):
    middle = values.shape[-1] // 2
    return jnp.concatenate([-values[..., middle:], values[..., :middle]], axis=-1)

def apply_rope(values, cosine_table, sine_table):
    return values * cosine_table[:, None, :] + rotate_half(values) * sine_table[:, None, :]

def rms_norm(values, gain):
    inverse = lax.rsqrt(lax.optimization_barrier(jnp.mean(values * values, axis=-1, keepdims=True)) + EPS)
    return values * inverse * gain

def product(left, right):
    return jnp.dot(left, right, precision=lax.Precision.HIGHEST, preferred_element_type=jnp.float32)

def layer_forward(inputs, w_query, w_key, w_value, w_out, gain_attn, gain_mlp, w_gate, w_up, w_down, documents, places, positions):
    row_total = inputs.shape[0]
    copies = max(1, N_SP // KV)
    share_heads = H // (KV * copies)
    score_scale = HD ** (-0.5)
    cosine_table, sine_table = rotation(positions)
    act_one = low(rms_norm(inputs, gain_attn))
    query_pre = low_back(product(act_one, w_query)).reshape(row_total, H, HD)
    key_pre = low_back(product(act_one, w_key)).reshape(row_total, KV, HD)
    value_pre = low_back(product(act_one, w_value)).reshape(row_total, KV, HD)
    query_rot = low_back(low(apply_rope(query_pre, cosine_table, sine_table)))
    key_rot = low_back(low(jnp.repeat(apply_rope(key_pre, cosine_table, sine_table), copies, axis=1)))
    value_rep = low_back(low(jnp.repeat(value_pre, copies, axis=1)))
    key_heads = jnp.repeat(key_rot, share_heads, axis=1)
    value_heads = jnp.repeat(value_rep, share_heads, axis=1)

    def one_block(block_args):
        query_block, block_docs, block_places = block_args
        scores = jnp.einsum('qhd,khd->hqk', query_block, key_heads, precision=lax.Precision.HIGHEST, preferred_element_type=jnp.float32) * score_scale
        scores = low_back(scores)
        allowed = (block_docs[:, None] == documents[None, :]) & (places[None, :] <= block_places[:, None])
        scores = jnp.where(allowed[None], scores, MASKED)
        shifted = jnp.exp(scores - lax.optimization_barrier(jnp.max(scores, axis=2, keepdims=True)))
        weights = low(shifted / lax.optimization_barrier(jnp.sum(shifted, axis=2, keepdims=True)))
        return jnp.einsum('hqk,khd->qhd', weights, value_heads, precision=lax.Precision.HIGHEST, preferred_element_type=jnp.float32)
    blocks = row_total // BLOCK
    attended = lax.map(jax.checkpoint(one_block), (query_rot.reshape(blocks, BLOCK, H, HD), documents.reshape(blocks, BLOCK), places.reshape(blocks, BLOCK)))
    attn_heads = low_back(low(attended.reshape(row_total, H * HD)))
    hidden_one = inputs + low_back(product(attn_heads, w_out))
    act_two = low(rms_norm(hidden_one, gain_mlp))
    gate_value = low_back(product(act_two, w_gate))
    up_value = low_back(product(act_two, w_up))
    hidden = low(jax.nn.silu(gate_value) * up_value)
    return hidden_one + low_back(product(hidden, w_down))

def reference(tokens, doc_lengths, w_query, w_key, w_value, w_out, gain_attn, gain_mlp, w_gate, w_up, w_down, cotangent):
    weights = (w_query, w_key, w_value, w_out, gain_attn, gain_mlp, w_gate, w_up, w_down)
    weights = tuple((weight.astype(jnp.float32) for weight in weights))
    inputs = tokens.astype(jnp.float32).reshape(GROUPS, GROUP_TOK, D)
    cotangents = cotangent.astype(jnp.float32).reshape(GROUPS, GROUP_TOK, D)

    def group_step(running, group_batch):
        group_inputs, group_cotangent, lengths = group_batch
        documents, places, positions = doc_layout(lengths, jnp.int32(0), GROUP_TOK)

        def forward(values, p_query, p_key, p_value, p_out, p_gain_attn, p_gain_mlp, p_gate, p_up, p_down):
            return layer_forward(values, p_query, p_key, p_value, p_out, p_gain_attn, p_gain_mlp, p_gate, p_up, p_down, documents, places, positions)
        outputs, pullback = jax.vjp(forward, group_inputs, weights[0], weights[1], weights[2], weights[3], weights[4], weights[5], weights[6], weights[7], weights[8])
        gradients = pullback(group_cotangent)
        running = tuple((summed + gradient for summed, gradient in zip(running, gradients[1:])))
        return (running, (outputs.astype(jnp.bfloat16), gradients[0]))
    initial = tuple((jnp.zeros(weight.shape, jnp.float32) for weight in weights))
    totals, (outputs, input_grads) = lax.scan(group_step, initial, (inputs, cotangents, doc_lengths))
    return (outputs.reshape(TOKENS, D), input_grads.reshape(TOKENS, D), totals[0], totals[1], totals[2], totals[3], totals[4], totals[5], totals[6], totals[7], totals[8])
```

```python
import jax
import jax.numpy as jnp
from jax import lax
from jax.sharding import PartitionSpec as P

HD = 64
BLOCK = 512


EPS = 1e-05
THETA = 500000.0
FACTOR = 32.0
LOW_FACTOR = 1.0
HIGH_FACTOR = 4.0
BASE_CONTEXT = 8192.0
MASKED = -1e30


def frequencies(head_size):
    half_index = jnp.arange(head_size // 2).astype(jnp.float32)
    inverse = THETA ** (-2.0 * half_index / head_size)
    wavelength = 2.0 * jnp.pi / inverse
    smooth = (BASE_CONTEXT / wavelength - LOW_FACTOR) / (HIGH_FACTOR - LOW_FACTOR)
    middle = (1.0 - smooth) * inverse / FACTOR + smooth * inverse
    slow_band = jnp.where(wavelength > BASE_CONTEXT / LOW_FACTOR, inverse / FACTOR, middle)
    return jnp.where(wavelength < BASE_CONTEXT / HIGH_FACTOR, inverse, slow_band)


def doc_layout(lengths, first_row, row_total):
    count = lengths.shape[0]
    upto = jnp.arange(count)[None, :] <= jnp.arange(count)[:, None]
    ends_at = jnp.sum(jnp.where(upto, lengths[None, :], 0), axis=1)
    starts_at = ends_at - lengths
    places = first_row + jnp.arange(row_total, dtype=jnp.int32)
    documents = jnp.sum((places[:, None] >= ends_at[None, :]).astype(jnp.int32), axis=1)
    begins = jnp.max(
        jnp.where(starts_at[None, :] <= places[:, None], starts_at[None, :], 0), axis=1
    )
    return (documents, places, places - begins)


def rotation(positions, head_size):
    angles = positions.astype(jnp.float32)[:, None] * frequencies(head_size)[None, :]
    cosine_table = jnp.concatenate([jnp.cos(angles), jnp.cos(angles)], axis=1)
    sine_table = jnp.concatenate([jnp.sin(angles), jnp.sin(angles)], axis=1)
    return (cosine_table, sine_table)


def rotate_half(values):
    middle = values.shape[-1] // 2
    return jnp.concatenate([-values[..., middle:], values[..., :middle]], axis=-1)


def apply_rope(values, cosine_table, sine_table):
    return values * cosine_table[:, None, :] + rotate_half(values) * sine_table[:, None, :]


def rope_back(gradients, cosine_table, sine_table):
    return gradients * cosine_table[:, None, :] - rotate_half(gradients) * sine_table[:, None, :]


def contract(left, right, left_dim, right_dim):
    return lax.dot_general(
        left, right, (((left_dim,), (right_dim,)), ((), ())), preferred_element_type=jnp.float32
    )


def block_rows(array, documents, block_index, heads):
    first_row = block_index * BLOCK
    row_block = lax.dynamic_slice_in_dim(array, first_row, BLOCK, 0).reshape(BLOCK, heads, HD)
    block_docs = lax.dynamic_slice_in_dim(documents, first_row, BLOCK, 0)
    places = first_row + jnp.arange(BLOCK, dtype=jnp.int32)
    return (row_block, block_docs, places)


def masked_scores(
    query_block, key_wide, query_docs, key_docs, query_places, key_places, score_scale
):
    scores = (
        jnp.einsum("qhd,khd->hqk", query_block, key_wide, preferred_element_type=jnp.float32)
        * score_scale
    )
    allowed = (query_docs[:, None] == key_docs[None, :]) & (
        key_places[None, :] <= query_places[:, None]
    )
    return jnp.where(allowed[None], scores, MASKED)


def add_block(whole, piece, block_index):
    current = lax.dynamic_slice_in_dim(whole, block_index * BLOCK, BLOCK, 0)
    return lax.dynamic_update_slice_in_dim(whole, current + piece, block_index * BLOCK, 0)


def attend(query_heads, key_heads, value_heads, documents, score_scale):
    total_rows = query_heads.shape[0]
    local_heads = query_heads.shape[1] // HD
    local_kv = key_heads.shape[1] // HD
    repeats = local_heads // local_kv
    blocks = total_rows // BLOCK

    def query_loop(block_index, carried):
        outputs, log_sums = carried
        query_block, query_docs, query_places = block_rows(
            query_heads, documents, block_index, local_heads
        )

        def scores_at(key_index):
            key_block, key_docs, key_places = block_rows(key_heads, documents, key_index, local_kv)
            return masked_scores(
                query_block,
                jnp.repeat(key_block, repeats, axis=1),
                query_docs,
                key_docs,
                query_places,
                key_places,
                score_scale,
            )

        def first_pass(key_index, running):
            running_max, running_sum = running
            scores = scores_at(key_index)
            new_max = jnp.maximum(running_max, jnp.max(scores, axis=2))
            running_sum = running_sum * jnp.exp(running_max - new_max) + jnp.sum(
                jnp.exp(scores - new_max[:, :, None]), axis=2
            )
            return (new_max, running_sum)

        initial = (
            jnp.full((local_heads, BLOCK), MASKED, jnp.float32),
            jnp.zeros((local_heads, BLOCK), jnp.float32),
        )
        running_max, running_sum = lax.fori_loop(0, block_index + 1, first_pass, initial)
        log_sum = running_max + jnp.log(running_sum)

        def second_pass(key_index, accumulated):
            value_block, _, _ = block_rows(value_heads, documents, key_index, local_kv)
            block_probs = jnp.exp(scores_at(key_index) - log_sum[:, :, None]).astype(jnp.bfloat16)
            return accumulated + jnp.einsum(
                "hqk,khd->qhd",
                block_probs,
                jnp.repeat(value_block, repeats, axis=1),
                preferred_element_type=jnp.float32,
            )

        block_out = lax.fori_loop(
            0, block_index + 1, second_pass, jnp.zeros((BLOCK, local_heads, HD), jnp.float32)
        )
        outputs = lax.dynamic_update_slice_in_dim(
            outputs,
            block_out.reshape(BLOCK, local_heads * HD).astype(jnp.bfloat16),
            block_index * BLOCK,
            0,
        )
        log_sums = lax.dynamic_update_slice_in_dim(log_sums, log_sum, block_index * BLOCK, 1)
        return (outputs, log_sums)

    initial = (
        jnp.zeros((total_rows, local_heads * HD), jnp.bfloat16),
        jnp.zeros((local_heads, total_rows), jnp.float32),
    )
    return lax.fori_loop(0, blocks, query_loop, initial)


def attend_back(query_heads, key_heads, value_heads, heads_back, log_sums, documents, score_scale):
    total_rows = query_heads.shape[0]
    local_heads = query_heads.shape[1] // HD
    local_kv = key_heads.shape[1] // HD
    repeats = local_heads // local_kv
    blocks = total_rows // BLOCK

    def query_loop(block_index, carried):
        query_grads, key_grads, value_grads = carried
        query_block, query_docs, query_places = block_rows(
            query_heads, documents, block_index, local_heads
        )
        back_block, _, _ = block_rows(heads_back, documents, block_index, local_heads)
        log_sum = lax.dynamic_slice_in_dim(log_sums, block_index * BLOCK, BLOCK, 1)

        def probs_at(key_index):
            key_block, key_docs, key_places = block_rows(key_heads, documents, key_index, local_kv)
            value_block, _, _ = block_rows(value_heads, documents, key_index, local_kv)
            key_wide = jnp.repeat(key_block, repeats, axis=1)
            value_wide = jnp.repeat(value_block, repeats, axis=1)
            scores = masked_scores(
                query_block, key_wide, query_docs, key_docs, query_places, key_places, score_scale
            )
            block_probs = jnp.exp(scores - log_sum[:, :, None])
            probs_back = jnp.einsum(
                "qhd,khd->hqk", back_block, value_wide, preferred_element_type=jnp.float32
            )
            return (block_probs, probs_back, key_wide)

        def delta_pass(key_index, accumulated):
            block_probs, probs_back, _ = probs_at(key_index)
            return accumulated + jnp.sum(block_probs * probs_back, axis=2)

        delta = lax.fori_loop(
            0, block_index + 1, delta_pass, jnp.zeros((local_heads, BLOCK), jnp.float32)
        )

        def grad_pass(key_index, inner):
            query_sum, key_whole, value_whole = inner
            block_probs, probs_back, key_wide = probs_at(key_index)
            scores_back = (block_probs * (probs_back - delta[:, :, None])).astype(jnp.bfloat16)
            query_sum = (
                query_sum
                + jnp.einsum(
                    "hqk,khd->qhd", scores_back, key_wide, preferred_element_type=jnp.float32
                )
                * score_scale
            )
            key_piece = (
                jnp.einsum(
                    "hqk,qhd->khd", scores_back, query_block, preferred_element_type=jnp.float32
                )
                * score_scale
            )
            value_piece = jnp.einsum(
                "hqk,qhd->khd",
                block_probs.astype(jnp.bfloat16),
                back_block,
                preferred_element_type=jnp.float32,
            )
            key_whole = add_block(
                key_whole, key_piece.reshape(BLOCK, local_kv, repeats, HD).sum(axis=2), key_index
            )
            value_whole = add_block(
                value_whole,
                value_piece.reshape(BLOCK, local_kv, repeats, HD).sum(axis=2),
                key_index,
            )
            return (query_sum, key_whole, value_whole)

        query_sum, key_grads, value_grads = lax.fori_loop(
            0,
            block_index + 1,
            grad_pass,
            (jnp.zeros((BLOCK, local_heads, HD), jnp.float32), key_grads, value_grads),
        )
        query_grads = lax.dynamic_update_slice_in_dim(
            query_grads,
            query_sum.reshape(BLOCK, local_heads * HD).astype(jnp.bfloat16),
            block_index * BLOCK,
            0,
        )
        return (query_grads, key_grads, value_grads)

    initial = (
        jnp.zeros((total_rows, local_heads * HD), jnp.bfloat16),
        jnp.zeros((total_rows, local_kv, HD), jnp.float32),
        jnp.zeros((total_rows, local_kv, HD), jnp.float32),
    )
    query_grads, key_grads, value_grads = lax.fori_loop(0, blocks, query_loop, initial)
    return (
        query_grads,
        key_grads.reshape(total_rows, local_kv * HD).astype(jnp.bfloat16),
        value_grads.reshape(total_rows, local_kv * HD).astype(jnp.bfloat16),
    )


def swap(values, distance, axis):
    size = lax.axis_size(axis)
    return lax.ppermute(values, axis, [(i, i ^ distance) for i in range(size)])


def block_order(shards):
    return list(range(0, shards, 2)) + list(range(1, shards, 2))


def gather_rel(values):
    shards = lax.axis_size("sp")
    if shards == 8:
        half = values.shape[0] // 2
        near = swap(values, 2, "sp")
        next_row = swap(values, 4, "sp")
        far = jnp.concatenate(
            [swap(near[:half], 4, "sp"), swap(next_row[half:], 2, "sp")], axis=0
        )
        evens = [values, near, next_row, far]
    else:
        evens = [values]
        distance = 2
        while distance < shards:
            evens = evens + [swap(block, distance, "sp") for block in evens]
            distance *= 2
    return evens + [swap(block, 1, "sp") for block in evens]


def scatter_rel(even_terms, odd_terms):
    shards = lax.axis_size("sp")
    rows = even_terms.shape[0] // (shards // 2)
    width = even_terms.shape[1]
    got = swap(odd_terms.astype(jnp.bfloat16), 1, "sp")
    sums = (even_terms + got.astype(jnp.float32)).reshape(shards // 2, rows, width)
    if shards == 8:
        half = rows // 2
        far = sums[3].astype(jnp.bfloat16)
        to_next = swap(far[:half], 2, "sp").astype(jnp.float32)
        to_near = swap(far[half:], 4, "sp").astype(jnp.float32)
        near = jnp.concatenate([sums[1][:half], sums[1][half:] + to_near], axis=0)
        next_row = jnp.concatenate([sums[2][:half] + to_next, sums[2][half:]], axis=0)
        return (
            sums[0]
            + swap(near.astype(jnp.bfloat16), 2, "sp").astype(jnp.float32)
            + swap(next_row.astype(jnp.bfloat16), 4, "sp").astype(jnp.float32)
        )
    distance = shards // 2
    while distance > 1:
        kept = distance // 2
        sums = sums[:kept] + swap(sums[kept:].astype(jnp.bfloat16), distance, "sp").astype(
            jnp.float32
        )
        distance //= 2
    return sums[0]


def reorder(values, seq_rank):
    shards = lax.axis_size("sp")
    order = block_order(shards)
    rows = values.shape[0] // shards
    return jnp.concatenate(
        [
            lax.dynamic_slice_in_dim(values, (seq_rank ^ distance) * rows, rows, 0)
            for distance in order
        ],
        axis=0,
    )


def to_token_order(values, seq_rank):
    shards = lax.axis_size("sp")
    order = block_order(shards)
    place = jnp.asarray([order.index(k) for k in range(shards)], jnp.int32)
    rows = values.shape[0] // shards
    return jnp.concatenate(
        [
            lax.dynamic_slice_in_dim(values, place[seq_rank ^ index] * rows, rows, 0)
            for index in range(shards)
        ],
        axis=0,
    )


def dp_scatter(terms):
    groups = lax.axis_size("dp")
    rank = lax.axis_index("dp")
    total = lax.dynamic_index_in_dim(terms, rank, 0, keepdims=False)
    for distance in range(1, groups):
        piece = lax.dynamic_index_in_dim(terms, rank ^ distance, 0, keepdims=False)
        total = total + swap(piece.astype(jnp.bfloat16), distance, "dp").astype(jnp.float32)
    return total


def dp_gather(piece):
    groups = lax.axis_size("dp")
    rank = lax.axis_index("dp")
    whole = jnp.zeros((groups,) + piece.shape, piece.dtype)
    for distance in range(groups):
        block = piece if distance == 0 else swap(piece, distance, "dp")
        whole = lax.dynamic_update_index_in_dim(whole, block, rank ^ distance, 0)
    return whole


def sum_all(values):
    for axis in ("sp", "dp"):
        distance = 1
        while distance < lax.axis_size(axis):
            values = values + swap(values, distance, axis)
            distance *= 2
    return values


def silu_parts(gate_value):
    sigmoid_gate = jax.nn.sigmoid(gate_value)
    return sigmoid_gate, gate_value * sigmoid_gate


def feed_forward(act_rows, cot_rows, w_gate, w_up, w_down):
    gate_value = jnp.dot(act_rows, w_gate, preferred_element_type=jnp.float32)
    up_value = jnp.dot(act_rows, w_up, preferred_element_type=jnp.float32)
    hidden_back = contract(cot_rows, w_down, 1, 1)
    sigmoid_gate, silu_gate = silu_parts(gate_value)
    hidden = (silu_gate * up_value).astype(jnp.bfloat16)
    gate_back = (
        hidden_back * up_value * sigmoid_gate * (1.0 + gate_value * (1.0 - sigmoid_gate))
    ).astype(jnp.bfloat16)
    up_back = (hidden_back * silu_gate).astype(jnp.bfloat16)
    return hidden, gate_back, up_back


def on_device(
    tokens,
    doc_lengths,
    w_query,
    w_key,
    w_value,
    w_out,
    gain_attn,
    gain_mlp,
    w_gate,
    w_up,
    w_down,
    cotangent,
):
    shards = lax.axis_size("sp")
    groups = lax.axis_size("dp")
    seq_rank = lax.axis_index("sp")
    tok_rows, width = tokens.shape
    group_rows = tok_rows * shards
    heads_total = w_query.shape[1] // HD
    kv_total = w_key.shape[1] // HD
    copies = max(1, shards // kv_total)
    q_cols = heads_total // shards * HD
    kv_cols = kv_total * copies // shards * HD
    part_rows = w_query.shape[0]
    score_scale = HD ** (-0.5)
    lengths = doc_lengths[0]
    documents, _, positions = doc_layout(lengths, jnp.int32(0), group_rows)
    cosine_table, sine_table = rotation(positions, HD)

    token_rows = jnp.concatenate(gather_rel(tokens), axis=0)

    def repeat_heads(weight):
        rows = weight.shape[0]
        return jnp.repeat(weight.reshape(rows, kv_total, 1, HD), copies, axis=2).reshape(
            rows, shards, kv_cols
        )

    w_mixed = jnp.concatenate(
        [
            w_query.reshape(part_rows, shards, q_cols),
            repeat_heads(w_key),
            repeat_heads(w_value),
        ],
        axis=2,
    )
    w_local = lax.all_to_all(
        jnp.transpose(w_mixed, (1, 0, 2)), "sp", split_axis=0, concat_axis=0, tiled=True
    ).reshape(width, q_cols + 2 * kv_cols)
    gains = lax.all_gather(jnp.stack([gain_attn, gain_mlp]), "sp", axis=1, tiled=True).astype(
        jnp.float32
    )
    gain_one, gain_two = gains[0], gains[1]

    def normed(values):
        inverse = lax.rsqrt(jnp.mean(values * values, axis=1, keepdims=True) + EPS)
        return inverse, values * inverse

    inputs = tokens.astype(jnp.float32)
    inverse_one, normed_one = normed(inputs)
    _, normed_rows = normed(token_rows.astype(jnp.float32))
    act_one = (normed_rows * gain_one).astype(jnp.bfloat16)
    mixed = to_token_order(
        jnp.dot(act_one, w_local, preferred_element_type=jnp.float32), seq_rank
    )
    query_heads = (
        apply_rope(mixed[:, :q_cols].reshape(group_rows, q_cols // HD, HD), cosine_table, sine_table)
        .astype(jnp.bfloat16)
        .reshape(group_rows, q_cols)
    )
    key_heads = (
        apply_rope(
            mixed[:, q_cols : q_cols + kv_cols].reshape(group_rows, kv_cols // HD, HD),
            cosine_table,
            sine_table,
        )
        .astype(jnp.bfloat16)
        .reshape(group_rows, kv_cols)
    )
    value_heads = mixed[:, q_cols + kv_cols :].astype(jnp.bfloat16)
    attn_heads, log_sums = attend(query_heads, key_heads, value_heads, documents, score_scale)
    attn_rel = reorder(attn_heads, seq_rank)
    half_rows = group_rows // 2

    def product_terms(term):
        odd = term(slice(half_rows, group_rows))
        even = term(slice(0, half_rows))
        return scatter_rel(even, odd)

    hidden_one = inputs + product_terms(
        lambda rows: jnp.dot(attn_rel[rows], w_out, preferred_element_type=jnp.float32)
    )
    inverse_two, normed_two = normed(hidden_one)
    act_two = (normed_two * gain_two).astype(jnp.bfloat16)

    cot_blocks = gather_rel(cotangent)
    cot_rows = jnp.concatenate(cot_blocks, axis=0)
    act_rows = jnp.concatenate(gather_rel(act_two), axis=0)
    hidden, gate_back, up_back = feed_forward(act_rows, cot_rows, w_gate, w_up, w_down)
    act_two_back = product_terms(
        lambda rows: contract(gate_back[rows], w_gate, 1, 1) + contract(up_back[rows], w_up, 1, 1)
    )
    mlp_out = product_terms(
        lambda rows: jnp.dot(hidden[rows], w_down, preferred_element_type=jnp.float32)
    )
    layer_out = (hidden_one + mlp_out).astype(jnp.bfloat16)
    grad_down = contract(hidden, cot_rows, 0, 0)
    grad_gate = contract(act_rows, gate_back, 0, 0)
    grad_up = contract(act_rows, up_back, 0, 0)
    if groups <= 4:
        for distance in range(1, groups):
            cot_other = jnp.concatenate(gather_rel(swap(cotangent, distance, "dp")), axis=0)
            act_other = jnp.concatenate(gather_rel(swap(act_two, distance, "dp")), axis=0)
            hidden_o, gate_o, up_o = feed_forward(act_other, cot_other, w_gate, w_up, w_down)
            grad_down = grad_down + contract(hidden_o, cot_other, 0, 0)
            grad_gate = grad_gate + contract(act_other, gate_o, 0, 0)
            grad_up = grad_up + contract(act_other, up_o, 0, 0)
    else:
        grad_down, grad_gate, grad_up = (
            lax.psum(grad.astype(jnp.bfloat16), "dp").astype(jnp.float32)
            for grad in (grad_down, grad_gate, grad_up)
        )

    normed_back_two = act_two_back * gain_two
    gain_mlp_terms = jnp.sum(act_two_back * normed_two, axis=0)
    hidden_one_back = cotangent.astype(jnp.float32) + inverse_two * (
        normed_back_two - normed_two * jnp.mean(normed_back_two * normed_two, axis=1, keepdims=True)
    )
    branch_rows = jnp.concatenate(gather_rel(hidden_one_back.astype(jnp.bfloat16)), axis=0)
    heads_back = to_token_order(
        contract(branch_rows, w_out, 1, 1).astype(jnp.bfloat16), seq_rank
    )
    grad_out_terms = contract(attn_rel, branch_rows, 0, 0)
    grad_out = (
        dp_gather(
            dp_scatter(grad_out_terms.reshape(groups, -1, width)).astype(jnp.bfloat16)
        )
        .astype(jnp.float32)
        .reshape(grad_out_terms.shape)
    )

    query_back, key_back, value_back = attend_back(
        query_heads, key_heads, value_heads, heads_back, log_sums, documents, score_scale
    )
    mixed_back = reorder(
        jnp.concatenate(
            [
                rope_back(
                    query_back.astype(jnp.float32).reshape(group_rows, q_cols // HD, HD),
                    cosine_table,
                    sine_table,
                )
                .astype(jnp.bfloat16)
                .reshape(group_rows, q_cols),
                rope_back(
                    key_back.astype(jnp.float32).reshape(group_rows, kv_cols // HD, HD),
                    cosine_table,
                    sine_table,
                )
                .astype(jnp.bfloat16)
                .reshape(group_rows, kv_cols),
                value_back,
            ],
            axis=1,
        ),
        seq_rank,
    )
    act_one_back = product_terms(lambda rows: contract(mixed_back[rows], w_local, 1, 1))
    grad_mixed = contract(act_one, mixed_back, 0, 0)
    strip = width // (shards * groups)
    columns = grad_mixed.shape[1]
    grad_strip = dp_scatter(
        jnp.transpose(grad_mixed.reshape(shards, groups, strip, columns), (1, 0, 2, 3))
    )
    grad_strip = lax.all_to_all(
        grad_strip.astype(jnp.bfloat16), "sp", split_axis=0, concat_axis=0, tiled=True
    )
    grad_parts = dp_gather(grad_strip).astype(jnp.float32)
    grad_parts = jnp.transpose(grad_parts, (0, 2, 1, 3)).reshape(part_rows, shards, columns)
    grad_query = grad_parts[:, :, :q_cols].reshape(part_rows, shards * q_cols)

    def sum_copies(parts):
        return parts.reshape(part_rows, kv_total, copies, HD).sum(axis=2).reshape(part_rows, -1)

    grad_key = sum_copies(grad_parts[:, :, q_cols : q_cols + kv_cols])
    grad_value = sum_copies(grad_parts[:, :, q_cols + kv_cols :])

    normed_back_one = act_one_back * gain_one
    gain_attn_terms = jnp.sum(act_one_back * normed_one, axis=0)
    grad_tokens = hidden_one_back + inverse_one * (
        normed_back_one - normed_one * jnp.mean(normed_back_one * normed_one, axis=1, keepdims=True)
    )
    grad_gains = lax.dynamic_slice_in_dim(
        sum_all(jnp.stack([gain_attn_terms, gain_mlp_terms])), seq_rank * part_rows, part_rows, 1
    )
    return (
        layer_out,
        grad_tokens,
        grad_query,
        grad_key,
        grad_value,
        grad_out,
        grad_gains[0],
        grad_gains[1],
        grad_gate,
        grad_up,
        grad_down,
    )


def solution(mesh):
    placed = (
        P(("dp", "sp"), None),
        P("dp", None),
        P("sp", None),
        P("sp", None),
        P("sp", None),
        P("sp", None),
        P("sp"),
        P("sp"),
        P(None, "sp"),
        P(None, "sp"),
        P("sp", None),
        P(("dp", "sp"), None),
    )
    return jax.shard_map(
        on_device,
        mesh=mesh,
        in_specs=placed,
        out_specs=(
            P(("dp", "sp"), None),
            P(("dp", "sp"), None),
            P("sp", None),
            P("sp", None),
            P("sp", None),
            P("sp", None),
            P("sp"),
            P("sp"),
            P(None, "sp"),
            P(None, "sp"),
            P("sp", None),
        ),
        check_vma=False,
    )
```

```python
import functools

import jax
import jax.numpy as jnp
from jax import lax
from jax.experimental import pallas as pl
from jax.experimental.pallas import tpu as pltpu
from jax.sharding import PartitionSpec as P

HD = 64
Q_ROWS = 256
F32 = jnp.float32
BF16 = jnp.bfloat16


EPS = 1e-05
THETA = 500000.0
FACTOR = 32.0
LOW_FACTOR = 1.0
HIGH_FACTOR = 4.0
BASE_CONTEXT = 8192.0
MASKED = -1e30


def frequencies(head_size):
    half_index = jnp.arange(head_size // 2).astype(jnp.float32)
    inverse = THETA ** (-2.0 * half_index / head_size)
    wavelength = 2.0 * jnp.pi / inverse
    smooth = (BASE_CONTEXT / wavelength - LOW_FACTOR) / (HIGH_FACTOR - LOW_FACTOR)
    middle = (1.0 - smooth) * inverse / FACTOR + smooth * inverse
    slow_band = jnp.where(wavelength > BASE_CONTEXT / LOW_FACTOR, inverse / FACTOR, middle)
    return jnp.where(wavelength < BASE_CONTEXT / HIGH_FACTOR, inverse, slow_band)


def contract(left, right, left_dim, right_dim):
    return lax.dot_general(
        left, right, (((left_dim,), (right_dim,)), ((), ())), preferred_element_type=jnp.float32
    )


SHORT = pl.CostEstimate(flops=0, bytes_accessed=0, transcendentals=0)


def product(left, right, left_dim, right_dim):
    return lax.dot_general(
        left, right, (((left_dim,), (right_dim,)), ((), ())), preferred_element_type=F32
    )


def whole_in_vmem(count):
    return [pl.BlockSpec(memory_space=pltpu.VMEM)] * count


def in_hbm(*values):
    return [pltpu.with_memory_space_constraint(one, pltpu.HBM) for one in values]


def after(values, *earlier):
    def body(*refs):
        pass

    return pl.pallas_call(
        body,
        out_shape=jax.ShapeDtypeStruct(values.shape, values.dtype),
        in_specs=[pl.BlockSpec(memory_space=pl.ANY)] * (1 + len(earlier)),
        out_specs=pl.BlockSpec(memory_space=pl.ANY),
        input_output_aliases={0: 0},
        cost_estimate=pl.CostEstimate(flops=0, bytes_accessed=0, transcendentals=0),
    )(values, *earlier)


def together(*values):
    def body(*refs):
        pass

    anywhere = pl.BlockSpec(memory_space=pl.ANY)
    call = pl.pallas_call(
        body,
        out_shape=tuple(jax.ShapeDtypeStruct(one.shape, one.dtype) for one in values),
        in_specs=[anywhere] * len(values),
        out_specs=(anywhere,) * len(values),
        input_output_aliases={n: n for n in range(len(values))},
        cost_estimate=pl.CostEstimate(flops=0, bytes_accessed=0, transcendentals=0),
    )
    return list(call(*values))


def turn_signed(values, signed_sine):
    lane = lax.broadcasted_iota(jnp.int32, values.shape, 1) % HD
    turned = jnp.where(
        lane < HD // 2, pltpu.roll(values, 128 - HD // 2, 1), pltpu.roll(values, HD // 2, 1)
    )
    return turned * signed_sine


def rope_tables(cosine, sine, last):
    if not last:
        return cosine, sine
    lane = lax.broadcasted_iota(jnp.int32, cosine.shape, 1)
    return jnp.where(lane < HD, cosine, 1.0), jnp.where(lane < HD, sine, 0.0)


def score_mask(starts_ref, first_row, rows, keys):
    place = first_row + lax.broadcasted_iota(jnp.int32, (rows, 1), 0)
    begin = jnp.zeros((rows, 1), jnp.int32)
    for index in range(starts_ref.shape[0]):
        start = starts_ref[index]
        begin = jnp.maximum(begin, jnp.where(place >= start, start, 0))
    key_place = lax.broadcasted_iota(jnp.int32, (rows, keys), 1)
    return (key_place >= begin) & (key_place <= place)


def attention_body(shards, q_cols, index_ref, starts_ref, *refs):
    tokens = refs[:shards]
    gain, weights, cosine, sine = refs[shards : shards + 4]
    act, mixed, out_rel, log_sums, out_rows = refs[shards + 4 :]
    rows = tokens[0].shape[0]
    total = rows * shards
    part = act.shape[1] // shards
    columns = mixed.shape[1]
    groups = columns // 128
    half = shards // 2
    for side in range(2):
        for block in range(side * half, side * half + half):
            values = tokens[block][...].astype(F32)
            inverse = lax.rsqrt(jnp.mean(values * values, axis=1, keepdims=True) + EPS)
            act[block * rows : (block + 1) * rows, :] = (values * inverse * gain[...]).astype(BF16)
        first = side * half * rows
        sums = jnp.zeros((half * rows, columns), F32)
        for source in range(shards):
            sums = sums + product(
                act[first : first + half * rows, source * part : (source + 1) * part],
                weights[source, :part, :],
                1,
                0,
            )
        for block in range(half):
            place = pl.multiple_of(index_ref[side * half + block] * rows, rows)
            cosine_rows = cosine[pl.ds(place, rows), :]
            sine_rows = sine[pl.ds(place, rows), :]
            for group in range(groups):
                piece = sums[block * rows : (block + 1) * rows, group * 128 : (group + 1) * 128]
                cosine_part, sine_part = rope_tables(cosine_rows, sine_rows, group == groups - 1)
                mixed[pl.ds(place, rows), group * 128 : (group + 1) * 128] = (
                    piece * cosine_part + turn_signed(piece, sine_part)
                ).astype(BF16)
    scale = HD ** (-0.5)
    for first in range(0, total, Q_ROWS):
        keys = first + Q_ROWS
        allowed = score_mask(starts_ref, first, Q_ROWS, keys)
        key_rows = mixed[:keys, q_cols : q_cols + HD]
        value_rows = mixed[:keys, q_cols + HD : q_cols + 2 * HD]
        for head in range(q_cols // HD):
            query = mixed[first:keys, head * HD : (head + 1) * HD] * jnp.asarray(scale, BF16)
            scores = jnp.where(allowed, product(query, key_rows, 1, 1), MASKED)
            largest = jnp.max(scores, axis=1, keepdims=True)
            weights_row = jnp.exp(scores - largest)
            total_weight = jnp.sum(weights_row, axis=1, keepdims=True)
            attended = product(weights_row.astype(BF16), value_rows, 1, 0) / total_weight
            out_rows[first:keys, head * HD : (head + 1) * HD] = attended.astype(BF16)
            log_sums[first:keys, head : head + 1] = largest + jnp.log(total_weight)
    for block in range(shards):
        place = pl.multiple_of(index_ref[block] * rows, rows)
        out_rel[block * rows : (block + 1) * rows, :] = out_rows[pl.ds(place, rows), :]


def attention(index, starts, tokens, gain, weights, cosine, sine, q_cols):
    shards = len(tokens)
    rows, width = tokens[0].shape
    total = rows * shards
    columns = weights.shape[2]
    smem = pl.BlockSpec(memory_space=pltpu.SMEM)
    return pl.pallas_call(
        functools.partial(attention_body, shards, q_cols),
        out_shape=(
            jax.ShapeDtypeStruct((total, width), BF16),
            jax.ShapeDtypeStruct((total, columns), BF16),
            jax.ShapeDtypeStruct((total, q_cols), BF16),
            jax.ShapeDtypeStruct((total, q_cols // HD), F32),
        ),
        in_specs=[smem, smem] + whole_in_vmem(shards + 4),
        out_specs=tuple(whole_in_vmem(4)),
        scratch_shapes=[pltpu.VMEM((total, q_cols), BF16)],
        compiler_params=pltpu.CompilerParams(vmem_limit_bytes=48 * 2**20),
        cost_estimate=SHORT,
    )(index, starts, *tokens, gain, weights, cosine, sine)


def attention_back_body(shards, q_cols, index_ref, starts_ref, *refs):
    branch = refs[:shards]
    w_out, mixed, log_sums, out_rel, cosine, sine = refs[shards : shards + 6]
    mixed_back, grad_out = refs[shards + 6 : shards + 8]
    branch_rows, heads_back, query_grads, key_grads, value_grads = refs[shards + 8 :]
    rows = branch[0].shape[0]
    total = rows * shards
    columns = mixed.shape[1]
    half = total // 2
    for block in range(shards):
        branch_rows[block * rows : (block + 1) * rows, :] = branch[block][...]
    for side in range(2):
        back = product(branch_rows[side * half : (side + 1) * half, :], w_out[...], 1, 1).astype(
            BF16
        )
        for block in range(shards // 2):
            place = pl.multiple_of(index_ref[side * (shards // 2) + block] * rows, rows)
            heads_back[pl.ds(place, rows), :] = back[block * rows : (block + 1) * rows, :]
    grad_out[...] = product(out_rel[...], branch_rows[...], 0, 0).astype(BF16)
    key_grads[...] = jnp.zeros_like(key_grads)
    value_grads[...] = jnp.zeros_like(value_grads)
    scale = HD ** (-0.5)
    for first in range(0, total, Q_ROWS):
        keys = first + Q_ROWS
        allowed = score_mask(starts_ref, first, Q_ROWS, keys)
        key_rows = mixed[:keys, q_cols : q_cols + HD]
        value_rows = mixed[:keys, q_cols + HD : q_cols + 2 * HD]
        for head in range(q_cols // HD):
            cut = slice(head * HD, (head + 1) * HD)
            query = mixed[first:keys, cut] * jnp.asarray(scale, BF16)
            back = heads_back[first:keys, cut]
            scores = jnp.where(allowed, product(query, key_rows, 1, 1), MASKED)
            probs = jnp.exp(scores - log_sums[first:keys, head : head + 1])
            probs_back = product(back, value_rows, 1, 1)
            delta = jnp.sum(probs * probs_back, axis=1, keepdims=True)
            scores_back = (probs * (probs_back - delta)).astype(BF16)
            query_grads[first:keys, cut] = product(scores_back, key_rows, 1, 0) * scale
            key_grads[:keys, :] += product(scores_back, query, 0, 0)
            value_grads[:keys, :] += product(probs.astype(BF16), back, 0, 0)
    for block in range(shards):
        place = pl.multiple_of(index_ref[block] * rows, rows)
        window = pl.ds(place, rows)
        cosine_rows, sine_rows = cosine[window, :], sine[window, :]
        for group in range(columns // 128):
            last = group == columns // 128 - 1
            if last:
                piece = jnp.concatenate([key_grads[window, :], value_grads[window, :]], axis=1)
            else:
                piece = query_grads[window, group * 128 : (group + 1) * 128]
            cosine_part, sine_part = rope_tables(cosine_rows, sine_rows, last)
            mixed_back[block * rows : (block + 1) * rows, group * 128 : (group + 1) * 128] = (
                piece * cosine_part - turn_signed(piece, sine_part)
            ).astype(BF16)


def attention_back(index, starts, branch, w_out, mixed, log_sums, out_rel, cosine, sine):
    shards = len(branch)
    rows, width = branch[0].shape
    total = rows * shards
    columns = mixed.shape[1]
    q_cols = out_rel.shape[1]
    smem = pl.BlockSpec(memory_space=pltpu.SMEM)
    return pl.pallas_call(
        functools.partial(attention_back_body, shards, q_cols),
        out_shape=(
            jax.ShapeDtypeStruct((total, columns), BF16),
            jax.ShapeDtypeStruct((q_cols, width), BF16),
        ),
        in_specs=[smem, smem] + whole_in_vmem(shards + 6),
        out_specs=tuple(whole_in_vmem(2)),
        scratch_shapes=[
            pltpu.VMEM((total, width), BF16),
            pltpu.VMEM((total, q_cols), BF16),
            pltpu.VMEM((total, q_cols), F32),
            pltpu.VMEM((total, HD), F32),
            pltpu.VMEM((total, HD), F32),
        ],
        compiler_params=pltpu.CompilerParams(vmem_limit_bytes=48 * 2**20),
        cost_estimate=SHORT,
    )(index, starts, *branch, w_out, mixed, log_sums, out_rel, cosine, sine)


def ffn_body(pieces, waits, *refs):
    act, cot = refs[:pieces], refs[pieces : 2 * pieces]
    w_gate, w_up, w_down = refs[2 * pieces : 2 * pieces + 3]
    outs = refs[2 * pieces + 3 + waits :]
    hidden, gate_back, up_back, act_out, cot_out = outs[:5]
    act_rows, cot_rows = outs[5:]
    step = pl.program_id(0)

    @pl.when(step == 0)
    def _():
        for parts, rows in ((act, act_rows), (cot, cot_rows)):
            first = 0
            for part in parts:
                rows[first : first + part.shape[0], :] = part[...]
                first += part.shape[0]

    strip = act_out.shape[1]
    window = pl.ds(pl.multiple_of(step * strip, strip), strip)
    act_out[...] = act_rows[:, window]
    cot_out[...] = cot_rows[:, window]
    gate_value = product(act_rows[...], w_gate[...], 1, 0)
    up_value = product(act_rows[...], w_up[...], 1, 0)
    hidden_back = product(cot_rows[...], w_down[...], 1, 1)
    sigmoid_gate = 1.0 / (1.0 + jnp.exp(-gate_value))
    silu_gate = gate_value * sigmoid_gate
    hidden[...] = (silu_gate * up_value).astype(BF16)
    gate_back[...] = (
        hidden_back * up_value * sigmoid_gate * (1.0 + gate_value * (1.0 - sigmoid_gate))
    ).astype(BF16)
    up_back[...] = (hidden_back * silu_gate).astype(BF16)


def ffn(rows, act, cot, w_gate, w_up, w_down, waits=()):
    pieces = len(act)
    width = w_gate.shape[0]
    total = rows * pieces
    units = w_gate.shape[1]
    tile = min(256, units)
    steps = units // tile
    strip = width // steps
    once = pl.Buffered(1)

    def rows_spec(number):
        return pl.BlockSpec((rows, width), lambda j: (number, 0), pipeline_mode=once)

    columns = pl.BlockSpec((width, tile), lambda j: (0, j))
    out = pl.BlockSpec((total, tile), lambda j: (0, j))
    wide = pl.BlockSpec((total, strip), lambda j: (0, j))
    out_shape = (pltpu.HBM((total, units), BF16),) * 3 + (pltpu.HBM((total, width), BF16),) * 2
    out_specs = (out, out, out, wide, wide)
    return pl.pallas_call(
        functools.partial(ffn_body, pieces, len(waits)),
        out_shape=out_shape,
        grid=(steps,),
        in_specs=[rows_spec(number) for _, number in (*act, *cot)]
        + [columns, columns, pl.BlockSpec((tile, width), lambda j: (j, 0))]
        + [pl.BlockSpec(memory_space=pl.ANY)] * len(waits),
        out_specs=out_specs,
        scratch_shapes=[pltpu.VMEM((total, width), BF16)] * 2,
        compiler_params=pltpu.CompilerParams(vmem_limit_bytes=48 * 2**20),
        cost_estimate=SHORT,
    )(
        *(one for one, _ in (*act, *cot)),
        *in_hbm(w_gate, w_up, w_down),
        *waits,
    )


def ffn_others_body(waits, which, act, cot, w_gate, w_up, w_down, *refs):
    hidden, gate_back, up_back, gates, ups, backs = refs[waits:]
    now = lax.rem(pl.program_id(0), 2)
    last = 1 - now
    gate_value, up_value, hidden_back = gates[last], ups[last], backs[last]
    gates[now] = product(act[...], w_gate[...], 1, 0)
    ups[now] = product(act[...], w_up[...], 1, 0)
    backs[now] = product(cot[...], w_down[...], 1, 1)
    sigmoid_gate = 1.0 / (1.0 + jnp.exp(-gate_value))
    silu_gate = gate_value * sigmoid_gate
    hidden[...] = (silu_gate * up_value).astype(BF16)
    gate_back[...] = (
        hidden_back * up_value * sigmoid_gate * (1.0 + gate_value * (1.0 - sigmoid_gate))
    ).astype(BF16)
    up_back[...] = (hidden_back * silu_gate).astype(BF16)


def ffn_others(which, act_all, cot_all, w_gate, w_up, w_down, rows, waits=()):
    count = which.shape[0]
    width, units = w_gate.shape
    tall, tile = rows // 2, min(256, units)
    tiles = units // tile
    steps = 2 * count * tiles

    def block(step):
        step = jnp.minimum(step, steps - 1)
        return step // tiles, lax.rem(step, tiles)

    def rows_map(step, w):
        part, _ = block(step)
        return (w[part // 2] * 2 + lax.rem(part, 2), 0)

    def out_map(step, w):
        return block(jnp.maximum(step - 1, 0))

    rows_spec = pl.BlockSpec((tall, width), rows_map)
    columns = pl.BlockSpec((width, tile), lambda step, w: (0, block(step)[1]))
    out = pl.BlockSpec((tall, tile), out_map)
    return pl.pallas_call(
        functools.partial(ffn_others_body, len(waits)),
        out_shape=(pltpu.HBM((rows * count, units), BF16),) * 3,
        grid_spec=pltpu.PrefetchScalarGridSpec(
            num_scalar_prefetch=1,
            grid=(steps + 1,),
            in_specs=[
                rows_spec,
                rows_spec,
                columns,
                columns,
                pl.BlockSpec((tile, width), lambda step, w: (block(step)[1], 0)),
            ]
            + [pl.BlockSpec(memory_space=pl.ANY)] * len(waits),
            out_specs=(out, out, out),
            scratch_shapes=[pltpu.VMEM((2, tall, tile), F32)] * 3,
        ),
        compiler_params=pltpu.CompilerParams(vmem_limit_bytes=40 * 2**20),
        cost_estimate=SHORT,
    )(which, *in_hbm(act_all, cot_all, w_gate, w_up, w_down), *waits)


def act_back_body(gate_back, up_back, w_gate, w_up, *refs):
    out = refs[-1]
    out[...] = (
        product(gate_back[...], w_gate[...], 1, 1) + product(up_back[...], w_up[...], 1, 1)
    ).astype(out.dtype)


def act_back(side, gate_back, up_back, w_gate, w_up, dtype, waits=()):
    total, units = gate_back.shape[0] // 2, gate_back.shape[1]
    width = w_gate.shape[0]
    tile = 512
    rows = pl.BlockSpec((total, units), lambda j: (side, 0), pipeline_mode=pl.Buffered(1))
    weights = pl.BlockSpec((tile, units), lambda j: (j, 0))
    return pl.pallas_call(
        act_back_body,
        out_shape=jax.ShapeDtypeStruct((total, width), dtype),
        grid=(width // tile,),
        in_specs=[rows, rows, weights, weights]
        + [pl.BlockSpec(memory_space=pl.ANY)] * len(waits),
        out_specs=pl.BlockSpec((total, tile), lambda j: (0, j)),
        compiler_params=pltpu.CompilerParams(vmem_limit_bytes=32 * 2**20),
        cost_estimate=SHORT,
    )(*in_hbm(gate_back, up_back, w_gate, w_up), *waits)


def weight_grad_body(pieces, began, *refs):
    left, right, out = refs[:pieces], refs[pieces : 2 * pieces], refs[-1]
    total = product(left[0][...], right[0][...], 0, 0)
    if began:
        total = total + refs[2 * pieces][...]
    for piece in range(1, pieces):
        total = total + product(left[piece][...], right[piece][...], 0, 0)
    out[...] = total


def weight_grad(left, right, row_tile, column_tile, waits=(), began=None):
    pieces = len(left)
    rows, height = left[0].shape
    width = right[0].shape[1]
    row_tile, column_tile = min(row_tile, height), min(column_tile, width)
    tile_spec = pl.BlockSpec((row_tile, column_tile), lambda j, i: (i, j))
    start = () if began is None else (began,)
    return pl.pallas_call(
        functools.partial(weight_grad_body, pieces, began is not None),
        out_shape=pltpu.HBM((height, width), F32),
        grid=(width // column_tile, height // row_tile),
        in_specs=[pl.BlockSpec((rows, row_tile), lambda j, i: (0, i))] * pieces
        + [pl.BlockSpec((rows, column_tile), lambda j, i: (0, j))] * pieces
        + [tile_spec] * len(start)
        + [pl.BlockSpec(memory_space=pl.ANY)] * len(waits),
        out_specs=tile_spec,
        compiler_params=pltpu.CompilerParams(vmem_limit_bytes=48 * 2**20),
        cost_estimate=SHORT,
    )(*in_hbm(*left, *right, *start), *waits)


def pack_weights_body(shards, copies, w_query, w_key, w_value, gains, out):
    part, q_cols = w_query.shape[0], w_query.shape[1] // shards
    out[:, part:, :] = jnp.broadcast_to(gains[...][None], (shards,) + gains.shape)
    for shard in range(shards):
        head = shard // copies * HD
        out[shard, :part, :q_cols] = w_query[:, shard * q_cols : (shard + 1) * q_cols]
        out[shard, :part, q_cols:] = jnp.concatenate(
            [w_key[:, head : head + HD], w_value[:, head : head + HD]], axis=1
        )


def pack_weights(shards, copies, w_query, w_key, w_value, gain_attn, gain_mlp):
    part = w_query.shape[0]
    columns = w_query.shape[1] // shards + 2 * HD
    gains = jnp.zeros((16, columns), BF16)
    gains = gains.at[0, :part].set(gain_attn).at[1, :part].set(gain_mlp)
    return pl.pallas_call(
        functools.partial(pack_weights_body, shards, copies),
        out_shape=jax.ShapeDtypeStruct((shards, part + 16, columns), BF16),
        in_specs=whole_in_vmem(4),
        out_specs=whole_in_vmem(1)[0],
        compiler_params=pltpu.CompilerParams(vmem_limit_bytes=16 * 2**20),
    )(w_query, w_key, w_value, gains)


def unpack_grads_body(q_cols, index_ref, *refs):
    pieces, (query, key, value) = refs[:-3], refs[-3:]
    shards, strip, _ = pieces[0].shape
    for number, piece in enumerate(pieces):
        rows = pl.ds(pl.multiple_of(index_ref[number] * strip, strip), strip)
        for shard in range(shards):
            query[rows, shard * q_cols : (shard + 1) * q_cols] = piece[shard, :, :q_cols].astype(
                F32
            )
        for shard in range(0, shards, 2):
            for place, out in ((q_cols, key), (q_cols + HD, value)):
                out[rows, shard * HD : (shard + 2) * HD] = jnp.concatenate(
                    [piece[shard + n, :, place : place + HD] for n in range(2)], axis=1
                ).astype(F32)


def unpack_grads(index, pieces, q_cols):
    shards, strip, _ = pieces[0].shape
    rows = strip * len(pieces)
    return pl.pallas_call(
        functools.partial(unpack_grads_body, q_cols),
        out_shape=(
            jax.ShapeDtypeStruct((rows, shards * q_cols), F32),
            jax.ShapeDtypeStruct((rows, shards * HD), F32),
            jax.ShapeDtypeStruct((rows, shards * HD), F32),
        ),
        in_specs=[pl.BlockSpec(memory_space=pltpu.SMEM)] + whole_in_vmem(len(pieces)),
        out_specs=tuple(whole_in_vmem(3)),
        compiler_params=pltpu.CompilerParams(vmem_limit_bytes=24 * 2**20),
    )(index, *pieces)


def grad_others_body(count, waits, turned, which, *refs):
    rows, units, began = refs[:count], refs[count : 2 * count], refs[2 * count]
    out = refs[-1]
    total = began[...]
    for one, two in zip(rows, units, strict=True):
        if turned:
            one, two = two, one
        total = total + product(one[...], two[...], 0, 0)
    out[...] = total


def grad_others(which, rows_all, units_all, began, row_tile, column_tile, turned, waits=()):
    count = which.shape[0]
    rows = units_all.shape[0] // count
    height, width = began.shape
    wide, narrow = (column_tile, row_tile) if turned else (row_tile, column_tile)

    def rows_spec(number):
        if turned:
            return pl.BlockSpec((rows, wide), lambda j, i, w: (w[number], j))
        return pl.BlockSpec((rows, wide), lambda j, i, w: (w[number], i))

    def units_spec(number):
        if turned:
            return pl.BlockSpec((rows, narrow), lambda j, i, w: (number, i))
        return pl.BlockSpec((rows, narrow), lambda j, i, w: (number, j))

    tile_spec = pl.BlockSpec((row_tile, column_tile), lambda j, i, w: (i, j))
    return pl.pallas_call(
        functools.partial(grad_others_body, count, len(waits), turned),
        out_shape=pltpu.HBM((height, width), F32),
        grid_spec=pltpu.PrefetchScalarGridSpec(
            num_scalar_prefetch=1,
            grid=(width // column_tile, height // row_tile),
            in_specs=[rows_spec(n) for n in range(count)]
            + [units_spec(n) for n in range(count)]
            + [tile_spec]
            + [pl.BlockSpec(memory_space=pl.ANY)] * len(waits),
            out_specs=tile_spec,
        ),
        compiler_params=pltpu.CompilerParams(vmem_limit_bytes=48 * 2**20),
        cost_estimate=SHORT,
    )(which, *in_hbm(*[rows_all] * count, *[units_all] * count, began), *waits)


def small_call(body, out_shape, *operands):
    return pl.pallas_call(
        body,
        out_shape=tuple(jax.ShapeDtypeStruct(shape, dtype) for shape, dtype in out_shape),
        in_specs=whole_in_vmem(len(operands)),
        out_specs=tuple(whole_in_vmem(len(out_shape))),
        compiler_params=pltpu.CompilerParams(vmem_limit_bytes=24 * 2**20),
        cost_estimate=SHORT,
    )(*operands)


def halves_body(near, next_row, upper, lower):
    half = upper.shape[0]
    upper[...] = near[:half, :]
    lower[...] = next_row[half:, :]


def join_body(upper, lower, out):
    half = upper.shape[0]
    out[:half, :] = upper[...]
    out[half:, :] = lower[...]


def pairs_body(even, got, upper, lower, own, near, next_row):
    rows, half = own.shape[0], upper.shape[0]

    def add(first, count):
        window = slice(first, first + count)
        return even[window, :].astype(F32) + got[window, :].astype(F32)

    upper[...] = add(3 * rows, half).astype(BF16)
    lower[...] = add(3 * rows + half, half).astype(BF16)
    for number, out in enumerate((own, near, next_row)):
        out[...] = add(number * rows, rows)


def far_body(near, next_row, to_next, to_near, near_out, next_out):
    half = to_next.shape[0]
    near_out[:half, :] = near[:half, :].astype(BF16)
    near_out[half:, :] = (near[half:, :] + to_near[...].astype(F32)).astype(BF16)
    next_out[:half, :] = (next_row[:half, :] + to_next[...].astype(F32)).astype(BF16)
    next_out[half:, :] = next_row[half:, :].astype(BF16)


def row_mean(values):
    return jnp.mean(values, axis=1, keepdims=True)


def norm_two_body(own, one, two, tokens, gain, hidden_one, act_two):
    total = tokens[...].astype(F32) + own[...] + one[...].astype(F32) + two[...].astype(F32)
    hidden_one[...] = total
    inverse = lax.rsqrt(row_mean(total * total) + EPS)
    act_two[...] = (total * inverse * gain[...]).astype(BF16)


def norm_back_body(own, one, two, values, gain, beside, back, back_low, gain_terms):
    act_back = own[...] + one[...].astype(F32) + two[...].astype(F32)
    rows = values[...].astype(F32)
    inverse = lax.rsqrt(row_mean(rows * rows) + EPS)
    normed = rows * inverse
    gain_terms[...] = jnp.sum(act_back * normed, axis=0, keepdims=True)
    scaled = act_back * gain[...]
    total = beside[...].astype(F32) + inverse * (scaled - normed * row_mean(scaled * normed))
    back[...] = total
    back_low[...] = total.astype(BF16)


def layer_out_body(own, one, two, hidden_one, out):
    total = hidden_one[...] + own[...] + one[...].astype(F32) + two[...].astype(F32)
    out[...] = total.astype(BF16)


def swap(values, distance, axis):
    size = lax.axis_size(axis)
    return lax.ppermute(values, axis, [(i, i ^ distance) for i in range(size)])


def block_order(shards):
    return list(range(0, shards, 2)) + list(range(1, shards, 2))


class RowGather:
    def __init__(self, values):
        self.values = values
        self.moving = [swap(values, 2, "sp"), swap(values, 4, "sp")]

    def forward(self):
        self.near, self.next_row = self.moving
        rows, width = self.values.shape
        half = ((rows // 2, width), BF16)
        upper, lower = small_call(halves_body, (half, half), self.near, self.next_row)
        self.moving = [swap(upper, 4, "sp"), swap(lower, 2, "sp")]

    def cores(self):
        (far,) = small_call(join_body, ((self.values.shape, BF16),), *self.moving)
        self.evens = [self.values, self.near, self.next_row, far]
        self.moving = [swap(block, 1, "sp") for block in self.evens]

    def blocks(self):
        return self.evens + self.moving


class RowSum:
    def __init__(self, odd_terms):
        self.moving = [swap(odd_terms, 1, "sp")]

    def add_pairs(self, even_terms):
        rows, width = even_terms.shape[0] // 4, even_terms.shape[1]
        half, whole = ((rows // 2, width), BF16), ((rows, width), F32)
        upper, lower, self.own, self.near, self.next_row = small_call(
            pairs_body, (half, half, whole, whole, whole), even_terms, *self.moving
        )
        self.moving = [swap(upper, 2, "sp"), swap(lower, 4, "sp")]

    def add_far(self):
        whole = (self.own.shape, BF16)
        near, next_row = small_call(
            far_body, (whole, whole), self.near, self.next_row, *self.moving
        )
        self.moving = [swap(near, 2, "sp"), swap(next_row, 4, "sp")]

    def terms(self):
        return self.own, *self.moving


class DpSum:
    def __init__(self, terms):
        rank = lax.axis_index("dp")
        self.own = lax.dynamic_index_in_dim(terms, rank, 0, keepdims=False)
        self.moving = [
            swap(lax.dynamic_index_in_dim(terms, rank ^ d, 0, keepdims=False).astype(BF16), d, "dp")
            for d in range(1, lax.axis_size("dp"))
        ]

    def add(self):
        return self.own + sum(one.astype(F32) for one in self.moving)


def gather_rel(values):
    evens, distance = [values], 2
    while distance < lax.axis_size("sp"):
        evens = evens + [swap(block, distance, "sp") for block in evens]
        distance *= 2
    return evens + [swap(block, 1, "sp") for block in evens]


def scatter_rel(even_terms, odd_terms):
    shards = lax.axis_size("sp")
    got = swap(odd_terms, 1, "sp").astype(F32)
    sums = (even_terms.astype(F32) + got).reshape(shards // 2, -1, even_terms.shape[1])
    distance = shards // 2
    while distance > 1:
        kept = distance // 2
        sums = sums[:kept] + swap(sums[kept:].astype(BF16), distance, "sp").astype(F32)
        distance //= 2
    return sums[0]


def dp_share(piece):
    return [piece] + [swap(piece, d, "dp") for d in range(1, lax.axis_size("dp"))]


def on_device(
    tokens,
    doc_lengths,
    w_query,
    w_key,
    w_value,
    w_out,
    gain_attn,
    gain_mlp,
    w_gate,
    w_up,
    w_down,
    cotangent,
):
    shards = lax.axis_size("sp")
    groups = lax.axis_size("dp")
    seq_rank = lax.axis_index("sp")
    tok_rows, width = tokens.shape
    group_rows = tok_rows * shards
    heads_total = w_query.shape[1] // HD
    kv_total = w_key.shape[1] // HD
    copies = max(1, shards // kv_total)
    q_cols = heads_total // shards * HD
    part_rows = w_query.shape[0]
    half = shards // 2

    planned = shards == 8 and groups == 4
    w_mixed = pack_weights(shards, copies, w_query, w_key, w_value, gain_attn, gain_mlp)
    columns = w_mixed.shape[2]
    w_local = lax.all_to_all(w_mixed, "sp", split_axis=0, concat_axis=0, tiled=True)
    gain_one = w_local[:, part_rows, :part_rows].reshape(1, width).astype(F32)
    gain_two = w_local[:, part_rows + 1, :part_rows].reshape(1, width).astype(F32)

    lengths = doc_lengths[0]
    count = lengths.shape[0]
    before = jnp.arange(count)[None, :] < jnp.arange(count)[:, None]
    starts = jnp.sum(jnp.where(before, lengths[None, :], 0), axis=1).astype(jnp.int32)
    places = jnp.arange(group_rows, dtype=jnp.int32)
    begins = jnp.max(jnp.where(starts[None, :] <= places[:, None], starts[None, :], 0), axis=1)
    angles = (places - begins).astype(F32)[:, None] * frequencies(HD)[None, :]
    cosine_half, sine_half = jnp.cos(angles), jnp.sin(angles)
    cosine = jnp.concatenate([cosine_half] * 4, axis=1)
    sine = jnp.concatenate([-sine_half, sine_half] * 2, axis=1)
    index = jnp.asarray(block_order(shards), jnp.int32) ^ seq_rank.astype(jnp.int32)

    def attend(blocks, weights):
        gain = weights[:, part_rows, :part_rows].reshape(1, width).astype(F32)
        return attention(index, starts, blocks, gain, weights, cosine, sine, q_cols)

    half_rows = group_rows // 2

    def terms(values, weights, side, turned=False):
        rows = values[side * half_rows : (side + 1) * half_rows]
        if turned:
            return contract(rows, weights, 1, 1).astype(BF16)
        return jnp.dot(rows, weights, preferred_element_type=F32).astype(BF16)

    rows_f32, rows_bf16 = ((tok_rows, width), F32), ((tok_rows, width), BF16)

    def norm_two(summed):
        return small_call(norm_two_body, (rows_f32, rows_bf16), *summed, tokens, gain_two)

    def norm_back(summed, values, gain, beside):
        outs = (rows_f32, rows_bf16, ((1, width), F32))
        return small_call(norm_back_body, outs, *summed, values, gain, beside)

    def attend_back(blocks):
        return attention_back(
            index, starts, blocks, w_out, mixed, log_sums, out_rel, cosine, sine
        )

    strip = width // (shards * groups)

    def strips(grad_mixed):
        return jnp.transpose(grad_mixed.reshape(shards, groups, strip, columns), (1, 0, 2, 3))

    def to_rows(strip_sum):
        return lax.all_to_all(
            strip_sum.astype(BF16), "sp", split_axis=0, concat_axis=0, tiled=True
        )

    def gain_part(vectors, distance):
        return lax.dynamic_slice_in_dim(vectors, (seq_rank ^ distance) * part_rows, part_rows, 1)

    def plain(pieces):
        return [(one, 0) for one in pieces]

    def run_ffn(act, cot, *waits):
        return ffn(tok_rows, act, cot, w_gate, w_up, w_down, waits)

    def grow(kind, works, began, *waits):
        cot_rows, act_rows = [work[4] for work in works], [work[3] for work in works]
        mine = [work[(1, 2, 0)[kind]] for work in works]
        if kind == 2:
            return weight_grad(mine, cot_rows, 1024, 256, waits, began)
        return weight_grad(act_rows, mine, 256, 1024, waits, began)

    w_projections = w_local[:, :part_rows, :].reshape(width, columns)
    dp_rank = lax.axis_index("dp").astype(jnp.int32)

    if planned:
        which = dp_rank ^ jnp.arange(1, groups, dtype=jnp.int32)
        cot_all = lax.all_gather(cotangent, ("dp", "sp"), axis=0, tiled=True)
        token_gather = RowGather(tokens)
        *token_gather.moving, cosine, sine = together(*token_gather.moving, cosine, sine)
        token_gather.forward()
        token_gather.cores()
        *token_blocks, w_local = together(*token_gather.evens[1:], *token_gather.moving, w_local)
        token_blocks = [tokens] + token_blocks
        w_projections = w_local[:, :part_rows, :].reshape(width, columns)

        cot_gather = RowGather(after(cotangent, w_local))
        act_one, mixed, out_rel, log_sums = attend(token_blocks, w_local)
        out_rel, *cot_gather.moving = together(out_rel, *cot_gather.moving)

        out_sum = RowSum(terms(out_rel, w_out, 1))
        out_even = terms(out_rel, w_out, 0)
        cot_gather.forward()
        out_even, *out_sum.moving = together(out_even, *out_sum.moving)

        out_sum.add_pairs(out_even)
        moving = together(*out_sum.moving, *cot_gather.moving)
        out_sum.moving, cot_gather.moving = moving[:2], moving[2:]

        out_sum.add_far()
        cot_gather.cores()
        *out_sum.moving, one, two, three, four = together(*out_sum.moving, *cot_gather.moving)
        cot_blocks = cot_gather.evens + [one, two, three, four]
        hidden_one, act_two = norm_two(out_sum.terms())

        act_all = lax.all_gather(act_two, ("dp", "sp"), axis=0, tiled=True)
        act_gather = RowGather(act_two)
        act_gather.moving = together(*act_gather.moving)
        act_gather.forward()
        act_gather.cores()
        act_gather.moving = together(*act_gather.moving)

        own = run_ffn(plain(act_gather.blocks()), plain(cot_blocks))
        back_sum = RowSum(act_back(1, own[1], own[2], w_gate, w_up, BF16))
        even_back = act_back(0, own[1], own[2], w_gate, w_up, BF16)
        even_back, *back_sum.moving = together(even_back, *back_sum.moving)

        back_sum.add_pairs(even_back)
        grad_gate = grow(0, [own], None, even_back)
        grad_gate, *back_sum.moving = together(grad_gate, *back_sum.moving)

        back_sum.add_far()
        grad_up = grow(1, [own], None, grad_gate)
        mlp_odd = terms(after(own[0], grad_gate), w_down, 1)
        grad_up, mlp_odd, *back_sum.moving = together(grad_up, mlp_odd, *back_sum.moving)
        hidden_one_back, branch, gain_mlp_terms = norm_back(
            back_sum.terms(), hidden_one, gain_two, cotangent
        )

        branch_gather = RowGather(branch)
        grad_down = grow(2, [own], None, branch)
        mlp_even = terms(after(own[0], branch), w_down, 0)
        grad_down, mlp_even, *branch_gather.moving = together(
            grad_down, mlp_even, *branch_gather.moving
        )

        branch_gather.forward()
        branch_gather.cores()
        mlp_odd, *branch_gather.moving = together(mlp_odd, *branch_gather.moving)

        mlp_sum = RowSum(mlp_odd)
        mixed_back, grad_out_terms = attend_back(branch_gather.blocks())
        mixed_back, *mlp_sum.moving = together(mixed_back, *mlp_sum.moving)

        grad_out = lax.psum(grad_out_terms, "dp")
        mixed_sum = DpSum(strips(contract(act_one, mixed_back, 0, 0)))
        one_sum = RowSum(terms(mixed_back, w_projections, 1, True))
        one_even = terms(mixed_back, w_projections, 0, True)
        mlp_sum.add_pairs(mlp_even)
        one_even, *moving = together(one_even, *one_sum.moving, *mlp_sum.moving)
        one_sum.moving, mlp_sum.moving = moving[:1], moving[1:]

        one_sum.add_pairs(one_even)
        mlp_sum.add_far()
        others = ffn_others(
            which, act_all, cot_all, w_gate, w_up, w_down, group_rows, (one_even, mlp_odd)
        )
        *others, one, two, three, four, five, six, seven = together(
            *others, *one_sum.moving, *mlp_sum.moving, *mixed_sum.moving
        )
        one_sum.moving, mlp_sum.moving = [one, two], [three, four]
        mixed_sum.moving = [five, six, seven]

        mixed_rows = to_rows(mixed_sum.add())
        one_sum.add_far()
        (layer_out,) = small_call(layer_out_body, (rows_bf16,), *mlp_sum.terms(), hidden_one)
        grad_gate = grad_others(
            which, act_all, others[1], grad_gate, 256, 1024, False, (others[0],)
        )
        grad_gate, mixed_rows, *one_sum.moving = together(grad_gate, mixed_rows, *one_sum.moving)

        mixed_pieces = dp_share(mixed_rows)
        grad_tokens, _, gain_attn_terms = norm_back(
            one_sum.terms(), tokens, gain_one, hidden_one_back
        )
        gain_terms = jnp.concatenate([gain_attn_terms, gain_mlp_terms], axis=0)
        grad_up = grad_others(
            which, act_all, others[2], grad_up, 256, 1024, False, (gain_attn_terms,)
        )
        gain_moving = [swap(gain_terms, 1, "sp")]
        grad_up, *gain_moving = together(grad_up, *gain_moving)
        gain_terms = gain_terms + gain_moving[0]
        gain_moving = [swap(gain_part(gain_terms, d), d, "sp") for d in (2, 4, 6)]
        grad_down = grad_others(
            which, cot_all, others[0], grad_down, 1024, 256, True, (gain_terms,)
        )
        grad_down, *moving = together(grad_down, *gain_moving, *mixed_pieces[1:])
        gain_moving, mixed_pieces = moving[:3], mixed_pieces[:1] + moving[3:]
        grad_gains = gain_part(gain_terms, 0) + sum(gain_moving)
        grad_gains = grad_gains + sum(swap(grad_gains, d, "dp") for d in range(1, groups))
        grad_out = after(grad_out, grad_down).astype(F32)
    else:
        act_one, mixed, out_rel, log_sums = attend(gather_rel(tokens), w_local)
        zero = jnp.zeros((tok_rows, width), BF16)
        hidden_one, act_two = norm_two(
            (scatter_rel(terms(out_rel, w_out, 0), terms(out_rel, w_out, 1)), zero, zero)
        )
        act_blocks, cot_blocks, half = gather_rel(act_two), gather_rel(cotangent), shards // 2
        own = [
            jnp.concatenate(parts, axis=0)
            for parts in zip(
                run_ffn(plain(act_blocks[:half]), plain(cot_blocks[:half])),
                run_ffn(plain(act_blocks[half:]), plain(cot_blocks[half:])),
                strict=True,
            )
        ]
        act_two_back = scatter_rel(
            act_back(0, own[1], own[2], w_gate, w_up, BF16),
            act_back(1, own[1], own[2], w_gate, w_up, BF16),
        )
        hidden_one_back, branch, gain_mlp_terms = norm_back(
            (act_two_back, zero, zero), hidden_one, gain_two, cotangent
        )
        mixed_back, grad_out_terms = attend_back(gather_rel(branch))
        act_one_back = scatter_rel(
            terms(mixed_back, w_projections, 0, True), terms(mixed_back, w_projections, 1, True)
        )
        mixed_rows = to_rows(DpSum(strips(contract(act_one, mixed_back, 0, 0))).add())
        mixed_pieces = dp_share(mixed_rows)
        mlp_out = scatter_rel(terms(own[0], w_down, 0), terms(own[0], w_down, 1))
        layer_out = (hidden_one + mlp_out).astype(BF16)
        grad_tokens, _, gain_attn_terms = norm_back(
            (act_one_back, zero, zero), tokens, gain_one, hidden_one_back
        )
        grad_gains = lax.psum(
            jnp.concatenate([gain_attn_terms, gain_mlp_terms], axis=0), ("dp", "sp")
        )
        grad_gains = gain_part(grad_gains, 0)
        grad_out, grad_gate, grad_up, grad_down = (
            lax.psum(grad.astype(BF16), "dp").astype(F32)
            for grad in (grad_out_terms, *(grow(kind, [own], None) for kind in range(3)))
        )
    if copies == 1:
        dp_index = dp_rank ^ jnp.arange(groups, dtype=jnp.int32)
        grad_query, grad_key, grad_value = unpack_grads(dp_index, mixed_pieces, q_cols)
    else:
        parts = jnp.zeros((groups,) + mixed_pieces[0].shape, F32)
        for d, one in enumerate(mixed_pieces):
            parts = lax.dynamic_update_index_in_dim(parts, one.astype(F32), dp_rank ^ d, 0)
        parts = jnp.transpose(parts, (0, 2, 1, 3)).reshape(part_rows, shards, columns)
        grad_query = parts[:, :, :q_cols].reshape(part_rows, shards * q_cols)
        grad_key, grad_value = (
            parts[:, :, first : first + HD]
            .reshape(part_rows, kv_total, copies, HD)
            .sum(axis=2)
            .reshape(part_rows, -1)
            for first in (q_cols, q_cols + HD)
        )
    return (
        layer_out,
        grad_tokens,
        grad_query,
        grad_key,
        grad_value,
        grad_out,
        grad_gains[0],
        grad_gains[1],
        grad_gate,
        grad_up,
        grad_down,
    )


def solution(mesh):
    placed = (
        P(("dp", "sp"), None),
        P("dp", None),
        P("sp", None),
        P("sp", None),
        P("sp", None),
        P("sp", None),
        P("sp"),
        P("sp"),
        P(None, "sp"),
        P(None, "sp"),
        P("sp", None),
        P(("dp", "sp"), None),
    )
    return jax.shard_map(
        on_device,
        mesh=mesh,
        in_specs=placed,
        out_specs=(
            P(("dp", "sp"), None),
            P(("dp", "sp"), None),
            P("sp", None),
            P("sp", None),
            P("sp", None),
            P("sp", None),
            P("sp"),
            P("sp"),
            P(None, "sp"),
            P(None, "sp"),
            P("sp", None),
        ),
        check_vma=False,
    )
```

```python
import functools

import jax
import jax.numpy as jnp
from jax import lax
from jax.experimental import pallas as pl
from jax.experimental.pallas import tpu as pltpu
from jax.sharding import PartitionSpec as P

HD = 64
Q_ROWS = 256
F32 = jnp.float32
BF16 = jnp.bfloat16


EPS = 1e-05
THETA = 500000.0
FACTOR = 32.0
LOW_FACTOR = 1.0
HIGH_FACTOR = 4.0
BASE_CONTEXT = 8192.0
MASKED = -1e30


def frequencies(head_size):
    half_index = jnp.arange(head_size // 2).astype(jnp.float32)
    inverse = THETA ** (-2.0 * half_index / head_size)
    wavelength = 2.0 * jnp.pi / inverse
    smooth = (BASE_CONTEXT / wavelength - LOW_FACTOR) / (HIGH_FACTOR - LOW_FACTOR)
    middle = (1.0 - smooth) * inverse / FACTOR + smooth * inverse
    slow_band = jnp.where(wavelength > BASE_CONTEXT / LOW_FACTOR, inverse / FACTOR, middle)
    return jnp.where(wavelength < BASE_CONTEXT / HIGH_FACTOR, inverse, slow_band)


def contract(left, right, left_dim, right_dim):
    return lax.dot_general(
        left, right, (((left_dim,), (right_dim,)), ((), ())), preferred_element_type=jnp.float32
    )


SHORT = pl.CostEstimate(flops=0, bytes_accessed=0, transcendentals=0)


def product(left, right, left_dim, right_dim):
    return lax.dot_general(
        left, right, (((left_dim,), (right_dim,)), ((), ())), preferred_element_type=F32
    )


def whole_in_vmem(count):
    return [pl.BlockSpec(memory_space=pltpu.VMEM)] * count


def in_hbm(*values):
    return [pltpu.with_memory_space_constraint(one, pltpu.HBM) for one in values]


def after(values, *earlier):
    def body(*refs):
        pass

    return pl.pallas_call(
        body,
        out_shape=pltpu.HBM(values.shape, values.dtype),
        in_specs=[pl.BlockSpec(memory_space=pl.ANY)] * (1 + len(earlier)),
        out_specs=pl.BlockSpec(memory_space=pl.ANY),
        input_output_aliases={0: 0},
        cost_estimate=pl.CostEstimate(flops=0, bytes_accessed=0, transcendentals=0),
    )(*in_hbm(values, *earlier))


def together(*values):
    def body(*refs):
        pass

    anywhere = pl.BlockSpec(memory_space=pl.ANY)
    call = pl.pallas_call(
        body,
        out_shape=tuple(pltpu.HBM(one.shape, one.dtype) for one in values),
        in_specs=[anywhere] * len(values),
        out_specs=(anywhere,) * len(values),
        input_output_aliases={n: n for n in range(len(values))},
        cost_estimate=pl.CostEstimate(flops=0, bytes_accessed=0, transcendentals=0),
    )
    return list(call(*in_hbm(*values)))


def turn_signed(values, signed_sine):
    lane = lax.broadcasted_iota(jnp.int32, values.shape, 1) % HD
    turned = jnp.where(
        lane < HD // 2, pltpu.roll(values, 128 - HD // 2, 1), pltpu.roll(values, HD // 2, 1)
    )
    return turned * signed_sine


def rope_tables(cosine, sine, last):
    if not last:
        return cosine, sine
    lane = lax.broadcasted_iota(jnp.int32, cosine.shape, 1)
    return jnp.where(lane < HD, cosine, 1.0), jnp.where(lane < HD, sine, 0.0)


def score_mask(starts_ref, first_row, rows, keys):
    place = first_row + lax.broadcasted_iota(jnp.int32, (rows, 1), 0)
    begin = jnp.zeros((rows, 1), jnp.int32)
    for index in range(starts_ref.shape[0]):
        start = starts_ref[index]
        begin = jnp.maximum(begin, jnp.where(place >= start, start, 0))
    key_place = lax.broadcasted_iota(jnp.int32, (rows, keys), 1)
    return (key_place >= begin) & (key_place <= place)


def attention_body(shards, q_cols, index_ref, starts_ref, *refs):
    tokens = refs[:shards]
    gain, weights, cosine, sine = refs[shards : shards + 4]
    act, mixed, out_rel, log_sums, out_rows = refs[shards + 4 :]
    rows = tokens[0].shape[0]
    total = rows * shards
    part = act.shape[1] // shards
    columns = mixed.shape[1]
    groups = columns // 128
    half = shards // 2
    for side in range(2):
        for block in range(side * half, side * half + half):
            values = tokens[block][...].astype(F32)
            inverse = lax.rsqrt(jnp.mean(values * values, axis=1, keepdims=True) + EPS)
            act[block * rows : (block + 1) * rows, :] = (values * inverse * gain[...]).astype(BF16)
        first = side * half * rows
        sums = jnp.zeros((half * rows, columns), F32)
        for source in range(shards):
            sums = sums + product(
                act[first : first + half * rows, source * part : (source + 1) * part],
                weights[source, :part, :],
                1,
                0,
            )
        for block in range(half):
            place = pl.multiple_of(index_ref[side * half + block] * rows, rows)
            cosine_rows = cosine[pl.ds(place, rows), :]
            sine_rows = sine[pl.ds(place, rows), :]
            for group in range(groups):
                piece = sums[block * rows : (block + 1) * rows, group * 128 : (group + 1) * 128]
                cosine_part, sine_part = rope_tables(cosine_rows, sine_rows, group == groups - 1)
                mixed[pl.ds(place, rows), group * 128 : (group + 1) * 128] = (
                    piece * cosine_part + turn_signed(piece, sine_part)
                ).astype(BF16)
    scale = HD ** (-0.5)
    for first in range(0, total, Q_ROWS):
        keys = first + Q_ROWS
        allowed = score_mask(starts_ref, first, Q_ROWS, keys)
        key_rows = mixed[:keys, q_cols : q_cols + HD]
        value_rows = mixed[:keys, q_cols + HD : q_cols + 2 * HD]
        for head in range(q_cols // HD):
            query = mixed[first:keys, head * HD : (head + 1) * HD] * jnp.asarray(scale, BF16)
            scores = jnp.where(allowed, product(query, key_rows, 1, 1), MASKED)
            largest = jnp.max(scores, axis=1, keepdims=True)
            weights_row = jnp.exp(scores - largest)
            total_weight = jnp.sum(weights_row, axis=1, keepdims=True)
            attended = product(weights_row.astype(BF16), value_rows, 1, 0) / total_weight
            out_rows[first:keys, head * HD : (head + 1) * HD] = attended.astype(BF16)
            log_sums[first:keys, head : head + 1] = largest + jnp.log(total_weight)
    for block in range(shards):
        place = pl.multiple_of(index_ref[block] * rows, rows)
        out_rel[block * rows : (block + 1) * rows, :] = out_rows[pl.ds(place, rows), :]


def attention(index, starts, tokens, gain, weights, cosine, sine, q_cols):
    shards = len(tokens)
    rows, width = tokens[0].shape
    total = rows * shards
    columns = weights.shape[2]
    smem = pl.BlockSpec(memory_space=pltpu.SMEM)
    return pl.pallas_call(
        functools.partial(attention_body, shards, q_cols),
        out_shape=(
            pltpu.HBM((total, width), BF16),
            pltpu.HBM((total, columns), BF16),
            pltpu.HBM((total, q_cols), BF16),
            pltpu.HBM((total, q_cols // HD), F32),
        ),
        in_specs=[smem, smem] + whole_in_vmem(shards + 4),
        out_specs=tuple(whole_in_vmem(4)),
        scratch_shapes=[pltpu.VMEM((total, q_cols), BF16)],
        compiler_params=pltpu.CompilerParams(vmem_limit_bytes=48 * 2**20),
        cost_estimate=SHORT,
    )(index, starts, *in_hbm(*tokens, gain, weights, cosine, sine))


def attention_back_body(shards, rows, q_cols, waits, index_ref, starts_ref, *refs):
    branch = refs[:shards]
    w_out, mixed, log_sums, out_rel, cosine, sine = refs[shards : shards + 6]
    mixed_back, grad_out, *scratch = refs[shards + 6 + waits :]
    branch_rows, heads_back, query_grads, key_grads, value_grads = scratch
    total = rows * shards
    columns = mixed.shape[1]
    half = total // 2
    gain_terms = jnp.zeros(branch[0].shape[1:], F32)[None]
    for block in range(shards):
        branch_rows[block * rows : (block + 1) * rows, :] = branch[block][:rows, :]
        gain_terms = gain_terms + branch[block][rows:, :].astype(F32)[:1, :]
    grad_out[q_cols:, :] = jnp.broadcast_to(gain_terms, (16, gain_terms.shape[1])).astype(BF16)
    for side in range(2):
        back = product(branch_rows[side * half : (side + 1) * half, :], w_out[...], 1, 1).astype(
            BF16
        )
        for block in range(shards // 2):
            place = pl.multiple_of(index_ref[side * (shards // 2) + block] * rows, rows)
            heads_back[pl.ds(place, rows), :] = back[block * rows : (block + 1) * rows, :]
    grad_out[:q_cols, :] = product(out_rel[...], branch_rows[...], 0, 0).astype(BF16)
    key_grads[...] = jnp.zeros_like(key_grads)
    value_grads[...] = jnp.zeros_like(value_grads)
    scale = HD ** (-0.5)
    for first in range(0, total, Q_ROWS):
        keys = first + Q_ROWS
        allowed = score_mask(starts_ref, first, Q_ROWS, keys)
        key_rows = mixed[:keys, q_cols : q_cols + HD]
        value_rows = mixed[:keys, q_cols + HD : q_cols + 2 * HD]
        for head in range(q_cols // HD):
            cut = slice(head * HD, (head + 1) * HD)
            query = mixed[first:keys, cut] * jnp.asarray(scale, BF16)
            back = heads_back[first:keys, cut]
            scores = jnp.where(allowed, product(query, key_rows, 1, 1), MASKED)
            probs = jnp.exp(scores - log_sums[first:keys, head : head + 1])
            probs_back = product(back, value_rows, 1, 1)
            delta = jnp.sum(probs * probs_back, axis=1, keepdims=True)
            scores_back = (probs * (probs_back - delta)).astype(BF16)
            query_grads[first:keys, cut] = product(scores_back, key_rows, 1, 0) * scale
            key_grads[:keys, :] += product(scores_back, query, 0, 0)
            value_grads[:keys, :] += product(probs.astype(BF16), back, 0, 0)
    for block in range(shards):
        place = pl.multiple_of(index_ref[block] * rows, rows)
        window = pl.ds(place, rows)
        cosine_rows, sine_rows = cosine[window, :], sine[window, :]
        for group in range(columns // 128):
            last = group == columns // 128 - 1
            if last:
                piece = jnp.concatenate([key_grads[window, :], value_grads[window, :]], axis=1)
            else:
                piece = query_grads[window, group * 128 : (group + 1) * 128]
            cosine_part, sine_part = rope_tables(cosine_rows, sine_rows, last)
            mixed_back[block * rows : (block + 1) * rows, group * 128 : (group + 1) * 128] = (
                piece * cosine_part - turn_signed(piece, sine_part)
            ).astype(BF16)


def attention_back(
    index, starts, branch, w_out, mixed, log_sums, out_rel, cosine, sine, waits=()
):
    shards = len(branch)
    width = branch[0].shape[1]
    total, columns = mixed.shape
    rows = total // shards
    q_cols = out_rel.shape[1]
    smem = pl.BlockSpec(memory_space=pltpu.SMEM)
    return pl.pallas_call(
        functools.partial(attention_back_body, shards, rows, q_cols, len(waits)),
        out_shape=(
            pltpu.HBM((total, columns), BF16),
            pltpu.HBM((q_cols + 16, width), BF16),
        ),
        in_specs=[smem, smem]
        + whole_in_vmem(shards + 6)
        + [pl.BlockSpec(memory_space=pl.ANY)] * len(waits),
        out_specs=tuple(whole_in_vmem(2)),
        scratch_shapes=[
            pltpu.VMEM((total, width), BF16),
            pltpu.VMEM((total, q_cols), BF16),
            pltpu.VMEM((total, q_cols), F32),
            pltpu.VMEM((total, HD), F32),
            pltpu.VMEM((total, HD), F32),
        ],
        compiler_params=pltpu.CompilerParams(vmem_limit_bytes=48 * 2**20),
        cost_estimate=SHORT,
    )(index, starts, *in_hbm(*branch, w_out, mixed, log_sums, out_rel, cosine, sine, *waits))


def ffn_body(pieces, *refs):
    act, cot = refs[:pieces], refs[pieces : 2 * pieces]
    w_gate, w_up, w_down = refs[2 * pieces : 2 * pieces + 3]
    hidden, gate_back, up_back, act_out, cot_out, act_rows, cot_rows = refs[2 * pieces + 3 :]
    step = pl.program_id(0)

    @pl.when(step == 0)
    def _():
        for parts, rows in ((act, act_rows), (cot, cot_rows)):
            first = 0
            for part in parts:
                rows[first : first + part.shape[0], :] = part[...]
                first += part.shape[0]

    strip = act_out.shape[1]
    window = pl.ds(pl.multiple_of(step * strip, strip), strip)
    act_out[...] = act_rows[:, window]
    cot_out[...] = cot_rows[:, window]
    gate_value = product(act_rows[...], w_gate[...], 1, 0)
    up_value = product(act_rows[...], w_up[...], 1, 0)
    hidden_back = product(cot_rows[...], w_down[...], 1, 1)
    sigmoid_gate = 1.0 / (1.0 + jnp.exp(-gate_value))
    silu_gate = gate_value * sigmoid_gate
    hidden[...] = (silu_gate * up_value).astype(BF16)
    gate_back[...] = (
        hidden_back * up_value * sigmoid_gate * (1.0 + gate_value * (1.0 - sigmoid_gate))
    ).astype(BF16)
    up_back[...] = (hidden_back * silu_gate).astype(BF16)


def ffn(act, cot, w_gate, w_up, w_down):
    pieces = len(act)
    rows, width = act[0].shape
    total = rows * pieces
    units = w_gate.shape[1]
    tile = min(256, units)
    steps = units // tile
    strip = width // steps
    block = pl.BlockSpec((rows, width), lambda j: (0, 0), pipeline_mode=pl.Buffered(1))
    columns = pl.BlockSpec((width, tile), lambda j: (0, j))
    out = pl.BlockSpec((total, tile), lambda j: (0, j))
    wide = pl.BlockSpec((total, strip), lambda j: (0, j))
    return pl.pallas_call(
        functools.partial(ffn_body, pieces),
        out_shape=(pltpu.HBM((total, units), BF16),) * 3 + (pltpu.HBM((total, width), BF16),) * 2,
        grid=(steps,),
        in_specs=[block] * (2 * pieces)
        + [columns, columns, pl.BlockSpec((tile, width), lambda j: (j, 0))],
        out_specs=(out, out, out, wide, wide),
        scratch_shapes=[pltpu.VMEM((total, width), BF16)] * 2,
        compiler_params=pltpu.CompilerParams(vmem_limit_bytes=48 * 2**20),
        cost_estimate=SHORT,
    )(*in_hbm(*act, *cot, w_gate, w_up, w_down))


def ffn_others_body(waits, which, act, cot, w_gate, w_up, w_down, *refs):
    hidden, gate_back, up_back = refs[waits:]
    act_rows = act[...].reshape(hidden.shape[0], w_gate.shape[0])
    cot_rows = cot[...].reshape(act_rows.shape)
    gate_value = product(act_rows, w_gate[...], 1, 0)
    up_value = product(act_rows, w_up[...], 1, 0)
    hidden_back = product(cot_rows, w_down[...], 1, 1)
    sigmoid_gate = 1.0 / (1.0 + jnp.exp(-gate_value))
    silu_gate = gate_value * sigmoid_gate
    hidden[...] = (silu_gate * up_value).astype(BF16)
    gate_back[...] = (
        hidden_back * up_value * sigmoid_gate * (1.0 + gate_value * (1.0 - sigmoid_gate))
    ).astype(BF16)
    up_back[...] = (hidden_back * silu_gate).astype(BF16)


def ffn_others(which, both, w_gate, w_up, w_down, waits=()):
    count = which.shape[0]
    _, shards, _, rows, width = both.shape
    units, total = w_gate.shape[1], shards * rows
    tile = min(512, units)

    def rows_spec(kind):
        return pl.BlockSpec(
            (None, shards, None, rows, width), lambda i, j, w: (w[i], 0, kind, 0, 0)
        )

    columns = pl.BlockSpec((width, tile), lambda i, j, w: (0, j))
    out = pl.BlockSpec((total, tile), lambda i, j, w: (i, j))
    return pl.pallas_call(
        functools.partial(ffn_others_body, len(waits)),
        out_shape=(pltpu.HBM((total * count, units), BF16),) * 3,
        grid_spec=pltpu.PrefetchScalarGridSpec(
            num_scalar_prefetch=1,
            grid=(count, units // tile),
            in_specs=[
                rows_spec(0),
                rows_spec(1),
                columns,
                columns,
                pl.BlockSpec((tile, width), lambda i, j, w: (j, 0)),
            ]
            + [pl.BlockSpec(memory_space=pl.ANY)] * len(waits),
            out_specs=(out, out, out),
        ),
        compiler_params=pltpu.CompilerParams(vmem_limit_bytes=58 * 2**20),
        cost_estimate=SHORT,
    )(which, *in_hbm(both, both, w_gate, w_up, w_down, *waits))


def act_back_body(gate_back, up_back, w_gate, w_up, *refs):
    out = refs[-1]
    out[...] = (
        product(gate_back[...], w_gate[...], 1, 1) + product(up_back[...], w_up[...], 1, 1)
    ).astype(out.dtype)


def act_back(side, gate_back, up_back, w_gate, w_up, dtype, waits=()):
    total, units = gate_back.shape[0] // 2, gate_back.shape[1]
    width = w_gate.shape[0]
    tile = 512
    rows = pl.BlockSpec((total, units), lambda j: (side, 0), pipeline_mode=pl.Buffered(1))
    weights = pl.BlockSpec((tile, units), lambda j: (j, 0))
    return pl.pallas_call(
        act_back_body,
        out_shape=pltpu.HBM((total, width), dtype),
        grid=(width // tile,),
        in_specs=[rows, rows, weights, weights]
        + [pl.BlockSpec(memory_space=pl.ANY)] * len(waits),
        out_specs=pl.BlockSpec((total, tile), lambda j: (0, j)),
        compiler_params=pltpu.CompilerParams(vmem_limit_bytes=32 * 2**20),
        cost_estimate=SHORT,
    )(*in_hbm(gate_back, up_back, w_gate, w_up, *waits))


def weight_grad_body(pieces, began, *refs):
    left, right, out = refs[:pieces], refs[pieces : 2 * pieces], refs[-1]
    total = product(left[0][...], right[0][...], 0, 0)
    if began:
        total = total + refs[2 * pieces][...]
    for piece in range(1, pieces):
        total = total + product(left[piece][...], right[piece][...], 0, 0)
    out[...] = total


def weight_grad(left, right, row_tile, column_tile, waits=(), began=None):
    pieces = len(left)
    rows, height = left[0].shape
    width = right[0].shape[1]
    row_tile, column_tile = min(row_tile, height), min(column_tile, width)
    tile_spec = pl.BlockSpec((row_tile, column_tile), lambda j, i: (i, j))
    start = () if began is None else (began,)
    return pl.pallas_call(
        functools.partial(weight_grad_body, pieces, began is not None),
        out_shape=pltpu.HBM((height, width), F32),
        grid=(width // column_tile, height // row_tile),
        in_specs=[pl.BlockSpec((rows, row_tile), lambda j, i: (0, i))] * pieces
        + [pl.BlockSpec((rows, column_tile), lambda j, i: (0, j))] * pieces
        + [tile_spec] * len(start)
        + [pl.BlockSpec(memory_space=pl.ANY)] * len(waits),
        out_specs=tile_spec,
        compiler_params=pltpu.CompilerParams(vmem_limit_bytes=48 * 2**20),
        cost_estimate=SHORT,
    )(*in_hbm(*left, *right, *start, *waits))


def pack_weights_body(shards, copies, w_query, w_key, w_value, gains, out):
    part, q_cols = w_query.shape[0], w_query.shape[1] // shards
    out[:, part:, :] = jnp.broadcast_to(gains[...][None], (shards,) + gains.shape)
    for shard in range(shards):
        head = shard // copies * HD
        out[shard, :part, :q_cols] = w_query[:, shard * q_cols : (shard + 1) * q_cols]
        out[shard, :part, q_cols:] = jnp.concatenate(
            [w_key[:, head : head + HD], w_value[:, head : head + HD]], axis=1
        )


def pack_weights(shards, copies, w_query, w_key, w_value, gain_attn, gain_mlp):
    part = w_query.shape[0]
    columns = w_query.shape[1] // shards + 2 * HD
    gains = jnp.zeros((16, columns), BF16)
    gains = gains.at[0, :part].set(gain_attn).at[1, :part].set(gain_mlp)
    return pl.pallas_call(
        functools.partial(pack_weights_body, shards, copies),
        out_shape=pltpu.HBM((shards, part + 16, columns), BF16),
        in_specs=whole_in_vmem(4),
        out_specs=whole_in_vmem(1)[0],
        compiler_params=pltpu.CompilerParams(vmem_limit_bytes=16 * 2**20),
    )(*in_hbm(w_query, w_key, w_value, gains))


def unpack_grads_body(q_cols, index_ref, *refs):
    pieces, weights = refs[:-7], refs[-7:-4]
    query, key, value, products = refs[-4:]
    shards, strip, _ = pieces[0].shape
    for number, piece in enumerate(pieces):
        rows = pl.ds(pl.multiple_of(index_ref[number] * strip, strip), strip)
        for shard in range(shards):
            query[rows, shard * q_cols : (shard + 1) * q_cols] = piece[shard, :, :q_cols].astype(
                F32
            )
        for shard in range(0, shards, 2):
            for place, out in ((q_cols, key), (q_cols + HD, value)):
                out[rows, shard * HD : (shard + 2) * HD] = jnp.concatenate(
                    [piece[shard + n, :, place : place + HD] for n in range(2)], axis=1
                ).astype(F32)
    total = jnp.zeros(products.shape, F32)
    for weight, grad in zip(weights, (query, key, value), strict=True):
        terms = weight[...].astype(F32) * grad[...]
        total = total + jnp.sum(terms, axis=1, keepdims=True)
    products[...] = total


def unpack_grads(index, pieces, weights, q_cols):
    shards, strip, _ = pieces[0].shape
    rows = strip * len(pieces)
    return pl.pallas_call(
        functools.partial(unpack_grads_body, q_cols),
        out_shape=(
            jax.ShapeDtypeStruct((rows, shards * q_cols), F32),
            jax.ShapeDtypeStruct((rows, shards * HD), F32),
            jax.ShapeDtypeStruct((rows, shards * HD), F32),
            jax.ShapeDtypeStruct((rows, 1), F32),
        ),
        in_specs=[pl.BlockSpec(memory_space=pltpu.SMEM)] + whole_in_vmem(len(pieces) + 3),
        out_specs=tuple(whole_in_vmem(4)),
        compiler_params=pltpu.CompilerParams(vmem_limit_bytes=24 * 2**20),
    )(index, *in_hbm(*pieces, *weights))


def grad_others_body(count, kind, which, *refs):
    rows, units, began = refs[:count], refs[count : 2 * count], refs[2 * count]
    out = refs[-1]
    total = began[...]
    for one, two in zip(rows, units, strict=True):
        one = one[...].reshape(two.shape[0], one.shape[-1])
        if kind:
            total = total + product(two[...], one, 0, 0)
        else:
            total = total + product(one, two[...], 0, 0)
    out[...] = total


def grad_others(which, both, kind, units_all, began, row_tile, column_tile, waits=()):
    count = which.shape[0]
    shards, rows = both.shape[1], both.shape[3]
    total = shards * rows
    height, width = began.shape
    wide, narrow = (column_tile, row_tile) if kind else (row_tile, column_tile)

    def rows_spec(number):
        def place(j, i, w):
            return (w[number], 0, kind, 0, j if kind else i)

        return pl.BlockSpec((None, shards, None, rows, wide), place)

    def units_spec(number):
        return pl.BlockSpec((total, narrow), lambda j, i, w: (number, i if kind else j))

    tile_spec = pl.BlockSpec((row_tile, column_tile), lambda j, i, w: (i, j))
    return pl.pallas_call(
        functools.partial(grad_others_body, count, kind),
        out_shape=pltpu.HBM((height, width), F32),
        grid_spec=pltpu.PrefetchScalarGridSpec(
            num_scalar_prefetch=1,
            grid=(width // column_tile, height // row_tile),
            in_specs=[rows_spec(n) for n in range(count)]
            + [units_spec(n) for n in range(count)]
            + [tile_spec]
            + [pl.BlockSpec(memory_space=pl.ANY)] * len(waits),
            out_specs=tile_spec,
        ),
        compiler_params=pltpu.CompilerParams(vmem_limit_bytes=48 * 2**20),
        cost_estimate=SHORT,
    )(which, *in_hbm(*[both] * count, *[units_all] * count, began, *waits))


def rows_product_body(turned, values, weights, *refs):
    out = refs[-1]
    out[...] = product(values[...], weights[...], 1, 1 if turned else 0).astype(out.dtype)


def rows_product(side, values, weights, turned=False, waits=()):
    rows, depth = values.shape[0] // 2, values.shape[1]
    width = weights.shape[0] if turned else weights.shape[1]
    tile = 512
    if turned:
        weight_spec = pl.BlockSpec((tile, depth), lambda j: (j, 0))
    else:
        weight_spec = pl.BlockSpec((depth, tile), lambda j: (0, j))
    return pl.pallas_call(
        functools.partial(rows_product_body, turned),
        out_shape=pltpu.HBM((rows, width), BF16),
        grid=(width // tile,),
        in_specs=[
            pl.BlockSpec((rows, depth), lambda j: (side, 0), pipeline_mode=pl.Buffered(1)),
            weight_spec,
        ]
        + [pl.BlockSpec(memory_space=pl.ANY)] * len(waits),
        out_specs=pl.BlockSpec((rows, tile), lambda j: (0, j)),
        compiler_params=pltpu.CompilerParams(vmem_limit_bytes=24 * 2**20),
        cost_estimate=SHORT,
    )(*in_hbm(values, weights, *waits))


def small_call(body, out_shape, *operands):
    return pl.pallas_call(
        body,
        out_shape=tuple(pltpu.HBM(shape, dtype) for shape, dtype in out_shape),
        in_specs=whole_in_vmem(len(operands)),
        out_specs=tuple(whole_in_vmem(len(out_shape))),
        compiler_params=pltpu.CompilerParams(vmem_limit_bytes=24 * 2**20),
        cost_estimate=SHORT,
    )(*in_hbm(*operands))


def halves_body(near, next_row, upper, lower):
    half = upper.shape[0]
    upper[...] = near[:half, :]
    lower[...] = next_row[half:, :]


def join_body(upper, lower, out):
    half = upper.shape[0]
    out[:half, :] = upper[...]
    out[half:, :] = lower[...]


def pairs_body(even, got, own, *outs):
    rows = own.shape[0]
    for number, out in enumerate((own, *outs)):
        window = slice(number * rows, (number + 1) * rows)
        total = even[window, :].astype(F32) + got[window, :].astype(F32)
        out[...] = total.astype(out.dtype)


def row_mean(values):
    return jnp.mean(values, axis=1, keepdims=True)


def summed(terms):
    total = terms[0][...].astype(F32)
    for one in terms[1:]:
        total = total + one[...].astype(F32)
    return total


def norm_two_body(tokens, gain, *refs):
    terms, (hidden_one, act_two) = refs[:-2], refs[-2:]
    total = tokens[...].astype(F32) + summed(terms)
    hidden_one[...] = total
    inverse = lax.rsqrt(row_mean(total * total) + EPS)
    act_two[...] = (total * inverse * gain[...]).astype(BF16)


def norm_back(values, gain, beside, terms):
    act_back = summed(terms)
    rows = values[...].astype(F32)
    inverse = lax.rsqrt(row_mean(rows * rows) + EPS)
    normed = rows * inverse
    scaled = act_back * gain[...]
    total = beside[...].astype(F32) + inverse * (scaled - normed * row_mean(scaled * normed))
    return total, act_back * normed


def norm_two_back_body(values, gain, beside, *refs):
    terms, (back, back_low) = refs[:-2], refs[-2:]
    rows = back.shape[0]
    back[...], gain_terms = norm_back(values, gain, beside, terms)
    back_low[:rows, :] = back[...].astype(BF16)
    gain_row = jnp.sum(gain_terms, axis=0, keepdims=True)
    back_low[rows:, :] = jnp.broadcast_to(gain_row, (16, back.shape[1])).astype(BF16)


def norm_one_back_body(values, gain, beside, *refs):
    terms, back = refs[:-1], refs[-1]
    back[...], _ = norm_back(values, gain, beside, terms)


def layer_out_body(hidden_one, *refs):
    refs[-1][...] = (hidden_one[...] + summed(refs[:-1])).astype(BF16)


def swap(values, distance, axis):
    size = lax.axis_size(axis)
    return lax.ppermute(values, axis, [(i, i ^ distance) for i in range(size)])


def block_order(shards):
    return list(range(0, shards, 2)) + list(range(1, shards, 2))


class RowGather:
    def __init__(self, values):
        self.values = values
        self.moving = [swap(values, 2, "sp"), swap(values, 4, "sp")]

    def forward(self):
        self.near, self.next_row = self.moving
        rows, width = self.values.shape
        half = rows // 32 * 16
        shapes = (((half, width), BF16), ((rows - half, width), BF16))
        upper, lower = small_call(halves_body, shapes, self.near, self.next_row)
        self.sent = upper
        self.moving = [swap(upper, 4, "sp"), swap(lower, 2, "sp")]

    def cores(self):
        (far,) = small_call(join_body, ((self.values.shape, BF16),), *self.moving)
        self.evens = [self.values, self.near, self.next_row, far]
        self.sent = far
        self.moving = [swap(block, 1, "sp") for block in self.evens]

    def blocks(self):
        return self.evens + self.moving


class RowSum:
    def __init__(self, odd_terms):
        self.moving = [swap(odd_terms, 1, "sp")]

    def add_pairs(self, even_terms):
        shape = (even_terms.shape[0] // 4, even_terms.shape[1])
        self.own, *self.sent = small_call(
            pairs_body, ((shape, F32), *((shape, BF16),) * 3), even_terms, *self.moving
        )
        self.moving = [swap(one, n, "sp") for one, n in zip(self.sent, (2, 4, 6), strict=True)]

    def terms(self):
        return self.own, *self.moving


class DpSum:
    def __init__(self, terms):
        rank, groups = lax.axis_index("dp"), lax.axis_size("dp")
        self.own = lax.dynamic_index_in_dim(terms, rank, 0, keepdims=False)
        self.sent = [
            lax.dynamic_index_in_dim(terms, rank ^ d, 0, keepdims=False).astype(BF16)
            for d in range(1, groups)
        ]
        self.moving = [swap(one, d, "dp") for d, one in enumerate(self.sent, 1)]

    def add(self):
        return self.own + sum(one.astype(F32) for one in self.moving)


def gather_rel(values):
    evens, distance = [values], 2
    while distance < lax.axis_size("sp"):
        evens = evens + [swap(block, distance, "sp") for block in evens]
        distance *= 2
    return evens + [swap(block, 1, "sp") for block in evens]


def scatter_rel(even_terms, odd_terms):
    shards = lax.axis_size("sp")
    got = swap(odd_terms, 1, "sp").astype(F32)
    sums = (even_terms.astype(F32) + got).reshape(shards // 2, -1, even_terms.shape[1])
    distance = shards // 2
    while distance > 1:
        kept = distance // 2
        sums = sums[:kept] + swap(sums[kept:].astype(BF16), distance, "sp").astype(F32)
        distance //= 2
    return sums[0]


def dp_share(piece):
    return [piece] + [swap(piece, d, "dp") for d in range(1, lax.axis_size("dp"))]


def on_device(
    tokens,
    doc_lengths,
    w_query,
    w_key,
    w_value,
    w_out,
    gain_attn,
    gain_mlp,
    w_gate,
    w_up,
    w_down,
    cotangent,
):
    shards = lax.axis_size("sp")
    groups = lax.axis_size("dp")
    seq_rank = lax.axis_index("sp")
    tok_rows, width = tokens.shape
    group_rows = tok_rows * shards
    heads_total = w_query.shape[1] // HD
    kv_total = w_key.shape[1] // HD
    copies = max(1, shards // kv_total)
    q_cols = heads_total // shards * HD
    part_rows = w_query.shape[0]
    half = shards // 2

    planned = shards == 8 and groups == 4
    w_mixed = pack_weights(shards, copies, w_query, w_key, w_value, gain_attn, gain_mlp)
    columns = w_mixed.shape[2]
    w_local = lax.all_to_all(w_mixed, "sp", split_axis=0, concat_axis=0, tiled=True)
    gain_one = w_local[:, part_rows, :part_rows].reshape(1, width).astype(F32)
    gain_two = w_local[:, part_rows + 1, :part_rows].reshape(1, width).astype(F32)

    lengths = doc_lengths[0]
    count = lengths.shape[0]
    before = jnp.arange(count)[None, :] < jnp.arange(count)[:, None]
    starts = jnp.sum(jnp.where(before, lengths[None, :], 0), axis=1).astype(jnp.int32)
    places = jnp.arange(group_rows, dtype=jnp.int32)
    begins = jnp.max(jnp.where(starts[None, :] <= places[:, None], starts[None, :], 0), axis=1)
    angles = (places - begins).astype(F32)[:, None] * frequencies(HD)[None, :]
    cosine_half, sine_half = jnp.cos(angles), jnp.sin(angles)
    cosine = jnp.concatenate([cosine_half] * 4, axis=1)
    sine = jnp.concatenate([-sine_half, sine_half] * 2, axis=1)
    index = jnp.asarray(block_order(shards), jnp.int32) ^ seq_rank.astype(jnp.int32)

    def attend(blocks, weights):
        gain = weights[:, part_rows, :part_rows].reshape(1, width).astype(F32)
        return attention(index, starts, blocks, gain, weights, cosine, sine, q_cols)

    half_rows = group_rows // 2

    def terms(values, weights, side, turned=False, waits=()):
        return rows_product(side, values, weights, turned, waits)

    rows_f32, rows_bf16 = ((tok_rows, width), F32), ((tok_rows, width), BF16)

    def norm_two(summed):
        return small_call(norm_two_body, (rows_f32, rows_bf16), tokens, gain_two, *summed)

    branch_shape = ((tok_rows + 16, width), BF16)

    def norm_two_back(summed, hidden_one):
        outs = (rows_f32, branch_shape)
        return small_call(norm_two_back_body, outs, hidden_one, gain_two, cotangent, *summed)

    def norm_one_back(summed, beside):
        (back,) = small_call(norm_one_back_body, (rows_f32,), tokens, gain_one, beside, *summed)
        return back

    def attend_back(blocks, waits=()):
        return attention_back(
            index, starts, blocks, w_out, mixed, log_sums, out_rel, cosine, sine, waits
        )

    strip = width // (shards * groups)

    def strips(grad_mixed):
        return jnp.transpose(grad_mixed.reshape(shards, groups, strip, columns), (1, 0, 2, 3))

    def to_rows(strip_sum):
        return lax.all_to_all(
            strip_sum.astype(BF16), "sp", split_axis=0, concat_axis=0, tiled=True
        )

    def grow(kind, works, began, *waits):
        cot_rows, act_rows = [work[4] for work in works], [work[3] for work in works]
        mine = [work[(1, 2, 0)[kind]] for work in works]
        if kind == 2:
            return weight_grad(mine, cot_rows, 1024, 512, waits, began)
        return weight_grad(act_rows, mine, 512, 1024, waits, began)

    w_projections = w_local[:, :part_rows, :].reshape(width, columns)
    dp_rank = lax.axis_index("dp").astype(jnp.int32)

    if planned:
        which = dp_rank ^ jnp.arange(1, groups, dtype=jnp.int32)
        token_gather = RowGather(tokens)
        *token_gather.moving, cosine, sine = together(*token_gather.moving, cosine, sine)
        token_gather.forward()
        token_gather.cores()
        *token_blocks, w_local = together(*token_gather.evens[1:], *token_gather.moving, w_local)
        token_blocks = [tokens] + token_blocks
        w_projections = w_local[:, :part_rows, :].reshape(width, columns)

        cot_gather = RowGather(after(cotangent, w_local))
        act_one, mixed, out_rel, log_sums = attend(token_blocks, w_local)
        out_rel, *cot_gather.moving = together(out_rel, *cot_gather.moving)

        cot_gather.forward()
        out_sum = RowSum(terms(out_rel, w_out, 1))
        out_even = terms(out_rel, w_out, 0)
        out_even, *moving = together(out_even, *out_sum.moving, *cot_gather.moving)
        out_sum.moving, cot_gather.moving = moving[:1], moving[1:]

        out_sum.add_pairs(out_even)
        cot_gather.cores()
        out_sum.moving = together(*out_sum.moving)
        hidden_one, act_two = norm_two(out_sum.terms())

        act_gather = RowGather(act_two)
        both = jnp.stack([act_two, cotangent])
        both = lax.all_gather(both, ("dp", "sp"), axis=0).reshape(
            groups, shards, 2, tok_rows, width
        )
        act_gather.moving = together(*act_gather.moving)
        act_gather.forward()
        act_gather.cores()
        *act_gather.moving, one, two, three, four = together(
            *act_gather.moving, *cot_gather.moving
        )
        cot_gather.moving = [one, two, three, four]

        own = ffn(act_gather.blocks(), cot_gather.blocks(), w_gate, w_up, w_down)
        back_sum = RowSum(act_back(1, own[1], own[2], w_gate, w_up, BF16))
        even_back = act_back(0, own[1], own[2], w_gate, w_up, BF16, (own[0],))
        even_back, *back_sum.moving = together(even_back, *back_sum.moving)

        back_sum.add_pairs(even_back)
        mlp_odd = terms(own[0], w_down, 1, False, back_sum.sent)
        grad_gate = grow(0, [own], None, mlp_odd)
        grad_up = grow(1, [own], None, grad_gate)
        grad_up, mlp_odd, *back_sum.moving = together(grad_up, mlp_odd, *back_sum.moving)
        hidden_one_back, branch = norm_two_back(back_sum.terms(), hidden_one)

        branch_gather = RowGather(branch)
        mlp_sum = RowSum(after(mlp_odd, branch))
        mlp_even = terms(own[0], w_down, 0, False, (branch,))
        grad_down = grow(2, [own], None, mlp_even)
        grad_down, mlp_even, *moving = together(
            grad_down, mlp_even, *branch_gather.moving, *mlp_sum.moving
        )
        branch_gather.moving, mlp_sum.moving = moving[:2], moving[2:]

        branch_gather.forward()
        branch_gather.cores()
        mlp_even, *branch_gather.moving = together(mlp_even, *branch_gather.moving)
        mlp_sum.add_pairs(mlp_even)
        mixed_back, grad_out_terms = attend_back(branch_gather.blocks(), mlp_sum.sent)
        grad_mixed = weight_grad([act_one], [mixed_back], 512, columns)
        one_odd = terms(mixed_back, w_projections, 1, True, (grad_mixed,))
        one_even = terms(mixed_back, w_projections, 0, True, (one_odd,))
        one_odd, one_even, grad_mixed, grad_out_terms, *mlp_sum.moving = together(
            one_odd, one_even, grad_mixed, grad_out_terms, *mlp_sum.moving
        )

        mixed_sum = DpSum(strips(grad_mixed))
        one_sum = RowSum(one_odd)
        others = ffn_others(which, both, w_gate, w_up, w_down, mixed_sum.sent)
        grad_out = lax.psum(grad_out_terms, "dp")
        *others, one_even, got, one, two, three = together(
            *others, one_even, *one_sum.moving, *mixed_sum.moving
        )
        one_sum.moving, mixed_sum.moving = [got], [one, two, three]

        mixed_strip = mixed_sum.add().astype(BF16)
        mixed_rows = to_rows(mixed_strip)
        one_sum.add_pairs(one_even)
        grad_gate = grad_others(
            which, both, 0, others[1], grad_gate, 512, 1024, (*one_sum.sent, mixed_strip)
        )
        (layer_out,) = small_call(
            layer_out_body, (rows_bf16,), after(hidden_one, grad_gate), *mlp_sum.terms()
        )
        layer_out, mixed_rows, *one_sum.moving = together(
            layer_out, mixed_rows, *one_sum.moving
        )

        mixed_pieces = dp_share(mixed_rows)
        grad_tokens = norm_one_back(one_sum.terms(), after(hidden_one_back, mixed_rows))
        grad_up = grad_others(
            which, both, 0, others[2], grad_up, 512, 1024, (mixed_rows, grad_tokens)
        )
        grad_down = grad_others(which, both, 1, others[0], grad_down, 1024, 512, (grad_up,))
        grad_down, *moving = together(grad_down, *mixed_pieces[1:])
        mixed_pieces = mixed_pieces[:1] + moving
        grad_out = after(grad_out, grad_down).astype(F32)
    else:
        act_one, mixed, out_rel, log_sums = attend(gather_rel(tokens), w_local)
        hidden_one, act_two = norm_two(
            (scatter_rel(terms(out_rel, w_out, 0), terms(out_rel, w_out, 1)),)
        )
        act_blocks, cot_blocks, half = gather_rel(act_two), gather_rel(cotangent), shards // 2
        own = [
            jnp.concatenate(parts, axis=0)
            for parts in zip(
                ffn(act_blocks[:half], cot_blocks[:half], w_gate, w_up, w_down),
                ffn(act_blocks[half:], cot_blocks[half:], w_gate, w_up, w_down),
                strict=True,
            )
        ]
        act_two_back = scatter_rel(
            act_back(0, own[1], own[2], w_gate, w_up, BF16),
            act_back(1, own[1], own[2], w_gate, w_up, BF16),
        )
        hidden_one_back, branch = norm_two_back((act_two_back,), hidden_one)
        mixed_back, grad_out_terms = attend_back(gather_rel(branch))
        act_one_back = scatter_rel(
            terms(mixed_back, w_projections, 0, True), terms(mixed_back, w_projections, 1, True)
        )
        mixed_rows = to_rows(DpSum(strips(contract(act_one, mixed_back, 0, 0))).add())
        mixed_pieces = dp_share(mixed_rows)
        mlp_out = scatter_rel(terms(own[0], w_down, 0), terms(own[0], w_down, 1))
        layer_out = (hidden_one + mlp_out).astype(BF16)
        grad_tokens = norm_one_back((act_one_back,), hidden_one_back)
        grad_out, grad_gate, grad_up, grad_down = (
            lax.psum(grad.astype(BF16), "dp").astype(F32)
            for grad in (grad_out_terms, *(grow(kind, [own], None) for kind in range(3)))
        )
    grad_gain_mlp = lax.dynamic_slice_in_dim(grad_out[q_cols], seq_rank * part_rows, part_rows, 0)
    grad_out = grad_out[:q_cols]
    if copies == 1:
        dp_index = dp_rank ^ jnp.arange(groups, dtype=jnp.int32)
        grad_query, grad_key, grad_value, products = unpack_grads(
            dp_index, mixed_pieces, (w_query, w_key, w_value), q_cols
        )
        products = products.reshape(part_rows)
    else:
        parts = jnp.zeros((groups,) + mixed_pieces[0].shape, F32)
        for d, one in enumerate(mixed_pieces):
            parts = lax.dynamic_update_index_in_dim(parts, one.astype(F32), dp_rank ^ d, 0)
        parts = jnp.transpose(parts, (0, 2, 1, 3)).reshape(part_rows, shards, columns)
        grad_query = parts[:, :, :q_cols].reshape(part_rows, shards * q_cols)
        grad_key, grad_value = (
            parts[:, :, first : first + HD]
            .reshape(part_rows, kv_total, copies, HD)
            .sum(axis=2)
            .reshape(part_rows, -1)
            for first in (q_cols, q_cols + HD)
        )
        products = sum(
            jnp.sum(weight.astype(F32) * grad, axis=1)
            for weight, grad in (
                (w_query, grad_query),
                (w_key, grad_key),
                (w_value, grad_value),
            )
        )
    grad_gain_attn = products / gain_attn.astype(F32)
    return (
        layer_out,
        grad_tokens,
        grad_query,
        grad_key,
        grad_value,
        grad_out,
        grad_gain_attn,
        grad_gain_mlp,
        grad_gate,
        grad_up,
        grad_down,
    )


def solution(mesh):
    placed = (
        P(("dp", "sp"), None),
        P("dp", None),
        P("sp", None),
        P("sp", None),
        P("sp", None),
        P("sp", None),
        P("sp"),
        P("sp"),
        P(None, "sp"),
        P(None, "sp"),
        P("sp", None),
        P(("dp", "sp"), None),
    )
    return jax.shard_map(
        on_device,
        mesh=mesh,
        in_specs=placed,
        out_specs=(
            P(("dp", "sp"), None),
            P(("dp", "sp"), None),
            P("sp", None),
            P("sp", None),
            P("sp", None),
            P("sp", None),
            P("sp"),
            P("sp"),
            P(None, "sp"),
            P(None, "sp"),
            P("sp", None),
        ),
        check_vma=False,
    )
```

```python
import functools

import jax
import jax.numpy as jnp
from jax import lax
from jax.experimental import pallas as pl
from jax.experimental.pallas import tpu as pltpu
from jax.sharding import PartitionSpec as P

HD = 64
Q_ROWS = 256
F32 = jnp.float32
BF16 = jnp.bfloat16


EPS = 1e-05
THETA = 500000.0
FACTOR = 32.0
LOW_FACTOR = 1.0
HIGH_FACTOR = 4.0
BASE_CONTEXT = 8192.0
MASKED = -1e30


def frequencies(head_size):
    half_index = jnp.arange(head_size // 2).astype(jnp.float32)
    inverse = THETA ** (-2.0 * half_index / head_size)
    wavelength = 2.0 * jnp.pi / inverse
    smooth = (BASE_CONTEXT / wavelength - LOW_FACTOR) / (HIGH_FACTOR - LOW_FACTOR)
    middle = (1.0 - smooth) * inverse / FACTOR + smooth * inverse
    slow_band = jnp.where(wavelength > BASE_CONTEXT / LOW_FACTOR, inverse / FACTOR, middle)
    return jnp.where(wavelength < BASE_CONTEXT / HIGH_FACTOR, inverse, slow_band)


def contract(left, right, left_dim, right_dim):
    return lax.dot_general(
        left, right, (((left_dim,), (right_dim,)), ((), ())), preferred_element_type=jnp.float32
    )


SHORT = pl.CostEstimate(flops=0, bytes_accessed=0, transcendentals=0)


def product(left, right, left_dim, right_dim):
    return lax.dot_general(
        left, right, (((left_dim,), (right_dim,)), ((), ())), preferred_element_type=F32
    )


def whole_in_vmem(count):
    return [pl.BlockSpec(memory_space=pltpu.VMEM)] * count


def in_hbm(*values):
    return [pltpu.with_memory_space_constraint(one, pltpu.HBM) for one in values]


def after(values, *earlier):
    def body(*refs):
        pass

    return pl.pallas_call(
        body,
        out_shape=pltpu.HBM(values.shape, values.dtype),
        in_specs=[pl.BlockSpec(memory_space=pl.ANY)] * (1 + len(earlier)),
        out_specs=pl.BlockSpec(memory_space=pl.ANY),
        input_output_aliases={0: 0},
        cost_estimate=pl.CostEstimate(flops=0, bytes_accessed=0, transcendentals=0),
    )(*in_hbm(values, *earlier))


def together(*values):
    def body(*refs):
        pass

    anywhere = pl.BlockSpec(memory_space=pl.ANY)
    call = pl.pallas_call(
        body,
        out_shape=tuple(pltpu.HBM(one.shape, one.dtype) for one in values),
        in_specs=[anywhere] * len(values),
        out_specs=(anywhere,) * len(values),
        input_output_aliases={n: n for n in range(len(values))},
        cost_estimate=pl.CostEstimate(flops=0, bytes_accessed=0, transcendentals=0),
    )
    return list(call(*in_hbm(*values)))


def turn_signed(values, signed_sine):
    lane = lax.broadcasted_iota(jnp.int32, values.shape, 1) % HD
    turned = jnp.where(
        lane < HD // 2, pltpu.roll(values, 128 - HD // 2, 1), pltpu.roll(values, HD // 2, 1)
    )
    return turned * signed_sine


def rope_tables(cosine, sine, last):
    if not last:
        return cosine, sine
    lane = lax.broadcasted_iota(jnp.int32, cosine.shape, 1)
    return jnp.where(lane < HD, cosine, 1.0), jnp.where(lane < HD, sine, 0.0)


def score_mask(starts_ref, first_row, rows, keys):
    place = first_row + lax.broadcasted_iota(jnp.int32, (rows, 1), 0)
    begin = jnp.zeros((rows, 1), jnp.int32)
    for index in range(starts_ref.shape[0]):
        start = starts_ref[index]
        begin = jnp.maximum(begin, jnp.where(place >= start, start, 0))
    key_place = lax.broadcasted_iota(jnp.int32, (rows, keys), 1)
    return (key_place >= begin) & (key_place <= place)


def attention_body(shards, q_cols, index_ref, starts_ref, *refs):
    tokens = refs[:shards]
    gain, weights, cosine, sine, w_out = refs[shards : shards + 5]
    act, mixed, out_rel, log_sums, even_terms, odd_terms, out_rows = refs[shards + 5 :]
    rows = tokens[0].shape[0]
    total = rows * shards
    part = act.shape[1] // shards
    columns = mixed.shape[1]
    groups = columns // 128
    half = shards // 2
    for side in range(2):
        for block in range(side * half, side * half + half):
            values = tokens[block][...].astype(F32)
            inverse = lax.rsqrt(jnp.mean(values * values, axis=1, keepdims=True) + EPS)
            act[block * rows : (block + 1) * rows, :] = (values * inverse * gain[...]).astype(BF16)
        first = side * half * rows
        sums = jnp.zeros((half * rows, columns), F32)
        for source in range(shards):
            sums = sums + product(
                act[first : first + half * rows, source * part : (source + 1) * part],
                weights[source, :part, :],
                1,
                0,
            )
        for block in range(half):
            place = pl.multiple_of(index_ref[side * half + block] * rows, rows)
            cosine_rows = cosine[pl.ds(place, rows), :]
            sine_rows = sine[pl.ds(place, rows), :]
            for group in range(groups):
                piece = sums[block * rows : (block + 1) * rows, group * 128 : (group + 1) * 128]
                cosine_part, sine_part = rope_tables(cosine_rows, sine_rows, group == groups - 1)
                mixed[pl.ds(place, rows), group * 128 : (group + 1) * 128] = (
                    piece * cosine_part + turn_signed(piece, sine_part)
                ).astype(BF16)
    scale = HD ** (-0.5)
    for first in range(0, total, Q_ROWS):
        keys = first + Q_ROWS
        allowed = score_mask(starts_ref, first, Q_ROWS, keys)
        key_rows = mixed[:keys, q_cols : q_cols + HD]
        value_rows = mixed[:keys, q_cols + HD : q_cols + 2 * HD]
        for head in range(q_cols // HD):
            query = mixed[first:keys, head * HD : (head + 1) * HD] * jnp.asarray(scale, BF16)
            scores = jnp.where(allowed, product(query, key_rows, 1, 1), MASKED)
            largest = jnp.max(scores, axis=1, keepdims=True)
            weights_row = jnp.exp(scores - largest)
            total_weight = jnp.sum(weights_row, axis=1, keepdims=True)
            attended = product(weights_row.astype(BF16), value_rows, 1, 0) / total_weight
            out_rows[first:keys, head * HD : (head + 1) * HD] = attended.astype(BF16)
            log_sums[first:keys, head : head + 1] = largest + jnp.log(total_weight)
    for block in range(shards):
        place = pl.multiple_of(index_ref[block] * rows, rows)
        out_rel[block * rows : (block + 1) * rows, :] = out_rows[pl.ds(place, rows), :]
    width = w_out.shape[1]
    for side, terms in enumerate((even_terms, odd_terms)):
        heads = out_rel[side * half * rows : (side + 1) * half * rows, :]
        for first in range(0, width, 512):
            cut = slice(first, first + 512)
            terms[:, cut] = product(heads, w_out[:, cut], 1, 0).astype(BF16)


def attention(index, starts, tokens, gain, weights, cosine, sine, w_out, q_cols):
    shards = len(tokens)
    rows, width = tokens[0].shape
    total = rows * shards
    columns = weights.shape[2]
    smem = pl.BlockSpec(memory_space=pltpu.SMEM)
    return pl.pallas_call(
        functools.partial(attention_body, shards, q_cols),
        out_shape=(
            pltpu.HBM((total, width), BF16),
            pltpu.HBM((total, columns), BF16),
            pltpu.HBM((total, q_cols), BF16),
            pltpu.HBM((total, q_cols // HD), F32),
            pltpu.HBM((total // 2, width), BF16),
            pltpu.HBM((total // 2, width), BF16),
        ),
        in_specs=[smem, smem] + whole_in_vmem(shards + 5),
        out_specs=tuple(whole_in_vmem(6)),
        scratch_shapes=[pltpu.VMEM((total, q_cols), BF16)],
        compiler_params=pltpu.CompilerParams(vmem_limit_bytes=58 * 2**20),
        cost_estimate=SHORT,
    )(index, starts, *in_hbm(*tokens, gain, weights, cosine, sine, w_out))


def attention_back_body(shards, rows, q_cols, waits, index_ref, starts_ref, *refs):
    branch = refs[:shards]
    w_out, mixed, log_sums, out_rel, cosine, sine = refs[shards : shards + 6]
    mixed_back, grad_out, *scratch = refs[shards + 6 + waits :]
    branch_rows, heads_back, query_grads, key_grads, value_grads = scratch
    total = rows * shards
    columns = mixed.shape[1]
    half = total // 2
    gain_terms = jnp.zeros(branch[0].shape[1:], F32)[None]
    for block in range(shards):
        branch_rows[block * rows : (block + 1) * rows, :] = branch[block][:rows, :]
        gain_terms = gain_terms + branch[block][rows:, :].astype(F32)[:1, :]
    grad_out[q_cols:, :] = jnp.broadcast_to(gain_terms, (16, gain_terms.shape[1])).astype(BF16)
    for side in range(2):
        back = product(branch_rows[side * half : (side + 1) * half, :], w_out[...], 1, 1).astype(
            BF16
        )
        for block in range(shards // 2):
            place = pl.multiple_of(index_ref[side * (shards // 2) + block] * rows, rows)
            heads_back[pl.ds(place, rows), :] = back[block * rows : (block + 1) * rows, :]
    grad_out[:q_cols, :] = product(out_rel[...], branch_rows[...], 0, 0).astype(BF16)
    key_grads[...] = jnp.zeros_like(key_grads)
    value_grads[...] = jnp.zeros_like(value_grads)
    scale = HD ** (-0.5)
    for first in range(0, total, Q_ROWS):
        keys = first + Q_ROWS
        allowed = score_mask(starts_ref, first, Q_ROWS, keys)
        key_rows = mixed[:keys, q_cols : q_cols + HD]
        value_rows = mixed[:keys, q_cols + HD : q_cols + 2 * HD]
        for head in range(q_cols // HD):
            cut = slice(head * HD, (head + 1) * HD)
            query = mixed[first:keys, cut] * jnp.asarray(scale, BF16)
            back = heads_back[first:keys, cut]
            scores = jnp.where(allowed, product(query, key_rows, 1, 1), MASKED)
            probs = jnp.exp(scores - log_sums[first:keys, head : head + 1])
            probs_back = product(back, value_rows, 1, 1)
            delta = jnp.sum(probs * probs_back, axis=1, keepdims=True)
            scores_back = (probs * (probs_back - delta)).astype(BF16)
            query_grads[first:keys, cut] = product(scores_back, key_rows, 1, 0) * scale
            key_grads[:keys, :] += product(scores_back, query, 0, 0)
            value_grads[:keys, :] += product(probs.astype(BF16), back, 0, 0)
    for block in range(shards):
        place = pl.multiple_of(index_ref[block] * rows, rows)
        window = pl.ds(place, rows)
        cosine_rows, sine_rows = cosine[window, :], sine[window, :]
        for group in range(columns // 128):
            last = group == columns // 128 - 1
            if last:
                piece = jnp.concatenate([key_grads[window, :], value_grads[window, :]], axis=1)
            else:
                piece = query_grads[window, group * 128 : (group + 1) * 128]
            cosine_part, sine_part = rope_tables(cosine_rows, sine_rows, last)
            mixed_back[block * rows : (block + 1) * rows, group * 128 : (group + 1) * 128] = (
                piece * cosine_part - turn_signed(piece, sine_part)
            ).astype(BF16)


def attention_back(
    index, starts, branch, w_out, mixed, log_sums, out_rel, cosine, sine, waits=()
):
    shards = len(branch)
    width = branch[0].shape[1]
    total, columns = mixed.shape
    rows = total // shards
    q_cols = out_rel.shape[1]
    smem = pl.BlockSpec(memory_space=pltpu.SMEM)
    return pl.pallas_call(
        functools.partial(attention_back_body, shards, rows, q_cols, len(waits)),
        out_shape=(
            pltpu.HBM((total, columns), BF16),
            pltpu.HBM((q_cols + 16, width), BF16),
        ),
        in_specs=[smem, smem]
        + whole_in_vmem(shards + 6)
        + [pl.BlockSpec(memory_space=pl.ANY)] * len(waits),
        out_specs=tuple(whole_in_vmem(2)),
        scratch_shapes=[
            pltpu.VMEM((total, width), BF16),
            pltpu.VMEM((total, q_cols), BF16),
            pltpu.VMEM((total, q_cols), F32),
            pltpu.VMEM((total, HD), F32),
            pltpu.VMEM((total, HD), F32),
        ],
        compiler_params=pltpu.CompilerParams(vmem_limit_bytes=48 * 2**20),
        cost_estimate=SHORT,
    )(index, starts, *in_hbm(*branch, w_out, mixed, log_sums, out_rel, cosine, sine, *waits))


def ffn_body(pieces, *refs):
    act, cot = refs[:pieces], refs[pieces : 2 * pieces]
    w_gate, w_up, w_down = refs[2 * pieces : 2 * pieces + 3]
    hidden, gate_back, up_back, act_out, cot_out, act_rows, cot_rows = refs[2 * pieces + 3 :]
    step = pl.program_id(0)

    @pl.when(step == 0)
    def _():
        for parts, rows in ((act, act_rows), (cot, cot_rows)):
            first = 0
            for part in parts:
                rows[first : first + part.shape[0], :] = part[...]
                first += part.shape[0]

    strip = act_out.shape[1]
    window = pl.ds(pl.multiple_of(step * strip, strip), strip)
    act_out[...] = act_rows[:, window]
    cot_out[...] = cot_rows[:, window]
    gate_value = product(act_rows[...], w_gate[...], 1, 0)
    up_value = product(act_rows[...], w_up[...], 1, 0)
    hidden_back = product(cot_rows[...], w_down[...], 1, 1)
    sigmoid_gate = 1.0 / (1.0 + jnp.exp(-gate_value))
    silu_gate = gate_value * sigmoid_gate
    hidden[...] = (silu_gate * up_value).astype(BF16)
    gate_back[...] = (
        hidden_back * up_value * sigmoid_gate * (1.0 + gate_value * (1.0 - sigmoid_gate))
    ).astype(BF16)
    up_back[...] = (hidden_back * silu_gate).astype(BF16)


def ffn(act, cot, w_gate, w_up, w_down):
    pieces = len(act)
    rows, width = act[0].shape
    total = rows * pieces
    units = w_gate.shape[1]
    tile = min(256, units)
    steps = units // tile
    strip = width // steps
    block = pl.BlockSpec((rows, width), lambda j: (0, 0), pipeline_mode=pl.Buffered(1))
    columns = pl.BlockSpec((width, tile), lambda j: (0, j))
    out = pl.BlockSpec((total, tile), lambda j: (0, j))
    wide = pl.BlockSpec((total, strip), lambda j: (0, j))
    return pl.pallas_call(
        functools.partial(ffn_body, pieces),
        out_shape=(pltpu.HBM((total, units), BF16),) * 3 + (pltpu.HBM((total, width), BF16),) * 2,
        grid=(steps,),
        in_specs=[block] * (2 * pieces)
        + [columns, columns, pl.BlockSpec((tile, width), lambda j: (j, 0))],
        out_specs=(out, out, out, wide, wide),
        scratch_shapes=[pltpu.VMEM((total, width), BF16)] * 2,
        compiler_params=pltpu.CompilerParams(vmem_limit_bytes=48 * 2**20),
        cost_estimate=SHORT,
    )(*in_hbm(*act, *cot, w_gate, w_up, w_down))


def ffn_others_body(waits, which, act, cot, w_gate, w_up, w_down, *refs):
    hidden, gate_back, up_back = refs[waits:]
    act_rows = act[...].reshape(hidden.shape[0], w_gate.shape[0])
    cot_rows = cot[...].reshape(act_rows.shape)
    gate_value = product(act_rows, w_gate[...], 1, 0)
    up_value = product(act_rows, w_up[...], 1, 0)
    hidden_back = product(cot_rows, w_down[...], 1, 1)
    sigmoid_gate = 1.0 / (1.0 + jnp.exp(-gate_value))
    silu_gate = gate_value * sigmoid_gate
    hidden[...] = (silu_gate * up_value).astype(BF16)
    gate_back[...] = (
        hidden_back * up_value * sigmoid_gate * (1.0 + gate_value * (1.0 - sigmoid_gate))
    ).astype(BF16)
    up_back[...] = (hidden_back * silu_gate).astype(BF16)


def ffn_others(which, both, w_gate, w_up, w_down, waits=()):
    count = which.shape[0]
    _, shards, _, rows, width = both.shape
    units, total = w_gate.shape[1], shards * rows
    tile = min(512, units)

    def rows_spec(kind):
        return pl.BlockSpec(
            (None, shards, None, rows, width), lambda i, j, w: (w[i], 0, kind, 0, 0)
        )

    columns = pl.BlockSpec((width, tile), lambda i, j, w: (0, j))
    out = pl.BlockSpec((total, tile), lambda i, j, w: (i, j))
    return pl.pallas_call(
        functools.partial(ffn_others_body, len(waits)),
        out_shape=(pltpu.HBM((total * count, units), BF16),) * 3,
        grid_spec=pltpu.PrefetchScalarGridSpec(
            num_scalar_prefetch=1,
            grid=(count, units // tile),
            in_specs=[
                rows_spec(0),
                rows_spec(1),
                columns,
                columns,
                pl.BlockSpec((tile, width), lambda i, j, w: (j, 0)),
            ]
            + [pl.BlockSpec(memory_space=pl.ANY)] * len(waits),
            out_specs=(out, out, out),
        ),
        compiler_params=pltpu.CompilerParams(vmem_limit_bytes=58 * 2**20),
        cost_estimate=SHORT,
    )(which, *in_hbm(both, both, w_gate, w_up, w_down, *waits))


def act_back_body(gate_back, up_back, w_gate, w_up, *refs):
    out = refs[-1]
    out[...] = (
        product(gate_back[...], w_gate[...], 1, 1) + product(up_back[...], w_up[...], 1, 1)
    ).astype(out.dtype)


def act_back(side, gate_back, up_back, w_gate, w_up, dtype, waits=()):
    total, units = gate_back.shape[0] // 2, gate_back.shape[1]
    width = w_gate.shape[0]
    tile = 512
    rows = pl.BlockSpec((total, units), lambda j: (side, 0), pipeline_mode=pl.Buffered(1))
    weights = pl.BlockSpec((tile, units), lambda j: (j, 0))
    return pl.pallas_call(
        act_back_body,
        out_shape=pltpu.HBM((total, width), dtype),
        grid=(width // tile,),
        in_specs=[rows, rows, weights, weights]
        + [pl.BlockSpec(memory_space=pl.ANY)] * len(waits),
        out_specs=pl.BlockSpec((total, tile), lambda j: (0, j)),
        compiler_params=pltpu.CompilerParams(vmem_limit_bytes=32 * 2**20),
        cost_estimate=SHORT,
    )(*in_hbm(gate_back, up_back, w_gate, w_up, *waits))


def weight_grad_body(pieces, began, *refs):
    left, right, out = refs[:pieces], refs[pieces : 2 * pieces], refs[-1]
    total = product(left[0][...], right[0][...], 0, 0)
    if began:
        total = total + refs[2 * pieces][...]
    for piece in range(1, pieces):
        total = total + product(left[piece][...], right[piece][...], 0, 0)
    out[...] = total.astype(out.dtype)


def weight_grad(left, right, row_tile, column_tile, waits=(), began=None, dtype=F32):
    pieces = len(left)
    rows, height = left[0].shape
    width = right[0].shape[1]
    row_tile, column_tile = min(row_tile, height), min(column_tile, width)
    tile_spec = pl.BlockSpec((row_tile, column_tile), lambda j, i: (i, j))
    start = () if began is None else (began,)
    return pl.pallas_call(
        functools.partial(weight_grad_body, pieces, began is not None),
        out_shape=pltpu.HBM((height, width), dtype),
        grid=(width // column_tile, height // row_tile),
        in_specs=[pl.BlockSpec((rows, row_tile), lambda j, i: (0, i))] * pieces
        + [pl.BlockSpec((rows, column_tile), lambda j, i: (0, j))] * pieces
        + [tile_spec] * len(start)
        + [pl.BlockSpec(memory_space=pl.ANY)] * len(waits),
        out_specs=tile_spec,
        compiler_params=pltpu.CompilerParams(vmem_limit_bytes=48 * 2**20),
        cost_estimate=SHORT,
    )(*in_hbm(*left, *right, *start, *waits))


def pack_weights_body(shards, copies, w_query, w_key, w_value, gains, out):
    part, q_cols = w_query.shape[0], w_query.shape[1] // shards
    out[:, part:, :] = jnp.broadcast_to(gains[...][None], (shards,) + gains.shape)
    for shard in range(shards):
        head = shard // copies * HD
        out[shard, :part, :q_cols] = w_query[:, shard * q_cols : (shard + 1) * q_cols]
        out[shard, :part, q_cols:] = jnp.concatenate(
            [w_key[:, head : head + HD], w_value[:, head : head + HD]], axis=1
        )


def pack_weights(shards, copies, w_query, w_key, w_value, gain_attn, gain_mlp):
    part = w_query.shape[0]
    columns = w_query.shape[1] // shards + 2 * HD
    gains = jnp.zeros((16, columns), BF16)
    gains = gains.at[0, :part].set(gain_attn).at[1, :part].set(gain_mlp)
    return pl.pallas_call(
        functools.partial(pack_weights_body, shards, copies),
        out_shape=pltpu.HBM((shards, part + 16, columns), BF16),
        in_specs=whole_in_vmem(4),
        out_specs=whole_in_vmem(1)[0],
        compiler_params=pltpu.CompilerParams(vmem_limit_bytes=16 * 2**20),
    )(*in_hbm(w_query, w_key, w_value, gains))


def unpack_grads_body(q_cols, pieces, *refs):
    weights = refs[:3]
    query, key, value, products = refs[3:]
    groups, shards, strip, _ = pieces.shape
    for number in range(groups):
        rows = slice(number * strip, (number + 1) * strip)
        for shard in range(shards):
            query[rows, shard * q_cols : (shard + 1) * q_cols] = pieces[
                number, shard, :, :q_cols
            ].astype(F32)
        for shard in range(0, shards, 2):
            for place, out in ((q_cols, key), (q_cols + HD, value)):
                out[rows, shard * HD : (shard + 2) * HD] = jnp.concatenate(
                    [pieces[number, shard + n, :, place : place + HD] for n in range(2)], axis=1
                ).astype(F32)
    total = jnp.zeros(products.shape, F32)
    for weight, grad in zip(weights, (query, key, value), strict=True):
        terms = weight[...].astype(F32) * grad[...]
        total = total + jnp.sum(terms, axis=1, keepdims=True)
    products[...] = total


def unpack_grads(pieces, weights, q_cols):
    groups, shards, strip, _ = pieces.shape
    rows = strip * groups
    return pl.pallas_call(
        functools.partial(unpack_grads_body, q_cols),
        out_shape=(
            jax.ShapeDtypeStruct((rows, shards * q_cols), F32),
            jax.ShapeDtypeStruct((rows, shards * HD), F32),
            jax.ShapeDtypeStruct((rows, shards * HD), F32),
            jax.ShapeDtypeStruct((rows, 1), F32),
        ),
        in_specs=whole_in_vmem(4),
        out_specs=tuple(whole_in_vmem(4)),
        compiler_params=pltpu.CompilerParams(vmem_limit_bytes=24 * 2**20),
    )(*in_hbm(pieces, *weights))


def grad_others_body(count, kind, which, *refs):
    rows, units, began = refs[:count], refs[count : 2 * count], refs[2 * count]
    out = refs[-1]
    total = began[...]
    for one, two in zip(rows, units, strict=True):
        one = one[...].reshape(two.shape[0], one.shape[-1])
        if kind:
            total = total + product(two[...], one, 0, 0)
        else:
            total = total + product(one, two[...], 0, 0)
    out[...] = total


def grad_others(which, both, kind, units_all, began, row_tile, column_tile, waits=()):
    count = which.shape[0]
    shards, rows = both.shape[1], both.shape[3]
    total = shards * rows
    height, width = began.shape
    wide, narrow = (column_tile, row_tile) if kind else (row_tile, column_tile)

    def rows_spec(number):
        def place(j, i, w):
            return (w[number], 0, kind, 0, j if kind else i)

        return pl.BlockSpec((None, shards, None, rows, wide), place)

    def units_spec(number):
        return pl.BlockSpec((total, narrow), lambda j, i, w: (number, i if kind else j))

    tile_spec = pl.BlockSpec((row_tile, column_tile), lambda j, i, w: (i, j))
    return pl.pallas_call(
        functools.partial(grad_others_body, count, kind),
        out_shape=pltpu.HBM((height, width), F32),
        grid_spec=pltpu.PrefetchScalarGridSpec(
            num_scalar_prefetch=1,
            grid=(width // column_tile, height // row_tile),
            in_specs=[rows_spec(n) for n in range(count)]
            + [units_spec(n) for n in range(count)]
            + [tile_spec]
            + [pl.BlockSpec(memory_space=pl.ANY)] * len(waits),
            out_specs=tile_spec,
        ),
        compiler_params=pltpu.CompilerParams(vmem_limit_bytes=48 * 2**20),
        cost_estimate=SHORT,
    )(which, *in_hbm(*[both] * count, *[units_all] * count, began, *waits))


def grad_pair_body(count, which, *refs):
    rows = [one[...] for one in refs[:count]]
    outs = refs[-2:]
    for kind, out in enumerate(outs):
        units = refs[count * (1 + kind) : count * (2 + kind)]
        total = refs[3 * count + kind][...]
        for one, two in zip(rows, units, strict=True):
            total = total + product(one.reshape(two.shape[0], one.shape[-1]), two[...], 0, 0)
        out[...] = total


def grad_pair(which, both, gates, ups, began_gate, began_up, row_tile, waits=()):
    count = which.shape[0]
    shards, rows = both.shape[1], both.shape[3]
    total = shards * rows
    height, width = began_gate.shape

    def rows_spec(number):
        return pl.BlockSpec(
            (None, shards, None, rows, row_tile), lambda i, w: (w[number], 0, 0, 0, i)
        )

    def units_spec(number):
        return pl.BlockSpec(
            (total, width), lambda i, w: (number, 0), pipeline_mode=pl.Buffered(1)
        )

    tile_spec = pl.BlockSpec((row_tile, width), lambda i, w: (i, 0))
    units_specs = [units_spec(n) for n in range(count)]
    return pl.pallas_call(
        functools.partial(grad_pair_body, count),
        out_shape=(pltpu.HBM((height, width), F32),) * 2,
        grid_spec=pltpu.PrefetchScalarGridSpec(
            num_scalar_prefetch=1,
            grid=(height // row_tile,),
            in_specs=[rows_spec(n) for n in range(count)]
            + units_specs
            + units_specs
            + [tile_spec] * 2
            + [pl.BlockSpec(memory_space=pl.ANY)] * len(waits),
            out_specs=(tile_spec, tile_spec),
        ),
        compiler_params=pltpu.CompilerParams(vmem_limit_bytes=56 * 2**20),
        cost_estimate=SHORT,
    )(
        which,
        *in_hbm(
            *[both] * count, *[gates] * count, *[ups] * count, began_gate, began_up, *waits
        ),
    )


def rows_product_body(turned, values, weights, *refs):
    out = refs[-1]
    out[...] = product(values[...], weights[...], 1, 1 if turned else 0).astype(out.dtype)


def rows_product(side, values, weights, turned=False, waits=()):
    rows, depth = values.shape[0] // 2, values.shape[1]
    width = weights.shape[0] if turned else weights.shape[1]
    tile = 512
    if turned:
        weight_spec = pl.BlockSpec((tile, depth), lambda j: (j, 0))
    else:
        weight_spec = pl.BlockSpec((depth, tile), lambda j: (0, j))
    return pl.pallas_call(
        functools.partial(rows_product_body, turned),
        out_shape=pltpu.HBM((rows, width), BF16),
        grid=(width // tile,),
        in_specs=[
            pl.BlockSpec((rows, depth), lambda j: (side, 0), pipeline_mode=pl.Buffered(1)),
            weight_spec,
        ]
        + [pl.BlockSpec(memory_space=pl.ANY)] * len(waits),
        out_specs=pl.BlockSpec((rows, tile), lambda j: (0, j)),
        compiler_params=pltpu.CompilerParams(vmem_limit_bytes=24 * 2**20),
        cost_estimate=SHORT,
    )(*in_hbm(values, weights, *waits))


def small_call(body, out_shape, *operands):
    return pl.pallas_call(
        body,
        out_shape=tuple(pltpu.HBM(shape, dtype) for shape, dtype in out_shape),
        in_specs=whole_in_vmem(len(operands)),
        out_specs=tuple(whole_in_vmem(len(out_shape))),
        compiler_params=pltpu.CompilerParams(vmem_limit_bytes=24 * 2**20),
        cost_estimate=SHORT,
    )(*in_hbm(*operands))


def halves_body(near, next_row, upper, lower):
    half = upper.shape[0]
    upper[...] = near[:half, :]
    lower[...] = next_row[half:, :]


def join_body(upper, lower, out):
    half = upper.shape[0]
    out[:half, :] = upper[...]
    out[half:, :] = lower[...]


def pairs_body(even, got, own, *outs):
    rows = own.shape[0]
    for number, out in enumerate((own, *outs)):
        window = slice(number * rows, (number + 1) * rows)
        total = even[window, :].astype(F32) + got[window, :].astype(F32)
        out[...] = total.astype(out.dtype)


def row_mean(values):
    return jnp.mean(values, axis=1, keepdims=True)


def summed(terms):
    total = terms[0][...].astype(F32)
    for one in terms[1:]:
        total = total + one[...].astype(F32)
    return total


def norm_two_body(tokens, gain, cot, *refs):
    terms, (hidden_one, act_two, both) = refs[:-3], refs[-3:]
    total = tokens[...].astype(F32) + summed(terms)
    hidden_one[...] = total
    inverse = lax.rsqrt(row_mean(total * total) + EPS)
    act_two[...] = (total * inverse * gain[...]).astype(BF16)
    both[0] = act_two[...]
    both[1] = cot[...]


def norm_back(values, gain, beside, terms):
    act_back = summed(terms)
    rows = values[...].astype(F32)
    inverse = lax.rsqrt(row_mean(rows * rows) + EPS)
    normed = rows * inverse
    scaled = act_back * gain[...]
    total = beside[...].astype(F32) + inverse * (scaled - normed * row_mean(scaled * normed))
    return total, act_back * normed


def norm_two_back_body(values, gain, beside, *refs):
    terms, (back, back_low) = refs[:-2], refs[-2:]
    rows = back.shape[0]
    back[...], gain_terms = norm_back(values, gain, beside, terms)
    back_low[:rows, :] = back[...].astype(BF16)
    gain_row = jnp.sum(gain_terms, axis=0, keepdims=True)
    back_low[rows:, :] = jnp.broadcast_to(gain_row, (16, back.shape[1])).astype(BF16)


def norm_one_back_body(values, gain, beside, *refs):
    terms, back = refs[:-1], refs[-1]
    back[...], _ = norm_back(values, gain, beside, terms)


def layer_out_body(hidden_one, *refs):
    refs[-1][...] = (hidden_one[...] + summed(refs[:-1])).astype(BF16)


def swap(values, distance, axis):
    size = lax.axis_size(axis)
    return lax.ppermute(values, axis, [(i, i ^ distance) for i in range(size)])


def block_order(shards):
    return list(range(0, shards, 2)) + list(range(1, shards, 2))


class RowGather:
    def __init__(self, values):
        self.values = values
        self.moving = [swap(values, 2, "sp"), swap(values, 4, "sp")]

    def forward(self):
        self.near, self.next_row = self.moving
        rows, width = self.values.shape
        half = rows // 32 * 16
        shapes = (((half, width), BF16), ((rows - half, width), BF16))
        upper, lower = small_call(halves_body, shapes, self.near, self.next_row)
        self.sent = upper
        self.moving = [swap(upper, 4, "sp"), swap(lower, 2, "sp")]

    def cores(self):
        (far,) = small_call(join_body, ((self.values.shape, BF16),), *self.moving)
        self.evens = [self.values, self.near, self.next_row, far]
        self.sent = far
        self.moving = [swap(block, 1, "sp") for block in self.evens]

    def blocks(self):
        return self.evens + self.moving


class RowSum:
    def __init__(self, odd_terms):
        self.moving = [swap(odd_terms, 1, "sp")]

    def add_pairs(self, even_terms):
        shape = (even_terms.shape[0] // 4, even_terms.shape[1])
        self.own, *self.sent = small_call(
            pairs_body, ((shape, F32), *((shape, BF16),) * 3), even_terms, *self.moving
        )
        self.send()

    def send(self):
        self.moving = [swap(one, n, "sp") for one, n in zip(self.sent, (2, 4, 6), strict=True)]

    def terms(self):
        return self.own, *self.moving


def gather_rel(values):
    evens, distance = [values], 2
    while distance < lax.axis_size("sp"):
        evens = evens + [swap(block, distance, "sp") for block in evens]
        distance *= 2
    return evens + [swap(block, 1, "sp") for block in evens]


def scatter_rel(even_terms, odd_terms):
    shards = lax.axis_size("sp")
    got = swap(odd_terms, 1, "sp").astype(F32)
    sums = (even_terms.astype(F32) + got).reshape(shards // 2, -1, even_terms.shape[1])
    distance = shards // 2
    while distance > 1:
        kept = distance // 2
        sums = sums[:kept] + swap(sums[kept:].astype(BF16), distance, "sp").astype(F32)
        distance //= 2
    return sums[0]


def on_device(
    tokens,
    doc_lengths,
    w_query,
    w_key,
    w_value,
    w_out,
    gain_attn,
    gain_mlp,
    w_gate,
    w_up,
    w_down,
    cotangent,
):
    shards = lax.axis_size("sp")
    groups = lax.axis_size("dp")
    seq_rank = lax.axis_index("sp")
    tok_rows, width = tokens.shape
    group_rows = tok_rows * shards
    heads_total = w_query.shape[1] // HD
    kv_total = w_key.shape[1] // HD
    copies = max(1, shards // kv_total)
    q_cols = heads_total // shards * HD
    part_rows = w_query.shape[0]
    half = shards // 2

    planned = shards == 8 and groups == 4
    w_mixed = pack_weights(shards, copies, w_query, w_key, w_value, gain_attn, gain_mlp)
    columns = w_mixed.shape[2]
    w_local = lax.all_to_all(w_mixed, "sp", split_axis=0, concat_axis=0, tiled=True)
    gain_one = w_local[:, part_rows, :part_rows].reshape(1, width).astype(F32)
    gain_two = w_local[:, part_rows + 1, :part_rows].reshape(1, width).astype(F32)

    lengths = doc_lengths[0]
    count = lengths.shape[0]
    before = jnp.arange(count)[None, :] < jnp.arange(count)[:, None]
    starts = jnp.sum(jnp.where(before, lengths[None, :], 0), axis=1).astype(jnp.int32)
    places = jnp.arange(group_rows, dtype=jnp.int32)
    begins = jnp.max(jnp.where(starts[None, :] <= places[:, None], starts[None, :], 0), axis=1)
    angles = (places - begins).astype(F32)[:, None] * frequencies(HD)[None, :]
    cosine_half, sine_half = jnp.cos(angles), jnp.sin(angles)
    cosine = jnp.concatenate([cosine_half] * 4, axis=1)
    sine = jnp.concatenate([-sine_half, sine_half] * 2, axis=1)
    index = jnp.asarray(block_order(shards), jnp.int32) ^ seq_rank.astype(jnp.int32)

    def attend(blocks, weights):
        gain = weights[:, part_rows, :part_rows].reshape(1, width).astype(F32)
        return attention(index, starts, blocks, gain, weights, cosine, sine, w_out, q_cols)

    half_rows = group_rows // 2

    def terms(values, weights, side, turned=False, waits=()):
        return rows_product(side, values, weights, turned, waits)

    rows_f32, rows_bf16 = ((tok_rows, width), F32), ((tok_rows, width), BF16)

    def norm_two(summed):
        outs = (rows_f32, rows_bf16, ((2, tok_rows, width), BF16))
        return small_call(norm_two_body, outs, tokens, gain_two, cotangent, *summed)

    branch_shape = ((tok_rows + 16, width), BF16)

    def norm_two_back(summed, hidden_one):
        outs = (rows_f32, branch_shape)
        return small_call(norm_two_back_body, outs, hidden_one, gain_two, cotangent, *summed)

    def norm_one_back(summed, beside):
        (back,) = small_call(norm_one_back_body, (rows_f32,), tokens, gain_one, beside, *summed)
        return back

    def attend_back(blocks, waits=()):
        return attention_back(
            index, starts, blocks, w_out, mixed, log_sums, out_rel, cosine, sine, waits
        )

    def to_rows(grad_mixed):
        blocks = grad_mixed.reshape(shards, part_rows, columns)
        return lax.all_to_all(blocks, "sp", split_axis=0, concat_axis=0, tiled=True)

    def grow(kind, works, began, *waits):
        cot_rows, act_rows = [work[4] for work in works], [work[3] for work in works]
        mine = [work[(1, 2, 0)[kind]] for work in works]
        if kind == 2:
            return weight_grad(mine, cot_rows, 1024, 512, waits, began)
        return weight_grad(act_rows, mine, 512, 1024, waits, began)

    dp_rank = lax.axis_index("dp").astype(jnp.int32)

    if planned:
        which = dp_rank ^ jnp.arange(1, groups, dtype=jnp.int32)
        token_gather = RowGather(tokens)
        *token_gather.moving, cosine, sine = together(*token_gather.moving, cosine, sine)
        token_gather.forward()
        token_gather.cores()
        *token_blocks, w_local = together(*token_gather.evens[1:], *token_gather.moving, w_local)
        token_blocks = [tokens] + token_blocks

        cot_gather = RowGather(after(cotangent, w_local))
        act_one, mixed, out_rel, log_sums, out_even, out_odd = attend(token_blocks, w_local)
        out_even, out_odd, *cot_gather.moving = together(
            out_even, out_odd, *cot_gather.moving
        )

        out_sum = RowSum(out_odd)
        out_even, *out_sum.moving = together(out_even, *out_sum.moving)
        out_sum.add_pairs(out_even)
        cot_gather.moving = [after(one, *out_sum.sent) for one in cot_gather.moving]
        cot_gather.forward()
        w_projections = after(w_local, *out_sum.sent)[:, :part_rows, :].reshape(width, columns)
        w_projections, *moving = together(w_projections, *out_sum.moving, *cot_gather.moving)
        out_sum.moving, cot_gather.moving = moving[:3], moving[3:]
        hidden_one, act_two, both = norm_two(out_sum.terms())

        act_gather = RowGather(act_two)
        both = lax.all_gather(both, ("dp", "sp"), axis=0).reshape(
            groups, shards, 2, tok_rows, width
        )
        act_gather.moving = together(*act_gather.moving)
        act_gather.forward()
        cot_gather.moving = [after(one, act_gather.sent) for one in cot_gather.moving]
        cot_gather.cores()
        act_gather.cores()
        *act_gather.moving, one, two, three, four = together(
            *act_gather.moving, *cot_gather.moving
        )
        cot_gather.moving = [one, two, three, four]

        own = ffn(act_gather.blocks(), cot_gather.blocks(), w_gate, w_up, w_down)
        back_sum = RowSum(act_back(1, own[1], own[2], w_gate, w_up, BF16))
        even_back = act_back(0, own[1], own[2], w_gate, w_up, BF16, (own[0],))
        even_back, *back_sum.moving = together(even_back, *back_sum.moving)

        back_sum.add_pairs(even_back)
        mlp_odd = terms(own[0], w_down, 1, False, back_sum.sent)
        grad_gate = grow(0, [own], None, mlp_odd)
        grad_up = grow(1, [own], None, grad_gate)
        grad_up, mlp_odd, *back_sum.moving = together(grad_up, mlp_odd, *back_sum.moving)
        hidden_one_back, branch = norm_two_back(back_sum.terms(), hidden_one)

        branch_gather = RowGather(branch)
        mlp_sum = RowSum(after(mlp_odd, branch))
        mlp_even = terms(own[0], w_down, 0, False, (branch,))
        grad_down = grow(2, [own], None, mlp_even)
        grad_down, mlp_even, *moving = together(
            grad_down, mlp_even, *branch_gather.moving, *mlp_sum.moving
        )
        branch_gather.moving, mlp_sum.moving = moving[:2], moving[2:]

        branch_gather.forward()
        branch_gather.cores()
        mlp_even, *branch_gather.moving = together(mlp_even, *branch_gather.moving)
        mixed_back, grad_out_terms = attend_back(branch_gather.blocks())
        grad_mixed = weight_grad([act_one], [mixed_back], 512, columns, (), None, BF16)
        mixed_sum, grad_out = lax.psum((grad_mixed, grad_out_terms), "dp")
        one_odd = terms(mixed_back, w_projections, 1, True, (grad_mixed,))
        one_sum = RowSum(one_odd)
        one_even = terms(mixed_back, w_projections, 0, True, (one_odd,))
        mlp_sum.add_pairs(after(mlp_even, one_even))
        others = ffn_others(which, both, w_gate, w_up, w_down, mlp_sum.sent)
        *others, one_even, got, one, two, three = together(
            *others, one_even, *one_sum.moving, *mlp_sum.moving
        )
        one_sum.moving, mlp_sum.moving = [got], [one, two, three]

        one_sum.add_pairs(one_even)
        grad_gate, grad_up = grad_pair(
            which,
            both,
            others[1],
            others[2],
            grad_gate,
            grad_up,
            256,
            one_sum.sent,
        )
        (layer_out,) = small_call(
            layer_out_body, (rows_bf16,), after(hidden_one, grad_gate), *mlp_sum.terms()
        )
        layer_out, *one_sum.moving = together(layer_out, *one_sum.moving)

        grad_tokens = norm_one_back(one_sum.terms(), hidden_one_back)
        mixed_sum, grad_out, grad_tokens = together(mixed_sum, grad_out, grad_tokens)
        mixed_rows = to_rows(mixed_sum)
        grad_down = grad_others(
            which, both, 1, others[0], grad_down, 1024, 512, (mixed_sum,)
        )
        grad_down, mixed_rows, grad_out = together(grad_down, mixed_rows, grad_out)
        grad_out = grad_out.astype(F32)
    else:
        w_projections = w_local[:, :part_rows, :].reshape(width, columns)
        act_one, mixed, out_rel, log_sums, out_even, out_odd = attend(gather_rel(tokens), w_local)
        hidden_one, act_two, _ = norm_two((scatter_rel(out_even, out_odd),))
        act_blocks, cot_blocks, half = gather_rel(act_two), gather_rel(cotangent), shards // 2
        own = [
            jnp.concatenate(parts, axis=0)
            for parts in zip(
                ffn(act_blocks[:half], cot_blocks[:half], w_gate, w_up, w_down),
                ffn(act_blocks[half:], cot_blocks[half:], w_gate, w_up, w_down),
                strict=True,
            )
        ]
        act_two_back = scatter_rel(
            act_back(0, own[1], own[2], w_gate, w_up, BF16),
            act_back(1, own[1], own[2], w_gate, w_up, BF16),
        )
        hidden_one_back, branch = norm_two_back((act_two_back,), hidden_one)
        mixed_back, grad_out_terms = attend_back(gather_rel(branch))
        act_one_back = scatter_rel(
            terms(mixed_back, w_projections, 0, True), terms(mixed_back, w_projections, 1, True)
        )
        mixed_rows = to_rows(lax.psum(contract(act_one, mixed_back, 0, 0).astype(BF16), "dp"))
        mlp_out = scatter_rel(terms(own[0], w_down, 0), terms(own[0], w_down, 1))
        layer_out = (hidden_one + mlp_out).astype(BF16)
        grad_tokens = norm_one_back((act_one_back,), hidden_one_back)
        grad_out, grad_gate, grad_up, grad_down = (
            lax.psum(grad.astype(BF16), "dp").astype(F32)
            for grad in (grad_out_terms, *(grow(kind, [own], None) for kind in range(3)))
        )
    grad_gain_mlp = lax.dynamic_slice_in_dim(grad_out[q_cols], seq_rank * part_rows, part_rows, 0)
    grad_out = grad_out[:q_cols]
    if copies == 1:
        grad_query, grad_key, grad_value, products = unpack_grads(
            mixed_rows[None], (w_query, w_key, w_value), q_cols
        )
        products = products.reshape(part_rows)
    else:
        parts = jnp.transpose(mixed_rows.astype(F32), (1, 0, 2))
        grad_query = parts[:, :, :q_cols].reshape(part_rows, shards * q_cols)
        grad_key, grad_value = (
            parts[:, :, first : first + HD]
            .reshape(part_rows, kv_total, copies, HD)
            .sum(axis=2)
            .reshape(part_rows, -1)
            for first in (q_cols, q_cols + HD)
        )
        products = sum(
            jnp.sum(weight.astype(F32) * grad, axis=1)
            for weight, grad in (
                (w_query, grad_query),
                (w_key, grad_key),
                (w_value, grad_value),
            )
        )
    grad_gain_attn = products / gain_attn.astype(F32)
    return (
        layer_out,
        grad_tokens,
        grad_query,
        grad_key,
        grad_value,
        grad_out,
        grad_gain_attn,
        grad_gain_mlp,
        grad_gate,
        grad_up,
        grad_down,
    )


def solution(mesh):
    placed = (
        P(("dp", "sp"), None),
        P("dp", None),
        P("sp", None),
        P("sp", None),
        P("sp", None),
        P("sp", None),
        P("sp"),
        P("sp"),
        P(None, "sp"),
        P(None, "sp"),
        P("sp", None),
        P(("dp", "sp"), None),
    )
    return jax.shard_map(
        on_device,
        mesh=mesh,
        in_specs=placed,
        out_specs=(
            P(("dp", "sp"), None),
            P(("dp", "sp"), None),
            P("sp", None),
            P("sp", None),
            P("sp", None),
            P("sp", None),
            P("sp"),
            P("sp"),
            P(None, "sp"),
            P(None, "sp"),
            P("sp", None),
        ),
        check_vma=False,
    )
```

```python
import functools

import jax
import jax.numpy as jnp
from jax import lax
from jax.experimental import pallas as pl
from jax.experimental.pallas import tpu as pltpu
from jax.sharding import PartitionSpec as P

HD = 64
Q_ROWS = 256
F32 = jnp.float32
BF16 = jnp.bfloat16


EPS = 1e-05
THETA = 500000.0
FACTOR = 32.0
LOW_FACTOR = 1.0
HIGH_FACTOR = 4.0
BASE_CONTEXT = 8192.0
MASKED = -1e30


def frequencies(head_size):
    half_index = jnp.arange(head_size // 2).astype(jnp.float32)
    inverse = THETA ** (-2.0 * half_index / head_size)
    wavelength = 2.0 * jnp.pi / inverse
    smooth = (BASE_CONTEXT / wavelength - LOW_FACTOR) / (HIGH_FACTOR - LOW_FACTOR)
    middle = (1.0 - smooth) * inverse / FACTOR + smooth * inverse
    slow_band = jnp.where(wavelength > BASE_CONTEXT / LOW_FACTOR, inverse / FACTOR, middle)
    return jnp.where(wavelength < BASE_CONTEXT / HIGH_FACTOR, inverse, slow_band)


def contract(left, right, left_dim, right_dim):
    return lax.dot_general(
        left, right, (((left_dim,), (right_dim,)), ((), ())), preferred_element_type=jnp.float32
    )


SHORT = pl.CostEstimate(flops=0, bytes_accessed=0, transcendentals=0)


def product(left, right, left_dim, right_dim):
    return lax.dot_general(
        left, right, (((left_dim,), (right_dim,)), ((), ())), preferred_element_type=F32
    )


def whole_in_vmem(count):
    return [pl.BlockSpec(memory_space=pltpu.VMEM)] * count


def in_hbm(*values):
    return [pltpu.with_memory_space_constraint(one, pltpu.HBM) for one in values]


def after(values, *earlier):
    def body(*refs):
        pass

    return pl.pallas_call(
        body,
        out_shape=pltpu.HBM(values.shape, values.dtype),
        in_specs=[pl.BlockSpec(memory_space=pl.ANY)] * (1 + len(earlier)),
        out_specs=pl.BlockSpec(memory_space=pl.ANY),
        input_output_aliases={0: 0},
        cost_estimate=pl.CostEstimate(flops=0, bytes_accessed=0, transcendentals=0),
    )(*in_hbm(values, *earlier))


def together(*values):
    def body(*refs):
        pass

    anywhere = pl.BlockSpec(memory_space=pl.ANY)
    call = pl.pallas_call(
        body,
        out_shape=tuple(pltpu.HBM(one.shape, one.dtype) for one in values),
        in_specs=[anywhere] * len(values),
        out_specs=(anywhere,) * len(values),
        input_output_aliases={n: n for n in range(len(values))},
        cost_estimate=pl.CostEstimate(flops=0, bytes_accessed=0, transcendentals=0),
    )
    return list(call(*in_hbm(*values)))


def turn_signed(values, signed_sine):
    lane = lax.broadcasted_iota(jnp.int32, values.shape, 1) % HD
    turned = jnp.where(
        lane < HD // 2, pltpu.roll(values, 128 - HD // 2, 1), pltpu.roll(values, HD // 2, 1)
    )
    return turned * signed_sine


def rope_tables(cosine, sine, last):
    if not last:
        return cosine, sine
    lane = lax.broadcasted_iota(jnp.int32, cosine.shape, 1)
    return jnp.where(lane < HD, cosine, 1.0), jnp.where(lane < HD, sine, 0.0)


def score_mask(starts_ref, first_row, rows, keys):
    place = first_row + lax.broadcasted_iota(jnp.int32, (rows, 1), 0)
    begin = jnp.zeros((rows, 1), jnp.int32)
    for index in range(starts_ref.shape[0]):
        start = starts_ref[index]
        begin = jnp.maximum(begin, jnp.where(place >= start, start, 0))
    key_place = lax.broadcasted_iota(jnp.int32, (rows, keys), 1)
    return (key_place >= begin) & (key_place <= place)


def attention_body(shards, q_cols, index_ref, starts_ref, *refs):
    tokens = refs[:shards]
    gain, weights, cosine, sine, w_out = refs[shards : shards + 5]
    act, mixed, out_rel, log_sums, even_terms, odd_terms, out_rows = refs[shards + 5 :]
    rows = tokens[0].shape[0]
    total = rows * shards
    part = act.shape[1] // shards
    columns = mixed.shape[1]
    groups = columns // 128
    half = shards // 2
    for side in range(2):
        for block in range(side * half, side * half + half):
            values = tokens[block][...].astype(F32)
            inverse = lax.rsqrt(jnp.mean(values * values, axis=1, keepdims=True) + EPS)
            act[block * rows : (block + 1) * rows, :] = (values * inverse * gain[...]).astype(BF16)
        first = side * half * rows
        sums = jnp.zeros((half * rows, columns), F32)
        for source in range(shards):
            sums = sums + product(
                act[first : first + half * rows, source * part : (source + 1) * part],
                weights[source, :part, :],
                1,
                0,
            )
        for block in range(half):
            place = pl.multiple_of(index_ref[side * half + block] * rows, rows)
            cosine_rows = cosine[pl.ds(place, rows), :]
            sine_rows = sine[pl.ds(place, rows), :]
            for group in range(groups):
                piece = sums[block * rows : (block + 1) * rows, group * 128 : (group + 1) * 128]
                cosine_part, sine_part = rope_tables(cosine_rows, sine_rows, group == groups - 1)
                mixed[pl.ds(place, rows), group * 128 : (group + 1) * 128] = (
                    piece * cosine_part + turn_signed(piece, sine_part)
                ).astype(BF16)
    scale = HD ** (-0.5)
    for first in range(0, total, Q_ROWS):
        keys = first + Q_ROWS
        allowed = score_mask(starts_ref, first, Q_ROWS, keys)
        key_rows = mixed[:keys, q_cols : q_cols + HD]
        value_rows = mixed[:keys, q_cols + HD : q_cols + 2 * HD]
        for head in range(q_cols // HD):
            query = mixed[first:keys, head * HD : (head + 1) * HD] * jnp.asarray(scale, BF16)
            scores = jnp.where(allowed, product(query, key_rows, 1, 1), MASKED)
            largest = jnp.max(scores, axis=1, keepdims=True)
            weights_row = jnp.exp(scores - largest)
            total_weight = jnp.sum(weights_row, axis=1, keepdims=True)
            attended = product(weights_row.astype(BF16), value_rows, 1, 0) / total_weight
            out_rows[first:keys, head * HD : (head + 1) * HD] = attended.astype(BF16)
            log_sums[first:keys, head : head + 1] = largest + jnp.log(total_weight)
    for block in range(shards):
        place = pl.multiple_of(index_ref[block] * rows, rows)
        out_rel[block * rows : (block + 1) * rows, :] = out_rows[pl.ds(place, rows), :]
    width = w_out.shape[1]
    for side, terms in enumerate((even_terms, odd_terms)):
        heads = out_rel[side * half * rows : (side + 1) * half * rows, :]
        for first in range(0, width, 512):
            cut = slice(first, first + 512)
            terms[:, cut] = product(heads, w_out[:, cut], 1, 0).astype(BF16)


def attention(index, starts, tokens, gain, weights, cosine, sine, w_out, q_cols):
    shards = len(tokens)
    rows, width = tokens[0].shape
    total = rows * shards
    columns = weights.shape[2]
    smem = pl.BlockSpec(memory_space=pltpu.SMEM)
    return pl.pallas_call(
        functools.partial(attention_body, shards, q_cols),
        out_shape=(
            pltpu.HBM((total, width), BF16),
            pltpu.HBM((total, columns), BF16),
            pltpu.HBM((total, q_cols), BF16),
            pltpu.HBM((total, q_cols // HD), F32),
            pltpu.HBM((total // 2, width), BF16),
            pltpu.HBM((total // 2, width), BF16),
        ),
        in_specs=[smem, smem] + whole_in_vmem(shards + 5),
        out_specs=tuple(whole_in_vmem(6)),
        scratch_shapes=[pltpu.VMEM((total, q_cols), BF16)],
        compiler_params=pltpu.CompilerParams(vmem_limit_bytes=58 * 2**20),
        cost_estimate=SHORT,
    )(index, starts, *in_hbm(*tokens, gain, weights, cosine, sine, w_out))


def attention_back_body(shards, rows, q_cols, waits, index_ref, starts_ref, *refs):
    branch = refs[:shards]
    w_out, mixed, log_sums, out_rel, cosine, sine = refs[shards : shards + 6]
    mixed_back, grad_out, *scratch = refs[shards + 6 + waits :]
    branch_rows, heads_back, query_grads, key_grads, value_grads = scratch
    total = rows * shards
    columns = mixed.shape[1]
    half = total // 2
    gain_terms = jnp.zeros(branch[0].shape[1:], F32)[None]
    for block in range(shards):
        branch_rows[block * rows : (block + 1) * rows, :] = branch[block][:rows, :]
        gain_terms = gain_terms + branch[block][rows:, :].astype(F32)[:1, :]
    grad_out[q_cols:, :] = jnp.broadcast_to(gain_terms, (16, gain_terms.shape[1])).astype(BF16)
    for side in range(2):
        back = product(branch_rows[side * half : (side + 1) * half, :], w_out[...], 1, 1).astype(
            BF16
        )
        for block in range(shards // 2):
            place = pl.multiple_of(index_ref[side * (shards // 2) + block] * rows, rows)
            heads_back[pl.ds(place, rows), :] = back[block * rows : (block + 1) * rows, :]
    grad_out[:q_cols, :] = product(out_rel[...], branch_rows[...], 0, 0).astype(BF16)
    key_grads[...] = jnp.zeros_like(key_grads)
    value_grads[...] = jnp.zeros_like(value_grads)
    scale = HD ** (-0.5)
    for first in range(0, total, Q_ROWS):
        keys = first + Q_ROWS
        allowed = score_mask(starts_ref, first, Q_ROWS, keys)
        key_rows = mixed[:keys, q_cols : q_cols + HD]
        value_rows = mixed[:keys, q_cols + HD : q_cols + 2 * HD]
        for head in range(q_cols // HD):
            cut = slice(head * HD, (head + 1) * HD)
            query = mixed[first:keys, cut] * jnp.asarray(scale, BF16)
            back = heads_back[first:keys, cut]
            scores = jnp.where(allowed, product(query, key_rows, 1, 1), MASKED)
            probs = jnp.exp(scores - log_sums[first:keys, head : head + 1])
            probs_back = product(back, value_rows, 1, 1)
            delta = jnp.sum(probs * probs_back, axis=1, keepdims=True)
            scores_back = (probs * (probs_back - delta)).astype(BF16)
            query_grads[first:keys, cut] = product(scores_back, key_rows, 1, 0) * scale
            key_grads[:keys, :] += product(scores_back, query, 0, 0)
            value_grads[:keys, :] += product(probs.astype(BF16), back, 0, 0)
    for block in range(shards):
        place = pl.multiple_of(index_ref[block] * rows, rows)
        window = pl.ds(place, rows)
        cosine_rows, sine_rows = cosine[window, :], sine[window, :]
        for group in range(columns // 128):
            last = group == columns // 128 - 1
            if last:
                piece = jnp.concatenate([key_grads[window, :], value_grads[window, :]], axis=1)
            else:
                piece = query_grads[window, group * 128 : (group + 1) * 128]
            cosine_part, sine_part = rope_tables(cosine_rows, sine_rows, last)
            mixed_back[block * rows : (block + 1) * rows, group * 128 : (group + 1) * 128] = (
                piece * cosine_part - turn_signed(piece, sine_part)
            ).astype(BF16)


def attention_back(
    index, starts, branch, w_out, mixed, log_sums, out_rel, cosine, sine, waits=()
):
    shards = len(branch)
    width = branch[0].shape[1]
    total, columns = mixed.shape
    rows = total // shards
    q_cols = out_rel.shape[1]
    smem = pl.BlockSpec(memory_space=pltpu.SMEM)
    return pl.pallas_call(
        functools.partial(attention_back_body, shards, rows, q_cols, len(waits)),
        out_shape=(
            pltpu.HBM((total, columns), BF16),
            pltpu.HBM((q_cols + 16, width), BF16),
        ),
        in_specs=[smem, smem]
        + whole_in_vmem(shards + 6)
        + [pl.BlockSpec(memory_space=pl.ANY)] * len(waits),
        out_specs=tuple(whole_in_vmem(2)),
        scratch_shapes=[
            pltpu.VMEM((total, width), BF16),
            pltpu.VMEM((total, q_cols), BF16),
            pltpu.VMEM((total, q_cols), F32),
            pltpu.VMEM((total, HD), F32),
            pltpu.VMEM((total, HD), F32),
        ],
        compiler_params=pltpu.CompilerParams(vmem_limit_bytes=48 * 2**20),
        cost_estimate=SHORT,
    )(index, starts, *in_hbm(*branch, w_out, mixed, log_sums, out_rel, cosine, sine, *waits))


def ffn_body(pieces, *refs):
    act, cot = refs[:pieces], refs[pieces : 2 * pieces]
    w_gate, w_up, w_down = refs[2 * pieces : 2 * pieces + 3]
    hidden, gate_back, up_back, act_out, cot_out, act_rows, cot_rows = refs[2 * pieces + 3 :]
    step = pl.program_id(0)

    @pl.when(step == 0)
    def _():
        for parts, rows in ((act, act_rows), (cot, cot_rows)):
            first = 0
            for part in parts:
                rows[first : first + part.shape[0], :] = part[...]
                first += part.shape[0]

    strip = act_out.shape[1]
    window = pl.ds(pl.multiple_of(step * strip, strip), strip)
    act_out[...] = act_rows[:, window]
    cot_out[...] = cot_rows[:, window]
    gate_value = product(act_rows[...], w_gate[...], 1, 0)
    up_value = product(act_rows[...], w_up[...], 1, 0)
    hidden_back = product(cot_rows[...], w_down[...], 1, 1)
    sigmoid_gate = 1.0 / (1.0 + jnp.exp(-gate_value))
    silu_gate = gate_value * sigmoid_gate
    hidden[...] = (silu_gate * up_value).astype(BF16)
    gate_back[...] = (
        hidden_back * up_value * sigmoid_gate * (1.0 + gate_value * (1.0 - sigmoid_gate))
    ).astype(BF16)
    up_back[...] = (hidden_back * silu_gate).astype(BF16)


def ffn(act, cot, w_gate, w_up, w_down):
    pieces = len(act)
    rows, width = act[0].shape
    total = rows * pieces
    units = w_gate.shape[1]
    tile = min(256, units)
    steps = units // tile
    strip = width // steps
    block = pl.BlockSpec((rows, width), lambda j: (0, 0), pipeline_mode=pl.Buffered(1))
    columns = pl.BlockSpec((width, tile), lambda j: (0, j))
    out = pl.BlockSpec((total, tile), lambda j: (0, j))
    wide = pl.BlockSpec((total, strip), lambda j: (0, j))
    return pl.pallas_call(
        functools.partial(ffn_body, pieces),
        out_shape=(pltpu.HBM((total, units), BF16),) * 3 + (pltpu.HBM((total, width), BF16),) * 2,
        grid=(steps,),
        in_specs=[block] * (2 * pieces)
        + [columns, columns, pl.BlockSpec((tile, width), lambda j: (j, 0))],
        out_specs=(out, out, out, wide, wide),
        scratch_shapes=[pltpu.VMEM((total, width), BF16)] * 2,
        compiler_params=pltpu.CompilerParams(vmem_limit_bytes=48 * 2**20),
        cost_estimate=SHORT,
    )(*in_hbm(*act, *cot, w_gate, w_up, w_down))


def ffn_others_body(waits, which, act, cot, w_gate, w_up, w_down, *refs):
    hidden, gate_back, up_back = refs[waits:]
    act_rows = act[...].reshape(hidden.shape[0], w_gate.shape[0])
    cot_rows = cot[...].reshape(act_rows.shape)
    gate_value = product(act_rows, w_gate[...], 1, 0)
    up_value = product(act_rows, w_up[...], 1, 0)
    hidden_back = product(cot_rows, w_down[...], 1, 1)
    sigmoid_gate = 1.0 / (1.0 + jnp.exp(-gate_value))
    silu_gate = gate_value * sigmoid_gate
    hidden[...] = (silu_gate * up_value).astype(BF16)
    gate_back[...] = (
        hidden_back * up_value * sigmoid_gate * (1.0 + gate_value * (1.0 - sigmoid_gate))
    ).astype(BF16)
    up_back[...] = (hidden_back * silu_gate).astype(BF16)


def ffn_others(which, both, w_gate, w_up, w_down, waits=()):
    count = which.shape[0]
    _, shards, _, rows, width = both.shape
    units, total = w_gate.shape[1], shards * rows
    tile = min(512, units)

    def rows_spec(kind):
        return pl.BlockSpec(
            (None, shards, None, rows, width), lambda i, j, w: (w[i], 0, kind, 0, 0)
        )

    columns = pl.BlockSpec((width, tile), lambda i, j, w: (0, j))
    out = pl.BlockSpec((total, tile), lambda i, j, w: (i, j))
    return pl.pallas_call(
        functools.partial(ffn_others_body, len(waits)),
        out_shape=(pltpu.HBM((total * count, units), BF16),) * 3,
        grid_spec=pltpu.PrefetchScalarGridSpec(
            num_scalar_prefetch=1,
            grid=(count, units // tile),
            in_specs=[
                rows_spec(0),
                rows_spec(1),
                columns,
                columns,
                pl.BlockSpec((tile, width), lambda i, j, w: (j, 0)),
            ]
            + [pl.BlockSpec(memory_space=pl.ANY)] * len(waits),
            out_specs=(out, out, out),
        ),
        compiler_params=pltpu.CompilerParams(vmem_limit_bytes=58 * 2**20),
        cost_estimate=SHORT,
    )(which, *in_hbm(both, both, w_gate, w_up, w_down, *waits))


def act_back_body(gate_back, up_back, w_gate, w_up, *refs):
    out = refs[-1]
    out[...] = (
        product(gate_back[...], w_gate[...], 1, 1) + product(up_back[...], w_up[...], 1, 1)
    ).astype(out.dtype)


def act_back(side, gate_back, up_back, w_gate, w_up, dtype, waits=()):
    total, units = gate_back.shape[0] // 2, gate_back.shape[1]
    width = w_gate.shape[0]
    tile = 512
    rows = pl.BlockSpec((total, units), lambda j: (side, 0), pipeline_mode=pl.Buffered(1))
    weights = pl.BlockSpec((tile, units), lambda j: (j, 0))
    return pl.pallas_call(
        act_back_body,
        out_shape=pltpu.HBM((total, width), dtype),
        grid=(width // tile,),
        in_specs=[rows, rows, weights, weights]
        + [pl.BlockSpec(memory_space=pl.ANY)] * len(waits),
        out_specs=pl.BlockSpec((total, tile), lambda j: (0, j)),
        compiler_params=pltpu.CompilerParams(vmem_limit_bytes=32 * 2**20),
        cost_estimate=SHORT,
    )(*in_hbm(gate_back, up_back, w_gate, w_up, *waits))


def weight_grad_body(pieces, began, *refs):
    left, right, out = refs[:pieces], refs[pieces : 2 * pieces], refs[-1]
    total = product(left[0][...], right[0][...], 0, 0)
    if began:
        total = total + refs[2 * pieces][...]
    for piece in range(1, pieces):
        total = total + product(left[piece][...], right[piece][...], 0, 0)
    out[...] = total.astype(out.dtype)


def weight_grad(left, right, row_tile, column_tile, waits=(), began=None, dtype=F32):
    pieces = len(left)
    rows, height = left[0].shape
    width = right[0].shape[1]
    row_tile, column_tile = min(row_tile, height), min(column_tile, width)
    tile_spec = pl.BlockSpec((row_tile, column_tile), lambda j, i: (i, j))
    start = () if began is None else (began,)
    return pl.pallas_call(
        functools.partial(weight_grad_body, pieces, began is not None),
        out_shape=pltpu.HBM((height, width), dtype),
        grid=(width // column_tile, height // row_tile),
        in_specs=[pl.BlockSpec((rows, row_tile), lambda j, i: (0, i))] * pieces
        + [pl.BlockSpec((rows, column_tile), lambda j, i: (0, j))] * pieces
        + [tile_spec] * len(start)
        + [pl.BlockSpec(memory_space=pl.ANY)] * len(waits),
        out_specs=tile_spec,
        compiler_params=pltpu.CompilerParams(vmem_limit_bytes=48 * 2**20),
        cost_estimate=SHORT,
    )(*in_hbm(*left, *right, *start, *waits))


def pack_weights_body(shards, copies, w_query, w_key, w_value, gains, out):
    part, q_cols = w_query.shape[0], w_query.shape[1] // shards
    out[:, part:, :] = jnp.broadcast_to(gains[...][None], (shards,) + gains.shape)
    for shard in range(shards):
        head = shard // copies * HD
        out[shard, :part, :q_cols] = w_query[:, shard * q_cols : (shard + 1) * q_cols]
        out[shard, :part, q_cols:] = jnp.concatenate(
            [w_key[:, head : head + HD], w_value[:, head : head + HD]], axis=1
        )


def pack_weights(shards, copies, w_query, w_key, w_value, gain_attn, gain_mlp):
    part = w_query.shape[0]
    columns = w_query.shape[1] // shards + 2 * HD
    gains = jnp.zeros((16, columns), BF16)
    gains = gains.at[0, :part].set(gain_attn).at[1, :part].set(gain_mlp)
    return pl.pallas_call(
        functools.partial(pack_weights_body, shards, copies),
        out_shape=pltpu.HBM((shards, part + 16, columns), BF16),
        in_specs=whole_in_vmem(4),
        out_specs=whole_in_vmem(1)[0],
        compiler_params=pltpu.CompilerParams(vmem_limit_bytes=16 * 2**20),
    )(*in_hbm(w_query, w_key, w_value, gains))


def unpack_grads_body(q_cols, pieces, sums, *refs):
    weights = refs[:3]
    query, key, value, products, out = refs[-5:]
    out[...] = sums[: out.shape[0], :].astype(F32)
    groups, shards, strip, _ = pieces.shape
    for number in range(groups):
        rows = slice(number * strip, (number + 1) * strip)
        for shard in range(shards):
            query[rows, shard * q_cols : (shard + 1) * q_cols] = pieces[
                number, shard, :, :q_cols
            ].astype(F32)
        for shard in range(0, shards, 2):
            for place, out in ((q_cols, key), (q_cols + HD, value)):
                out[rows, shard * HD : (shard + 2) * HD] = jnp.concatenate(
                    [pieces[number, shard + n, :, place : place + HD] for n in range(2)], axis=1
                ).astype(F32)
    total = jnp.zeros(products.shape, F32)
    for weight, grad in zip(weights, (query, key, value), strict=True):
        terms = weight[...].astype(F32) * grad[...]
        total = total + jnp.sum(terms, axis=1, keepdims=True)
    products[...] = total


def unpack_grads(pieces, sums, weights, q_cols, waits=()):
    groups, shards, strip, _ = pieces.shape
    rows = strip * groups
    return pl.pallas_call(
        functools.partial(unpack_grads_body, q_cols),
        out_shape=(
            jax.ShapeDtypeStruct((rows, shards * q_cols), F32),
            jax.ShapeDtypeStruct((rows, shards * HD), F32),
            jax.ShapeDtypeStruct((rows, shards * HD), F32),
            jax.ShapeDtypeStruct((rows, 1), F32),
            jax.ShapeDtypeStruct((q_cols, sums.shape[1]), F32),
        ),
        in_specs=whole_in_vmem(5) + [pl.BlockSpec(memory_space=pl.ANY)] * len(waits),
        out_specs=tuple(whole_in_vmem(5)),
        compiler_params=pltpu.CompilerParams(vmem_limit_bytes=24 * 2**20),
    )(pieces, *in_hbm(sums, *weights, *waits))


def grad_others_body(count, kind, which, *refs):
    rows, units, began = refs[:count], refs[count : 2 * count], refs[2 * count]
    out = refs[-1]
    total = began[...]
    for one, two in zip(rows, units, strict=True):
        one = one[...].reshape(two.shape[0], one.shape[-1])
        if kind:
            total = total + product(two[...], one, 0, 0)
        else:
            total = total + product(one, two[...], 0, 0)
    out[...] = total


def grad_others(which, both, kind, units_all, began, row_tile, column_tile, waits=()):
    count = which.shape[0]
    shards, rows = both.shape[1], both.shape[3]
    total = shards * rows
    height, width = began.shape
    wide, narrow = (column_tile, row_tile) if kind else (row_tile, column_tile)

    def rows_spec(number):
        def place(j, i, w):
            return (w[number], 0, kind, 0, j if kind else i)

        return pl.BlockSpec((None, shards, None, rows, wide), place)

    def units_spec(number):
        return pl.BlockSpec((total, narrow), lambda j, i, w: (number, i if kind else j))

    tile_spec = pl.BlockSpec((row_tile, column_tile), lambda j, i, w: (i, j))
    return pl.pallas_call(
        functools.partial(grad_others_body, count, kind),
        out_shape=pltpu.HBM((height, width), F32),
        grid_spec=pltpu.PrefetchScalarGridSpec(
            num_scalar_prefetch=1,
            grid=(width // column_tile, height // row_tile),
            in_specs=[rows_spec(n) for n in range(count)]
            + [units_spec(n) for n in range(count)]
            + [tile_spec]
            + [pl.BlockSpec(memory_space=pl.ANY)] * len(waits),
            out_specs=tile_spec,
        ),
        compiler_params=pltpu.CompilerParams(vmem_limit_bytes=48 * 2**20),
        cost_estimate=SHORT,
    )(which, *in_hbm(*[both] * count, *[units_all] * count, began, *waits))


def grad_pair_body(count, which, *refs):
    rows = [one[...] for one in refs[:count]]
    outs = refs[-2:]
    for kind, out in enumerate(outs):
        units = refs[count * (1 + kind) : count * (2 + kind)]
        total = refs[3 * count + kind][...]
        for one, two in zip(rows, units, strict=True):
            total = total + product(one.reshape(two.shape[0], one.shape[-1]), two[...], 0, 0)
        out[...] = total


def grad_pair(which, both, gates, ups, began_gate, began_up, row_tile, waits=()):
    count = which.shape[0]
    shards, rows = both.shape[1], both.shape[3]
    total = shards * rows
    height, width = began_gate.shape

    def rows_spec(number):
        return pl.BlockSpec(
            (None, shards, None, rows, row_tile), lambda i, w: (w[number], 0, 0, 0, i)
        )

    def units_spec(number):
        return pl.BlockSpec(
            (total, width), lambda i, w: (number, 0), pipeline_mode=pl.Buffered(1)
        )

    tile_spec = pl.BlockSpec((row_tile, width), lambda i, w: (i, 0))
    units_specs = [units_spec(n) for n in range(count)]
    return pl.pallas_call(
        functools.partial(grad_pair_body, count),
        out_shape=(pltpu.HBM((height, width), F32),) * 2,
        grid_spec=pltpu.PrefetchScalarGridSpec(
            num_scalar_prefetch=1,
            grid=(height // row_tile,),
            in_specs=[rows_spec(n) for n in range(count)]
            + units_specs
            + units_specs
            + [tile_spec] * 2
            + [pl.BlockSpec(memory_space=pl.ANY)] * len(waits),
            out_specs=(tile_spec, tile_spec),
        ),
        compiler_params=pltpu.CompilerParams(vmem_limit_bytes=56 * 2**20),
        cost_estimate=SHORT,
    )(
        which,
        *in_hbm(
            *[both] * count, *[gates] * count, *[ups] * count, began_gate, began_up, *waits
        ),
    )


def rows_product_body(turned, values, weights, *refs):
    out = refs[-1]
    out[...] = product(values[...], weights[...], 1, 1 if turned else 0).astype(out.dtype)


def rows_product(side, values, weights, turned=False, waits=()):
    rows, depth = values.shape[0] // 2, values.shape[1]
    width = weights.shape[0] if turned else weights.shape[1]
    tile = 512
    if turned:
        weight_spec = pl.BlockSpec((tile, depth), lambda j: (j, 0))
    else:
        weight_spec = pl.BlockSpec((depth, tile), lambda j: (0, j))
    return pl.pallas_call(
        functools.partial(rows_product_body, turned),
        out_shape=pltpu.HBM((rows, width), BF16),
        grid=(width // tile,),
        in_specs=[
            pl.BlockSpec((rows, depth), lambda j: (side, 0), pipeline_mode=pl.Buffered(1)),
            weight_spec,
        ]
        + [pl.BlockSpec(memory_space=pl.ANY)] * len(waits),
        out_specs=pl.BlockSpec((rows, tile), lambda j: (0, j)),
        compiler_params=pltpu.CompilerParams(vmem_limit_bytes=24 * 2**20),
        cost_estimate=SHORT,
    )(*in_hbm(values, weights, *waits))


def small_call(body, out_shape, *operands, free=0):
    held = len(operands) - free
    return pl.pallas_call(
        body,
        out_shape=tuple(pltpu.HBM(shape, dtype) for shape, dtype in out_shape),
        in_specs=whole_in_vmem(len(operands)),
        out_specs=tuple(whole_in_vmem(len(out_shape))),
        compiler_params=pltpu.CompilerParams(vmem_limit_bytes=24 * 2**20),
        cost_estimate=SHORT,
    )(*in_hbm(*operands[:held]), *operands[held:])


def halves_body(near, next_row, upper, lower):
    half = upper.shape[0]
    upper[...] = near[:half, :]
    lower[...] = next_row[half:, :]


def join_body(upper, lower, out):
    half = upper.shape[0]
    out[:half, :] = upper[...]
    out[half:, :] = lower[...]


def pairs_body(even, got, own, *outs):
    rows = own.shape[0]
    for number, out in enumerate((own, *outs)):
        window = slice(number * rows, (number + 1) * rows)
        total = even[window, :].astype(F32) + got[window, :].astype(F32)
        out[...] = total.astype(out.dtype)


def row_mean(values):
    return jnp.mean(values, axis=1, keepdims=True)


def summed(terms):
    total = terms[0][...].astype(F32)
    for one in terms[1:]:
        total = total + one[...].astype(F32)
    return total


def norm_two_body(tokens, gain, cot, *refs):
    terms, (hidden_one, act_two, both) = refs[:-3], refs[-3:]
    total = tokens[...].astype(F32) + summed(terms)
    hidden_one[...] = total
    inverse = lax.rsqrt(row_mean(total * total) + EPS)
    act_two[...] = (total * inverse * gain[...]).astype(BF16)
    both[0] = act_two[...]
    both[1] = cot[...]


def norm_back(values, gain, beside, terms):
    act_back = summed(terms)
    rows = values[...].astype(F32)
    inverse = lax.rsqrt(row_mean(rows * rows) + EPS)
    normed = rows * inverse
    scaled = act_back * gain[...]
    total = beside[...].astype(F32) + inverse * (scaled - normed * row_mean(scaled * normed))
    return total, act_back * normed


def norm_two_back_body(values, gain, beside, *refs):
    terms, (back, back_low) = refs[:-2], refs[-2:]
    rows = back.shape[0]
    back[...], gain_terms = norm_back(values, gain, beside, terms)
    back_low[:rows, :] = back[...].astype(BF16)
    gain_row = jnp.sum(gain_terms, axis=0, keepdims=True)
    back_low[rows:, :] = jnp.broadcast_to(gain_row, (16, back.shape[1])).astype(BF16)


def norm_one_back_body(values, gain, beside, *refs):
    terms, back = refs[:-1], refs[-1]
    back[...], _ = norm_back(values, gain, beside, terms)


def layer_out_body(hidden_one, *refs):
    refs[-1][...] = (hidden_one[...] + summed(refs[:-1])).astype(BF16)


def swap(values, distance, axis):
    size = lax.axis_size(axis)
    return lax.ppermute(values, axis, [(i, i ^ distance) for i in range(size)])


def block_order(shards):
    return list(range(0, shards, 2)) + list(range(1, shards, 2))


class RowGather:
    def __init__(self, values):
        self.values = values
        self.moving = [swap(values, 2, "sp"), swap(values, 4, "sp")]

    def forward(self):
        self.near, self.next_row = self.moving
        rows, width = self.values.shape
        half = rows // 32 * 16
        shapes = (((half, width), BF16), ((rows - half, width), BF16))
        upper, lower = small_call(halves_body, shapes, self.near, self.next_row)
        self.sent = upper
        self.moving = [swap(upper, 4, "sp"), swap(lower, 2, "sp")]

    def cores(self):
        (far,) = small_call(join_body, ((self.values.shape, BF16),), *self.moving)
        self.evens = [self.values, self.near, self.next_row, far]
        self.sent = far
        self.moving = [swap(block, 1, "sp") for block in self.evens]

    def blocks(self):
        return self.evens + self.moving


class RowSum:
    def __init__(self, odd_terms):
        self.moving = [swap(odd_terms, 1, "sp")]

    def add_pairs(self, even_terms):
        shape = (even_terms.shape[0] // 4, even_terms.shape[1])
        self.own, *self.sent = small_call(
            pairs_body, ((shape, F32), *((shape, BF16),) * 3), even_terms, *self.moving, free=1
        )
        self.send()

    def send(self):
        self.moving = [swap(one, n, "sp") for one, n in zip(self.sent, (2, 4, 6), strict=True)]

    def terms(self):
        return self.own, *self.moving


def gather_rel(values):
    evens, distance = [values], 2
    while distance < lax.axis_size("sp"):
        evens = evens + [swap(block, distance, "sp") for block in evens]
        distance *= 2
    return evens + [swap(block, 1, "sp") for block in evens]


def scatter_rel(even_terms, odd_terms):
    shards = lax.axis_size("sp")
    got = swap(odd_terms, 1, "sp").astype(F32)
    sums = (even_terms.astype(F32) + got).reshape(shards // 2, -1, even_terms.shape[1])
    distance = shards // 2
    while distance > 1:
        kept = distance // 2
        sums = sums[:kept] + swap(sums[kept:].astype(BF16), distance, "sp").astype(F32)
        distance //= 2
    return sums[0]


def on_device(
    tokens,
    doc_lengths,
    w_query,
    w_key,
    w_value,
    w_out,
    gain_attn,
    gain_mlp,
    w_gate,
    w_up,
    w_down,
    cotangent,
):
    shards = lax.axis_size("sp")
    groups = lax.axis_size("dp")
    seq_rank = lax.axis_index("sp")
    tok_rows, width = tokens.shape
    group_rows = tok_rows * shards
    heads_total = w_query.shape[1] // HD
    kv_total = w_key.shape[1] // HD
    copies = max(1, shards // kv_total)
    q_cols = heads_total // shards * HD
    part_rows = w_query.shape[0]
    half = shards // 2

    planned = shards == 8 and groups == 4
    w_mixed = pack_weights(shards, copies, w_query, w_key, w_value, gain_attn, gain_mlp)
    columns = w_mixed.shape[2]
    w_local = lax.all_to_all(w_mixed, "sp", split_axis=0, concat_axis=0, tiled=True)
    gain_one = w_local[:, part_rows, :part_rows].reshape(1, width).astype(F32)
    gain_two = w_local[:, part_rows + 1, :part_rows].reshape(1, width).astype(F32)

    lengths = doc_lengths[0]
    count = lengths.shape[0]
    before = jnp.arange(count)[None, :] < jnp.arange(count)[:, None]
    starts = jnp.sum(jnp.where(before, lengths[None, :], 0), axis=1).astype(jnp.int32)
    places = jnp.arange(group_rows, dtype=jnp.int32)
    begins = jnp.max(jnp.where(starts[None, :] <= places[:, None], starts[None, :], 0), axis=1)
    angles = (places - begins).astype(F32)[:, None] * frequencies(HD)[None, :]
    cosine_half, sine_half = jnp.cos(angles), jnp.sin(angles)
    cosine = jnp.concatenate([cosine_half] * 4, axis=1)
    sine = jnp.concatenate([-sine_half, sine_half] * 2, axis=1)
    index = jnp.asarray(block_order(shards), jnp.int32) ^ seq_rank.astype(jnp.int32)

    def attend(blocks, weights):
        gain = weights[:, part_rows, :part_rows].reshape(1, width).astype(F32)
        return attention(index, starts, blocks, gain, weights, cosine, sine, w_out, q_cols)

    half_rows = group_rows // 2

    def terms(values, weights, side, turned=False, waits=()):
        return rows_product(side, values, weights, turned, waits)

    rows_f32, rows_bf16 = ((tok_rows, width), F32), ((tok_rows, width), BF16)

    def norm_two(summed):
        outs = (rows_f32, rows_bf16, ((2, tok_rows, width), BF16))
        return small_call(norm_two_body, outs, tokens, gain_two, cotangent, *summed)

    branch_shape = ((tok_rows + 16, width), BF16)

    def norm_two_back(summed, hidden_one):
        outs = (rows_f32, branch_shape)
        return small_call(norm_two_back_body, outs, hidden_one, gain_two, cotangent, *summed)

    def norm_one_back(summed, beside):
        (back,) = small_call(norm_one_back_body, (rows_f32,), tokens, gain_one, beside, *summed)
        return back

    def attend_back(blocks, waits=()):
        return attention_back(
            index, starts, blocks, w_out, mixed, log_sums, out_rel, cosine, sine, waits
        )

    def to_rows(grad_mixed):
        blocks = grad_mixed.reshape(shards, part_rows, columns)
        return lax.all_to_all(blocks, "sp", split_axis=0, concat_axis=0, tiled=True)

    def grow(kind, works, began, *waits):
        cot_rows, act_rows = [work[4] for work in works], [work[3] for work in works]
        mine = [work[(1, 2, 0)[kind]] for work in works]
        if kind == 2:
            return weight_grad(mine, cot_rows, 1024, 512, waits, began)
        return weight_grad(act_rows, mine, 512, 1024, waits, began)

    dp_rank = lax.axis_index("dp").astype(jnp.int32)

    if planned:
        which = dp_rank ^ jnp.arange(1, groups, dtype=jnp.int32)
        token_gather = RowGather(tokens)
        *token_gather.moving, cosine, sine = together(*token_gather.moving, cosine, sine)
        token_gather.forward()
        token_gather.cores()
        *token_blocks, w_local = together(*token_gather.evens[1:], *token_gather.moving, w_local)
        token_blocks = [tokens] + token_blocks

        cot_gather = RowGather(after(cotangent, w_local))
        act_one, mixed, out_rel, log_sums, out_even, out_odd = attend(token_blocks, w_local)
        out_even, out_odd, *cot_gather.moving = together(
            out_even, out_odd, *cot_gather.moving
        )

        out_sum = RowSum(out_odd)
        out_sum.add_pairs(out_even)
        cot_gather.moving = [after(one, *out_sum.sent) for one in cot_gather.moving]
        cot_gather.forward()
        w_projections = after(w_local, *out_sum.sent)[:, :part_rows, :].reshape(width, columns)
        w_projections, *moving = together(w_projections, *out_sum.moving, *cot_gather.moving)
        out_sum.moving, cot_gather.moving = moving[:3], moving[3:]
        hidden_one, act_two, both = norm_two(out_sum.terms())

        act_gather = RowGather(act_two)
        both = lax.all_gather(both, ("dp", "sp"), axis=0).reshape(
            groups, shards, 2, tok_rows, width
        )
        act_gather.moving = together(*act_gather.moving)
        act_gather.forward()
        cot_gather.moving = [after(one, act_gather.sent) for one in cot_gather.moving]
        cot_gather.cores()
        act_gather.cores()
        *act_gather.moving, one, two, three, four = together(
            *act_gather.moving, *cot_gather.moving
        )
        cot_gather.moving = [one, two, three, four]

        own = ffn(act_gather.blocks(), cot_gather.blocks(), w_gate, w_up, w_down)
        back_sum = RowSum(act_back(1, own[1], own[2], w_gate, w_up, BF16))
        even_back = act_back(0, own[1], own[2], w_gate, w_up, BF16, (own[0],))
        back_sum.add_pairs(even_back)
        mlp_odd = terms(own[0], w_down, 1, False, back_sum.sent)
        grad_gate = grow(0, [own], None, mlp_odd)
        grad_up = grow(1, [own], None, grad_gate)
        grad_up, mlp_odd, *back_sum.moving = together(grad_up, mlp_odd, *back_sum.moving)
        hidden_one_back, branch = norm_two_back(back_sum.terms(), hidden_one)

        branch_gather = RowGather(branch)
        mlp_sum = RowSum(after(mlp_odd, branch))
        mlp_even = terms(own[0], w_down, 0, False, (branch,))
        grad_down = grow(2, [own], None, mlp_even)
        grad_down, mlp_even, *moving = together(
            grad_down, mlp_even, *branch_gather.moving, *mlp_sum.moving
        )
        branch_gather.moving, mlp_sum.moving = moving[:2], moving[2:]

        branch_gather.forward()
        branch_gather.cores()
        mlp_even, *branch_gather.moving = together(mlp_even, *branch_gather.moving)
        mixed_back, grad_out_terms = attend_back(branch_gather.blocks())
        grad_mixed = weight_grad([act_one], [mixed_back], 512, columns, (), None, BF16)
        mixed_sum, grad_out = lax.psum((grad_mixed, grad_out_terms), "dp")
        one_odd = terms(mixed_back, w_projections, 1, True, (grad_mixed,))
        one_sum = RowSum(one_odd)
        one_even = terms(mixed_back, w_projections, 0, True, (one_odd,))
        mlp_sum.add_pairs(after(mlp_even, one_even))
        others = ffn_others(which, both, w_gate, w_up, w_down, mlp_sum.sent)
        *others, one_even, got, one, two, three = together(
            *others, one_even, *one_sum.moving, *mlp_sum.moving
        )
        one_sum.moving, mlp_sum.moving = [got], [one, two, three]

        one_sum.add_pairs(one_even)
        grad_gate, grad_up = grad_pair(
            which,
            both,
            others[1],
            others[2],
            grad_gate,
            grad_up,
            256,
            one_sum.sent,
        )
        (layer_out,) = small_call(
            layer_out_body, (rows_bf16,), after(hidden_one, grad_gate), *mlp_sum.terms()
        )
        layer_out, *one_sum.moving = together(layer_out, *one_sum.moving)

        grad_tokens = norm_one_back(one_sum.terms(), hidden_one_back)
        mixed_sum, grad_out, grad_tokens = together(mixed_sum, grad_out, grad_tokens)
        mixed_rows = to_rows(mixed_sum)
        grad_down = grad_others(
            which, both, 1, others[0], grad_down, 1024, 512, (mixed_sum,)
        )
        waits = (grad_down,)
    else:
        waits = ()
        w_projections = w_local[:, :part_rows, :].reshape(width, columns)
        act_one, mixed, out_rel, log_sums, out_even, out_odd = attend(gather_rel(tokens), w_local)
        hidden_one, act_two, _ = norm_two((scatter_rel(out_even, out_odd),))
        act_blocks, cot_blocks, half = gather_rel(act_two), gather_rel(cotangent), shards // 2
        own = [
            jnp.concatenate(parts, axis=0)
            for parts in zip(
                ffn(act_blocks[:half], cot_blocks[:half], w_gate, w_up, w_down),
                ffn(act_blocks[half:], cot_blocks[half:], w_gate, w_up, w_down),
                strict=True,
            )
        ]
        act_two_back = scatter_rel(
            act_back(0, own[1], own[2], w_gate, w_up, BF16),
            act_back(1, own[1], own[2], w_gate, w_up, BF16),
        )
        hidden_one_back, branch = norm_two_back((act_two_back,), hidden_one)
        mixed_back, grad_out_terms = attend_back(gather_rel(branch))
        act_one_back = scatter_rel(
            terms(mixed_back, w_projections, 0, True), terms(mixed_back, w_projections, 1, True)
        )
        mixed_rows = to_rows(lax.psum(contract(act_one, mixed_back, 0, 0).astype(BF16), "dp"))
        mlp_out = scatter_rel(terms(own[0], w_down, 0), terms(own[0], w_down, 1))
        layer_out = (hidden_one + mlp_out).astype(BF16)
        grad_tokens = norm_one_back((act_one_back,), hidden_one_back)
        grad_out, grad_gate, grad_up, grad_down = (
            lax.psum(grad.astype(BF16), "dp").astype(F32)
            for grad in (grad_out_terms, *(grow(kind, [own], None) for kind in range(3)))
        )
    grad_gain_mlp = lax.dynamic_slice(
        grad_out, (q_cols, seq_rank * part_rows), (1, part_rows)
    ).astype(F32)[0]
    if copies == 1:
        grad_query, grad_key, grad_value, products, grad_out = unpack_grads(
            mixed_rows[None], grad_out, (w_query, w_key, w_value), q_cols, waits
        )
        products = products.reshape(part_rows)
    else:
        grad_out = grad_out[:q_cols].astype(F32)
        parts = jnp.transpose(mixed_rows.astype(F32), (1, 0, 2))
        grad_query = parts[:, :, :q_cols].reshape(part_rows, shards * q_cols)
        grad_key, grad_value = (
            parts[:, :, first : first + HD]
            .reshape(part_rows, kv_total, copies, HD)
            .sum(axis=2)
            .reshape(part_rows, -1)
            for first in (q_cols, q_cols + HD)
        )
        products = sum(
            jnp.sum(weight.astype(F32) * grad, axis=1)
            for weight, grad in (
                (w_query, grad_query),
                (w_key, grad_key),
                (w_value, grad_value),
            )
        )
    grad_gain_attn = products / gain_attn.astype(F32)
    return (
        layer_out,
        grad_tokens,
        grad_query,
        grad_key,
        grad_value,
        grad_out,
        grad_gain_attn,
        grad_gain_mlp,
        grad_gate,
        grad_up,
        grad_down,
    )


def solution(mesh):
    placed = (
        P(("dp", "sp"), None),
        P("dp", None),
        P("sp", None),
        P("sp", None),
        P("sp", None),
        P("sp", None),
        P("sp"),
        P("sp"),
        P(None, "sp"),
        P(None, "sp"),
        P("sp", None),
        P(("dp", "sp"), None),
    )
    return jax.shard_map(
        on_device,
        mesh=mesh,
        in_specs=placed,
        out_specs=(
            P(("dp", "sp"), None),
            P(("dp", "sp"), None),
            P("sp", None),
            P("sp", None),
            P("sp", None),
            P("sp", None),
            P("sp"),
            P("sp"),
            P(None, "sp"),
            P(None, "sp"),
            P("sp", None),
        ),
        check_vma=False,
    )
```

```python
import functools

import jax
import jax.numpy as jnp
from jax import lax
from jax.experimental import pallas as pl
from jax.experimental.pallas import tpu as pltpu
from jax.sharding import PartitionSpec as P

HD = 64
Q_ROWS = 256
F32 = jnp.float32
BF16 = jnp.bfloat16


EPS = 1e-05
THETA = 500000.0
FACTOR = 32.0
LOW_FACTOR = 1.0
HIGH_FACTOR = 4.0
BASE_CONTEXT = 8192.0
MASKED = -1e30


def frequencies(head_size):
    half_index = jnp.arange(head_size // 2).astype(jnp.float32)
    inverse = THETA ** (-2.0 * half_index / head_size)
    wavelength = 2.0 * jnp.pi / inverse
    smooth = (BASE_CONTEXT / wavelength - LOW_FACTOR) / (HIGH_FACTOR - LOW_FACTOR)
    middle = (1.0 - smooth) * inverse / FACTOR + smooth * inverse
    slow_band = jnp.where(wavelength > BASE_CONTEXT / LOW_FACTOR, inverse / FACTOR, middle)
    return jnp.where(wavelength < BASE_CONTEXT / HIGH_FACTOR, inverse, slow_band)


def contract(left, right, left_dim, right_dim):
    return lax.dot_general(
        left, right, (((left_dim,), (right_dim,)), ((), ())), preferred_element_type=jnp.float32
    )


SHORT = pl.CostEstimate(flops=0, bytes_accessed=0, transcendentals=0)


def product(left, right, left_dim, right_dim):
    return lax.dot_general(
        left, right, (((left_dim,), (right_dim,)), ((), ())), preferred_element_type=F32
    )


def whole_in_vmem(count):
    return [pl.BlockSpec(memory_space=pltpu.VMEM)] * count


def in_hbm(*values):
    return [pltpu.with_memory_space_constraint(one, pltpu.HBM) for one in values]


def after(values, *earlier):
    def body(*refs):
        pass

    return pl.pallas_call(
        body,
        out_shape=pltpu.HBM(values.shape, values.dtype),
        in_specs=[pl.BlockSpec(memory_space=pl.ANY)] * (1 + len(earlier)),
        out_specs=pl.BlockSpec(memory_space=pl.ANY),
        input_output_aliases={0: 0},
        cost_estimate=pl.CostEstimate(flops=0, bytes_accessed=0, transcendentals=0),
    )(*in_hbm(values, *earlier))


def together(*values):
    def body(*refs):
        pass

    anywhere = pl.BlockSpec(memory_space=pl.ANY)
    call = pl.pallas_call(
        body,
        out_shape=tuple(pltpu.HBM(one.shape, one.dtype) for one in values),
        in_specs=[anywhere] * len(values),
        out_specs=(anywhere,) * len(values),
        input_output_aliases={n: n for n in range(len(values))},
        cost_estimate=pl.CostEstimate(flops=0, bytes_accessed=0, transcendentals=0),
    )
    return list(call(*in_hbm(*values)))


def turn_signed(values, signed_sine):
    lane = lax.broadcasted_iota(jnp.int32, values.shape, 1) % HD
    turned = jnp.where(
        lane < HD // 2, pltpu.roll(values, 128 - HD // 2, 1), pltpu.roll(values, HD // 2, 1)
    )
    return turned * signed_sine


def rope_tables(cosine, sine, last):
    if not last:
        return cosine, sine
    lane = lax.broadcasted_iota(jnp.int32, cosine.shape, 1)
    return jnp.where(lane < HD, cosine, 1.0), jnp.where(lane < HD, sine, 0.0)


def score_mask(starts_ref, first_row, rows, keys):
    place = first_row + lax.broadcasted_iota(jnp.int32, (rows, 1), 0)
    begin = jnp.zeros((rows, 1), jnp.int32)
    for index in range(starts_ref.shape[0]):
        start = starts_ref[index]
        begin = jnp.maximum(begin, jnp.where(place >= start, start, 0))
    key_place = lax.broadcasted_iota(jnp.int32, (rows, keys), 1)
    return (key_place >= begin) & (key_place <= place)


def attention_body(shards, q_cols, index_ref, starts_ref, *refs):
    tokens = refs[:shards]
    gain, weights, cosine, sine, w_out = refs[shards : shards + 5]
    act, mixed, out_rel, log_sums, even_terms, odd_terms, out_rows = refs[shards + 5 :]
    rows = tokens[0].shape[0]
    total = rows * shards
    part = act.shape[1] // shards
    columns = mixed.shape[1]
    groups = columns // 128
    half = shards // 2
    for side in range(2):
        for block in range(side * half, side * half + half):
            values = tokens[block][...].astype(F32)
            inverse = lax.rsqrt(jnp.mean(values * values, axis=1, keepdims=True) + EPS)
            act[block * rows : (block + 1) * rows, :] = (values * inverse * gain[...]).astype(BF16)
        first = side * half * rows
        sums = jnp.zeros((half * rows, columns), F32)
        for source in range(shards):
            sums = sums + product(
                act[first : first + half * rows, source * part : (source + 1) * part],
                weights[source, :part, :],
                1,
                0,
            )
        for block in range(half):
            place = pl.multiple_of(index_ref[side * half + block] * rows, rows)
            cosine_rows = cosine[pl.ds(place, rows), :]
            sine_rows = sine[pl.ds(place, rows), :]
            for group in range(groups):
                piece = sums[block * rows : (block + 1) * rows, group * 128 : (group + 1) * 128]
                cosine_part, sine_part = rope_tables(cosine_rows, sine_rows, group == groups - 1)
                mixed[pl.ds(place, rows), group * 128 : (group + 1) * 128] = (
                    piece * cosine_part + turn_signed(piece, sine_part)
                ).astype(BF16)
    scale = HD ** (-0.5)
    for first in range(0, total, Q_ROWS):
        keys = first + Q_ROWS
        allowed = score_mask(starts_ref, first, Q_ROWS, keys)
        key_rows = mixed[:keys, q_cols : q_cols + HD]
        value_rows = mixed[:keys, q_cols + HD : q_cols + 2 * HD]
        for head in range(q_cols // HD):
            query = mixed[first:keys, head * HD : (head + 1) * HD] * jnp.asarray(scale, BF16)
            scores = jnp.where(allowed, product(query, key_rows, 1, 1), MASKED)
            largest = jnp.max(scores, axis=1, keepdims=True)
            weights_row = jnp.exp(scores - largest)
            total_weight = jnp.sum(weights_row, axis=1, keepdims=True)
            attended = product(weights_row.astype(BF16), value_rows, 1, 0) / total_weight
            out_rows[first:keys, head * HD : (head + 1) * HD] = attended.astype(BF16)
            log_sums[first:keys, head : head + 1] = largest + jnp.log(total_weight)
    for block in range(shards):
        place = pl.multiple_of(index_ref[block] * rows, rows)
        out_rel[block * rows : (block + 1) * rows, :] = out_rows[pl.ds(place, rows), :]
    width = w_out.shape[1]
    for side, terms in enumerate((even_terms, odd_terms)):
        heads = out_rel[side * half * rows : (side + 1) * half * rows, :]
        for first in range(0, width, 512):
            cut = slice(first, first + 512)
            terms[:, cut] = product(heads, w_out[:, cut], 1, 0).astype(BF16)


def attention(index, starts, tokens, gain, weights, cosine, sine, w_out, q_cols):
    shards = len(tokens)
    rows, width = tokens[0].shape
    total = rows * shards
    columns = weights.shape[2]
    smem = pl.BlockSpec(memory_space=pltpu.SMEM)
    return pl.pallas_call(
        functools.partial(attention_body, shards, q_cols),
        out_shape=(
            pltpu.HBM((total, width), BF16),
            pltpu.HBM((total, columns), BF16),
            pltpu.HBM((total, q_cols), BF16),
            pltpu.HBM((total, q_cols // HD), F32),
            pltpu.HBM((total // 2, width), BF16),
            pltpu.HBM((total // 2, width), BF16),
        ),
        in_specs=[smem, smem] + whole_in_vmem(shards + 5),
        out_specs=tuple(whole_in_vmem(6)),
        scratch_shapes=[pltpu.VMEM((total, q_cols), BF16)],
        compiler_params=pltpu.CompilerParams(vmem_limit_bytes=58 * 2**20),
        cost_estimate=SHORT,
    )(index, starts, *in_hbm(*tokens, gain, weights, cosine, sine, w_out))


def attention_back_body(shards, rows, q_cols, waits, index_ref, starts_ref, *refs):
    branch = refs[:shards]
    w_out, mixed, log_sums, out_rel, cosine, sine = refs[shards : shards + 6]
    mixed_back, grad_out, *scratch = refs[shards + 6 + waits :]
    branch_rows, heads_back, query_grads, key_grads, value_grads = scratch
    total = rows * shards
    columns = mixed.shape[1]
    half = total // 2
    gain_terms = jnp.zeros(branch[0].shape[1:], F32)[None]
    for block in range(shards):
        branch_rows[block * rows : (block + 1) * rows, :] = branch[block][:rows, :]
        gain_terms = gain_terms + branch[block][rows:, :].astype(F32)[:1, :]
    grad_out[q_cols:, :] = jnp.broadcast_to(gain_terms, (16, gain_terms.shape[1])).astype(BF16)
    for side in range(2):
        back = product(branch_rows[side * half : (side + 1) * half, :], w_out[...], 1, 1).astype(
            BF16
        )
        for block in range(shards // 2):
            place = pl.multiple_of(index_ref[side * (shards // 2) + block] * rows, rows)
            heads_back[pl.ds(place, rows), :] = back[block * rows : (block + 1) * rows, :]
    grad_out[:q_cols, :] = product(out_rel[...], branch_rows[...], 0, 0).astype(BF16)
    key_grads[...] = jnp.zeros_like(key_grads)
    value_grads[...] = jnp.zeros_like(value_grads)
    scale = HD ** (-0.5)
    for first in range(0, total, Q_ROWS):
        keys = first + Q_ROWS
        allowed = score_mask(starts_ref, first, Q_ROWS, keys)
        key_rows = mixed[:keys, q_cols : q_cols + HD]
        value_rows = mixed[:keys, q_cols + HD : q_cols + 2 * HD]
        for head in range(q_cols // HD):
            cut = slice(head * HD, (head + 1) * HD)
            query = mixed[first:keys, cut] * jnp.asarray(scale, BF16)
            back = heads_back[first:keys, cut]
            scores = jnp.where(allowed, product(query, key_rows, 1, 1), MASKED)
            probs = jnp.exp(scores - log_sums[first:keys, head : head + 1])
            probs_back = product(back, value_rows, 1, 1)
            delta = jnp.sum(probs * probs_back, axis=1, keepdims=True)
            scores_back = (probs * (probs_back - delta)).astype(BF16)
            query_grads[first:keys, cut] = product(scores_back, key_rows, 1, 0) * scale
            key_grads[:keys, :] += product(scores_back, query, 0, 0)
            value_grads[:keys, :] += product(probs.astype(BF16), back, 0, 0)
    for block in range(shards):
        place = pl.multiple_of(index_ref[block] * rows, rows)
        window = pl.ds(place, rows)
        cosine_rows, sine_rows = cosine[window, :], sine[window, :]
        for group in range(columns // 128):
            last = group == columns // 128 - 1
            if last:
                piece = jnp.concatenate([key_grads[window, :], value_grads[window, :]], axis=1)
            else:
                piece = query_grads[window, group * 128 : (group + 1) * 128]
            cosine_part, sine_part = rope_tables(cosine_rows, sine_rows, last)
            mixed_back[block * rows : (block + 1) * rows, group * 128 : (group + 1) * 128] = (
                piece * cosine_part - turn_signed(piece, sine_part)
            ).astype(BF16)


def attention_back(
    index, starts, branch, w_out, mixed, log_sums, out_rel, cosine, sine, waits=()
):
    shards = len(branch)
    width = branch[0].shape[1]
    total, columns = mixed.shape
    rows = total // shards
    q_cols = out_rel.shape[1]
    smem = pl.BlockSpec(memory_space=pltpu.SMEM)
    return pl.pallas_call(
        functools.partial(attention_back_body, shards, rows, q_cols, len(waits)),
        out_shape=(
            pltpu.HBM((total, columns), BF16),
            pltpu.HBM((q_cols + 16, width), BF16),
        ),
        in_specs=[smem, smem]
        + whole_in_vmem(shards + 6)
        + [pl.BlockSpec(memory_space=pl.ANY)] * len(waits),
        out_specs=tuple(whole_in_vmem(2)),
        scratch_shapes=[
            pltpu.VMEM((total, width), BF16),
            pltpu.VMEM((total, q_cols), BF16),
            pltpu.VMEM((total, q_cols), F32),
            pltpu.VMEM((total, HD), F32),
            pltpu.VMEM((total, HD), F32),
        ],
        compiler_params=pltpu.CompilerParams(vmem_limit_bytes=48 * 2**20),
        cost_estimate=SHORT,
    )(index, starts, *in_hbm(*branch, w_out, mixed, log_sums, out_rel, cosine, sine, *waits))


def ffn_body(pieces, *refs):
    act, cot = refs[:pieces], refs[pieces : 2 * pieces]
    w_gate, w_up, w_down = refs[2 * pieces : 2 * pieces + 3]
    hidden, gate_back, up_back, act_out, cot_out, act_rows, cot_rows = refs[2 * pieces + 3 :]
    step = pl.program_id(0)

    @pl.when(step == 0)
    def _():
        for parts, rows in ((act, act_rows), (cot, cot_rows)):
            first = 0
            for part in parts:
                rows[first : first + part.shape[0], :] = part[...]
                first += part.shape[0]

    strip = act_out.shape[1]
    window = pl.ds(pl.multiple_of(step * strip, strip), strip)
    act_out[...] = act_rows[:, window]
    cot_out[...] = cot_rows[:, window]
    gate_value = product(act_rows[...], w_gate[...], 1, 0)
    up_value = product(act_rows[...], w_up[...], 1, 0)
    hidden_back = product(cot_rows[...], w_down[...], 1, 1)
    sigmoid_gate = 1.0 / (1.0 + jnp.exp(-gate_value))
    silu_gate = gate_value * sigmoid_gate
    hidden[...] = (silu_gate * up_value).astype(BF16)
    gate_back[...] = (
        hidden_back * up_value * sigmoid_gate * (1.0 + gate_value * (1.0 - sigmoid_gate))
    ).astype(BF16)
    up_back[...] = (hidden_back * silu_gate).astype(BF16)


def ffn(act, cot, w_gate, w_up, w_down):
    pieces = len(act)
    rows, width = act[0].shape
    total = rows * pieces
    units = w_gate.shape[1]
    tile = min(256, units)
    steps = units // tile
    strip = width // steps
    block = pl.BlockSpec((rows, width), lambda j: (0, 0), pipeline_mode=pl.Buffered(1))
    columns = pl.BlockSpec((width, tile), lambda j: (0, j))
    out = pl.BlockSpec((total, tile), lambda j: (0, j))
    wide = pl.BlockSpec((total, strip), lambda j: (0, j))
    return pl.pallas_call(
        functools.partial(ffn_body, pieces),
        out_shape=(pltpu.HBM((total, units), BF16),) * 3 + (pltpu.HBM((total, width), BF16),) * 2,
        grid=(steps,),
        in_specs=[block] * (2 * pieces)
        + [columns, columns, pl.BlockSpec((tile, width), lambda j: (j, 0))],
        out_specs=(out, out, out, wide, wide),
        scratch_shapes=[pltpu.VMEM((total, width), BF16)] * 2,
        compiler_params=pltpu.CompilerParams(vmem_limit_bytes=48 * 2**20),
        cost_estimate=SHORT,
    )(*in_hbm(*act, *cot, w_gate, w_up, w_down))


def ffn_others_body(waits, which, act, cot, w_gate, w_up, w_down, *refs):
    hidden, gate_back, up_back = refs[waits:]
    act_rows = act[...].reshape(hidden.shape[0], w_gate.shape[0])
    cot_rows = cot[...].reshape(act_rows.shape)
    gate_value = product(act_rows, w_gate[...], 1, 0)
    up_value = product(act_rows, w_up[...], 1, 0)
    hidden_back = product(cot_rows, w_down[...], 1, 1)
    sigmoid_gate = 1.0 / (1.0 + jnp.exp(-gate_value))
    silu_gate = gate_value * sigmoid_gate
    hidden[...] = (silu_gate * up_value).astype(BF16)
    gate_back[...] = (
        hidden_back * up_value * sigmoid_gate * (1.0 + gate_value * (1.0 - sigmoid_gate))
    ).astype(BF16)
    up_back[...] = (hidden_back * silu_gate).astype(BF16)


def ffn_others(which, both, w_gate, w_up, w_down, waits=()):
    count = which.shape[0]
    _, shards, _, rows, width = both.shape
    units, total = w_gate.shape[1], shards * rows
    tile = min(512, units)

    def rows_spec(kind):
        return pl.BlockSpec(
            (None, shards, None, rows, width), lambda i, j, w: (w[i], 0, kind, 0, 0)
        )

    columns = pl.BlockSpec((width, tile), lambda i, j, w: (0, j))
    out = pl.BlockSpec((total, tile), lambda i, j, w: (i, j))
    return pl.pallas_call(
        functools.partial(ffn_others_body, len(waits)),
        out_shape=(pltpu.HBM((total * count, units), BF16),) * 3,
        grid_spec=pltpu.PrefetchScalarGridSpec(
            num_scalar_prefetch=1,
            grid=(count, units // tile),
            in_specs=[
                rows_spec(0),
                rows_spec(1),
                columns,
                columns,
                pl.BlockSpec((tile, width), lambda i, j, w: (j, 0)),
            ]
            + [pl.BlockSpec(memory_space=pl.ANY)] * len(waits),
            out_specs=(out, out, out),
        ),
        compiler_params=pltpu.CompilerParams(vmem_limit_bytes=58 * 2**20),
        cost_estimate=SHORT,
    )(which, *in_hbm(both, both, w_gate, w_up, w_down, *waits))


def act_back_body(gate_back, up_back, w_gate, w_up, *refs):
    out = refs[-1]
    out[...] = (
        product(gate_back[...], w_gate[...], 1, 1) + product(up_back[...], w_up[...], 1, 1)
    ).astype(out.dtype)


def act_back(side, gate_back, up_back, w_gate, w_up, dtype, waits=()):
    total, units = gate_back.shape[0] // 2, gate_back.shape[1]
    width = w_gate.shape[0]
    tile = 512
    rows = pl.BlockSpec((total, units), lambda j: (side, 0), pipeline_mode=pl.Buffered(1))
    weights = pl.BlockSpec((tile, units), lambda j: (j, 0))
    return pl.pallas_call(
        act_back_body,
        out_shape=pltpu.HBM((total, width), dtype),
        grid=(width // tile,),
        in_specs=[rows, rows, weights, weights]
        + [pl.BlockSpec(memory_space=pl.ANY)] * len(waits),
        out_specs=pl.BlockSpec((total, tile), lambda j: (0, j)),
        compiler_params=pltpu.CompilerParams(vmem_limit_bytes=32 * 2**20),
        cost_estimate=SHORT,
    )(*in_hbm(gate_back, up_back, w_gate, w_up, *waits))


def weight_grad_body(pieces, began, *refs):
    left, right, out = refs[:pieces], refs[pieces : 2 * pieces], refs[-1]
    total = product(left[0][...], right[0][...], 0, 0)
    if began:
        total = total + refs[2 * pieces][...]
    for piece in range(1, pieces):
        total = total + product(left[piece][...], right[piece][...], 0, 0)
    out[...] = total.astype(out.dtype)


def weight_grad(left, right, row_tile, column_tile, waits=(), began=None, dtype=F32):
    pieces = len(left)
    rows, height = left[0].shape
    width = right[0].shape[1]
    row_tile, column_tile = min(row_tile, height), min(column_tile, width)
    tile_spec = pl.BlockSpec((row_tile, column_tile), lambda j, i: (i, j))
    start = () if began is None else (began,)
    return pl.pallas_call(
        functools.partial(weight_grad_body, pieces, began is not None),
        out_shape=pltpu.HBM((height, width), dtype),
        grid=(width // column_tile, height // row_tile),
        in_specs=[pl.BlockSpec((rows, row_tile), lambda j, i: (0, i))] * pieces
        + [pl.BlockSpec((rows, column_tile), lambda j, i: (0, j))] * pieces
        + [tile_spec] * len(start)
        + [pl.BlockSpec(memory_space=pl.ANY)] * len(waits),
        out_specs=tile_spec,
        compiler_params=pltpu.CompilerParams(vmem_limit_bytes=48 * 2**20),
        cost_estimate=SHORT,
    )(*in_hbm(*left, *right, *start, *waits))


def pack_weights_body(shards, copies, w_query, w_key, w_value, gains, out):
    part, q_cols = w_query.shape[0], w_query.shape[1] // shards
    out[:, part:, :] = jnp.broadcast_to(gains[...][None], (shards,) + gains.shape)
    for shard in range(shards):
        head = shard // copies * HD
        out[shard, :part, :q_cols] = w_query[:, shard * q_cols : (shard + 1) * q_cols]
        out[shard, :part, q_cols:] = jnp.concatenate(
            [w_key[:, head : head + HD], w_value[:, head : head + HD]], axis=1
        )


def pack_weights(shards, copies, w_query, w_key, w_value, gain_attn, gain_mlp):
    part = w_query.shape[0]
    columns = w_query.shape[1] // shards + 2 * HD
    gains = jnp.zeros((16, columns), BF16)
    gains = gains.at[0, :part].set(gain_attn).at[1, :part].set(gain_mlp)
    return pl.pallas_call(
        functools.partial(pack_weights_body, shards, copies),
        out_shape=pltpu.HBM((shards, part + 16, columns), BF16),
        in_specs=whole_in_vmem(4),
        out_specs=whole_in_vmem(1)[0],
        compiler_params=pltpu.CompilerParams(vmem_limit_bytes=16 * 2**20),
    )(*in_hbm(w_query, w_key, w_value, gains))


def unpack_grads_body(q_cols, pieces, sums, *refs):
    weights = refs[:3]
    query, key, value, products, out = refs[-5:]
    out[...] = sums[: out.shape[0], :].astype(F32)
    groups, shards, strip, _ = pieces.shape
    for number in range(groups):
        rows = slice(number * strip, (number + 1) * strip)
        for shard in range(shards):
            query[rows, shard * q_cols : (shard + 1) * q_cols] = pieces[
                number, shard, :, :q_cols
            ].astype(F32)
        for shard in range(0, shards, 2):
            for place, out in ((q_cols, key), (q_cols + HD, value)):
                out[rows, shard * HD : (shard + 2) * HD] = jnp.concatenate(
                    [pieces[number, shard + n, :, place : place + HD] for n in range(2)], axis=1
                ).astype(F32)
    total = jnp.zeros(products.shape, F32)
    for weight, grad in zip(weights, (query, key, value), strict=True):
        terms = weight[...].astype(F32) * grad[...]
        total = total + jnp.sum(terms, axis=1, keepdims=True)
    products[...] = total


def unpack_grads(pieces, sums, weights, q_cols, waits=()):
    groups, shards, strip, _ = pieces.shape
    rows = strip * groups
    return pl.pallas_call(
        functools.partial(unpack_grads_body, q_cols),
        out_shape=(
            jax.ShapeDtypeStruct((rows, shards * q_cols), F32),
            jax.ShapeDtypeStruct((rows, shards * HD), F32),
            jax.ShapeDtypeStruct((rows, shards * HD), F32),
            jax.ShapeDtypeStruct((rows, 1), F32),
            jax.ShapeDtypeStruct((q_cols, sums.shape[1]), F32),
        ),
        in_specs=whole_in_vmem(5) + [pl.BlockSpec(memory_space=pl.ANY)] * len(waits),
        out_specs=tuple(whole_in_vmem(5)),
        compiler_params=pltpu.CompilerParams(vmem_limit_bytes=24 * 2**20),
    )(pieces, *in_hbm(sums, *weights, *waits))


def grad_others_body(count, kind, which, *refs):
    rows, units, began = refs[:count], refs[count : 2 * count], refs[2 * count]
    out = refs[-1]
    total = began[...]
    for one, two in zip(rows, units, strict=True):
        one = one[...].reshape(two.shape[0], one.shape[-1])
        if kind:
            total = total + product(two[...], one, 0, 0)
        else:
            total = total + product(one, two[...], 0, 0)
    out[...] = total


def grad_others(which, both, kind, units_all, began, row_tile, column_tile, waits=()):
    count = which.shape[0]
    shards, rows = both.shape[1], both.shape[3]
    total = shards * rows
    height, width = began.shape
    wide, narrow = (column_tile, row_tile) if kind else (row_tile, column_tile)

    def rows_spec(number):
        def place(j, i, w):
            return (w[number], 0, kind, 0, j if kind else i)

        return pl.BlockSpec((None, shards, None, rows, wide), place)

    def units_spec(number):
        return pl.BlockSpec((total, narrow), lambda j, i, w: (number, i if kind else j))

    tile_spec = pl.BlockSpec((row_tile, column_tile), lambda j, i, w: (i, j))
    return pl.pallas_call(
        functools.partial(grad_others_body, count, kind),
        out_shape=pltpu.HBM((height, width), F32),
        grid_spec=pltpu.PrefetchScalarGridSpec(
            num_scalar_prefetch=1,
            grid=(width // column_tile, height // row_tile),
            in_specs=[rows_spec(n) for n in range(count)]
            + [units_spec(n) for n in range(count)]
            + [tile_spec]
            + [pl.BlockSpec(memory_space=pl.ANY)] * len(waits),
            out_specs=tile_spec,
        ),
        compiler_params=pltpu.CompilerParams(vmem_limit_bytes=48 * 2**20),
        cost_estimate=SHORT,
    )(which, *in_hbm(*[both] * count, *[units_all] * count, began, *waits))


def grad_pair_body(count, which, *refs):
    rows = [one[...] for one in refs[:count]]
    outs = refs[-2:]
    for kind, out in enumerate(outs):
        units = refs[count * (1 + kind) : count * (2 + kind)]
        total = refs[3 * count + kind][...]
        for one, two in zip(rows, units, strict=True):
            total = total + product(one.reshape(two.shape[0], one.shape[-1]), two[...], 0, 0)
        out[...] = total


def grad_pair(which, both, gates, ups, began_gate, began_up, row_tile, waits=()):
    count = which.shape[0]
    shards, rows = both.shape[1], both.shape[3]
    total = shards * rows
    height, width = began_gate.shape

    def rows_spec(number):
        return pl.BlockSpec(
            (None, shards, None, rows, row_tile), lambda i, w: (w[number], 0, 0, 0, i)
        )

    def units_spec(number):
        return pl.BlockSpec(
            (total, width), lambda i, w: (number, 0), pipeline_mode=pl.Buffered(1)
        )

    tile_spec = pl.BlockSpec((row_tile, width), lambda i, w: (i, 0))
    units_specs = [units_spec(n) for n in range(count)]
    return pl.pallas_call(
        functools.partial(grad_pair_body, count),
        out_shape=(pltpu.HBM((height, width), F32),) * 2,
        grid_spec=pltpu.PrefetchScalarGridSpec(
            num_scalar_prefetch=1,
            grid=(height // row_tile,),
            in_specs=[rows_spec(n) for n in range(count)]
            + units_specs
            + units_specs
            + [tile_spec] * 2
            + [pl.BlockSpec(memory_space=pl.ANY)] * len(waits),
            out_specs=(tile_spec, tile_spec),
        ),
        compiler_params=pltpu.CompilerParams(vmem_limit_bytes=56 * 2**20),
        cost_estimate=SHORT,
    )(
        which,
        *in_hbm(
            *[both] * count, *[gates] * count, *[ups] * count, began_gate, began_up, *waits
        ),
    )


def rows_product_body(turned, values, weights, *refs):
    out = refs[-1]
    out[...] = product(values[...], weights[...], 1, 1 if turned else 0).astype(out.dtype)


def rows_product(side, values, weights, turned=False, waits=()):
    rows, depth = values.shape[0] // 2, values.shape[1]
    width = weights.shape[0] if turned else weights.shape[1]
    tile = 512
    if turned:
        weight_spec = pl.BlockSpec((tile, depth), lambda j: (j, 0))
    else:
        weight_spec = pl.BlockSpec((depth, tile), lambda j: (0, j))
    return pl.pallas_call(
        functools.partial(rows_product_body, turned),
        out_shape=pltpu.HBM((rows, width), BF16),
        grid=(width // tile,),
        in_specs=[
            pl.BlockSpec((rows, depth), lambda j: (side, 0), pipeline_mode=pl.Buffered(1)),
            weight_spec,
        ]
        + [pl.BlockSpec(memory_space=pl.ANY)] * len(waits),
        out_specs=pl.BlockSpec((rows, tile), lambda j: (0, j)),
        compiler_params=pltpu.CompilerParams(vmem_limit_bytes=24 * 2**20),
        cost_estimate=SHORT,
    )(*in_hbm(values, weights, *waits))


def small_call(body, out_shape, *operands, free=0):
    held = len(operands) - free
    return pl.pallas_call(
        body,
        out_shape=tuple(pltpu.HBM(shape, dtype) for shape, dtype in out_shape),
        in_specs=whole_in_vmem(len(operands)),
        out_specs=tuple(whole_in_vmem(len(out_shape))),
        compiler_params=pltpu.CompilerParams(vmem_limit_bytes=24 * 2**20),
        cost_estimate=SHORT,
    )(*in_hbm(*operands[:held]), *operands[held:])


def halves_body(near, next_row, upper, lower):
    half = upper.shape[0]
    upper[...] = near[:half, :]
    lower[...] = next_row[half:, :]


def join_body(upper, lower, out):
    half = upper.shape[0]
    out[:half, :] = upper[...]
    out[half:, :] = lower[...]


def pairs_body(even, got, own, *outs):
    rows = own.shape[0]
    for number, out in enumerate((own, *outs)):
        window = slice(number * rows, (number + 1) * rows)
        total = even[window, :].astype(F32) + got[window, :].astype(F32)
        out[...] = total.astype(out.dtype)


def row_mean(values):
    return jnp.mean(values, axis=1, keepdims=True)


def summed(terms):
    total = terms[0][...].astype(F32)
    for one in terms[1:]:
        total = total + one[...].astype(F32)
    return total


def norm_two_body(tokens, gain, cot, *refs):
    terms, (hidden_one, act_two, both) = refs[:-3], refs[-3:]
    total = tokens[...].astype(F32) + summed(terms)
    hidden_one[...] = total
    inverse = lax.rsqrt(row_mean(total * total) + EPS)
    act_two[...] = (total * inverse * gain[...]).astype(BF16)
    both[0] = act_two[...]
    both[1] = cot[...]


def norm_back(values, gain, beside, terms):
    act_back = summed(terms)
    rows = values[...].astype(F32)
    inverse = lax.rsqrt(row_mean(rows * rows) + EPS)
    normed = rows * inverse
    scaled = act_back * gain[...]
    total = beside[...].astype(F32) + inverse * (scaled - normed * row_mean(scaled * normed))
    return total, act_back * normed


def norm_two_back_body(values, gain, beside, *refs):
    terms, (back, back_low) = refs[:-2], refs[-2:]
    rows = back.shape[0]
    back[...], gain_terms = norm_back(values, gain, beside, terms)
    back_low[:rows, :] = back[...].astype(BF16)
    gain_row = jnp.sum(gain_terms, axis=0, keepdims=True)
    back_low[rows:, :] = jnp.broadcast_to(gain_row, (16, back.shape[1])).astype(BF16)


def norm_one_back_body(values, gain, beside, *refs):
    terms, back = refs[:-1], refs[-1]
    back[...], _ = norm_back(values, gain, beside, terms)


def layer_out_body(hidden_one, *refs):
    refs[-1][...] = (hidden_one[...] + summed(refs[:-1])).astype(BF16)


def swap(values, distance, axis):
    size = lax.axis_size(axis)
    return lax.ppermute(values, axis, [(i, i ^ distance) for i in range(size)])


def block_order(shards):
    return list(range(0, shards, 2)) + list(range(1, shards, 2))


class RowGather:
    def __init__(self, values):
        self.values = values
        self.moving = [swap(values, 2, "sp"), swap(values, 4, "sp")]

    def forward(self):
        self.near, self.next_row = self.moving
        rows, width = self.values.shape
        half = rows // 32 * 16
        shapes = (((half, width), BF16), ((rows - half, width), BF16))
        upper, lower = small_call(halves_body, shapes, self.near, self.next_row)
        self.sent = upper
        self.moving = [swap(upper, 4, "sp"), swap(lower, 2, "sp")]

    def cores(self):
        (far,) = small_call(join_body, ((self.values.shape, BF16),), *self.moving)
        self.evens = [self.values, self.near, self.next_row, far]
        self.sent = far
        self.moving = [swap(block, 1, "sp") for block in self.evens]

    def blocks(self):
        return self.evens + self.moving


class RowSum:
    def __init__(self, odd_terms):
        self.moving = [swap(odd_terms, 1, "sp")]

    def add_pairs(self, even_terms):
        shape = (even_terms.shape[0] // 4, even_terms.shape[1])
        self.own, *self.sent = small_call(
            pairs_body, ((shape, F32), *((shape, BF16),) * 3), even_terms, *self.moving, free=1
        )
        self.send()

    def send(self):
        self.moving = [swap(one, n, "sp") for one, n in zip(self.sent, (2, 4, 6), strict=True)]

    def terms(self):
        return self.own, *self.moving


def gather_rel(values):
    evens, distance = [values], 2
    while distance < lax.axis_size("sp"):
        evens = evens + [swap(block, distance, "sp") for block in evens]
        distance *= 2
    return evens + [swap(block, 1, "sp") for block in evens]


def scatter_rel(even_terms, odd_terms):
    shards = lax.axis_size("sp")
    got = swap(odd_terms, 1, "sp").astype(F32)
    sums = (even_terms.astype(F32) + got).reshape(shards // 2, -1, even_terms.shape[1])
    distance = shards // 2
    while distance > 1:
        kept = distance // 2
        sums = sums[:kept] + swap(sums[kept:].astype(BF16), distance, "sp").astype(F32)
        distance //= 2
    return sums[0]


def on_device(
    tokens,
    doc_lengths,
    w_query,
    w_key,
    w_value,
    w_out,
    gain_attn,
    gain_mlp,
    w_gate,
    w_up,
    w_down,
    cotangent,
):
    shards = lax.axis_size("sp")
    groups = lax.axis_size("dp")
    seq_rank = lax.axis_index("sp")
    tok_rows, width = tokens.shape
    group_rows = tok_rows * shards
    heads_total = w_query.shape[1] // HD
    kv_total = w_key.shape[1] // HD
    copies = max(1, shards // kv_total)
    q_cols = heads_total // shards * HD
    part_rows = w_query.shape[0]
    half = shards // 2

    planned = shards == 8 and groups == 4
    w_mixed = pack_weights(shards, copies, w_query, w_key, w_value, gain_attn, gain_mlp)
    columns = w_mixed.shape[2]
    w_local = lax.all_to_all(w_mixed, "sp", split_axis=0, concat_axis=0, tiled=True)
    gain_one = w_local[:, part_rows, :part_rows].reshape(1, width).astype(F32)
    gain_two = w_local[:, part_rows + 1, :part_rows].reshape(1, width).astype(F32)

    lengths = doc_lengths[0]
    count = lengths.shape[0]
    before = jnp.arange(count)[None, :] < jnp.arange(count)[:, None]
    starts = jnp.sum(jnp.where(before, lengths[None, :], 0), axis=1).astype(jnp.int32)
    places = jnp.arange(group_rows, dtype=jnp.int32)
    begins = jnp.max(jnp.where(starts[None, :] <= places[:, None], starts[None, :], 0), axis=1)
    angles = (places - begins).astype(F32)[:, None] * frequencies(HD)[None, :]
    cosine_half, sine_half = jnp.cos(angles), jnp.sin(angles)
    cosine = jnp.concatenate([cosine_half] * 4, axis=1)
    sine = jnp.concatenate([-sine_half, sine_half] * 2, axis=1)
    index = jnp.asarray(block_order(shards), jnp.int32) ^ seq_rank.astype(jnp.int32)

    def attend(blocks, weights):
        gain = weights[:, part_rows, :part_rows].reshape(1, width).astype(F32)
        return attention(index, starts, blocks, gain, weights, cosine, sine, w_out, q_cols)

    half_rows = group_rows // 2

    def terms(values, weights, side, turned=False, waits=()):
        return rows_product(side, values, weights, turned, waits)

    rows_f32, rows_bf16 = ((tok_rows, width), F32), ((tok_rows, width), BF16)

    def norm_two(summed):
        outs = (rows_f32, rows_bf16, ((2, tok_rows, width), BF16))
        return small_call(norm_two_body, outs, tokens, gain_two, cotangent, *summed)

    branch_shape = ((tok_rows + 16, width), BF16)

    def norm_two_back(summed, hidden_one):
        outs = (rows_f32, branch_shape)
        return small_call(norm_two_back_body, outs, hidden_one, gain_two, cotangent, *summed)

    def norm_one_back(summed, beside, free=0):
        operands = (tokens, gain_one, beside, *summed)
        (back,) = small_call(norm_one_back_body, (rows_f32,), *operands, free=free)
        return back

    def attend_back(blocks, waits=()):
        return attention_back(
            index, starts, blocks, w_out, mixed, log_sums, out_rel, cosine, sine, waits
        )

    def to_rows(grad_mixed):
        blocks = grad_mixed.reshape(shards, part_rows, columns)
        return lax.all_to_all(blocks, "sp", split_axis=0, concat_axis=0, tiled=True)

    def grow(kind, works, began, *waits):
        cot_rows, act_rows = [work[4] for work in works], [work[3] for work in works]
        mine = [work[(1, 2, 0)[kind]] for work in works]
        if kind == 2:
            return weight_grad(mine, cot_rows, 1024, 512, waits, began)
        return weight_grad(act_rows, mine, 512, 1024, waits, began)

    dp_rank = lax.axis_index("dp").astype(jnp.int32)

    if planned:
        which = dp_rank ^ jnp.arange(1, groups, dtype=jnp.int32)
        token_gather = RowGather(tokens)
        *token_gather.moving, cosine, sine = together(*token_gather.moving, cosine, sine)
        token_gather.forward()
        token_gather.cores()
        *token_blocks, w_local = together(*token_gather.evens[1:], *token_gather.moving, w_local)
        token_blocks = [tokens] + token_blocks

        cot_gather = RowGather(after(cotangent, w_local))
        act_one, mixed, out_rel, log_sums, out_even, out_odd = attend(token_blocks, w_local)
        out_even, out_odd, *cot_gather.moving = together(
            out_even, out_odd, *cot_gather.moving
        )

        out_sum = RowSum(out_odd)
        out_sum.add_pairs(out_even)
        cot_gather.moving = [after(one, *out_sum.sent) for one in cot_gather.moving]
        cot_gather.forward()
        w_projections = after(w_local, *out_sum.sent)[:, :part_rows, :].reshape(width, columns)
        w_projections, *moving = together(w_projections, *out_sum.moving, *cot_gather.moving)
        out_sum.moving, cot_gather.moving = moving[:3], moving[3:]
        hidden_one, act_two, both = norm_two(out_sum.terms())

        act_gather = RowGather(act_two)
        both = lax.all_gather(both, ("dp", "sp"), axis=0).reshape(
            groups, shards, 2, tok_rows, width
        )
        act_gather.moving = together(*act_gather.moving)
        act_gather.forward()
        cot_gather.moving = [after(one, act_gather.sent) for one in cot_gather.moving]
        cot_gather.cores()
        act_gather.cores()
        *act_gather.moving, one, two, three, four = together(
            *act_gather.moving, *cot_gather.moving
        )
        cot_gather.moving = [one, two, three, four]

        own = ffn(act_gather.blocks(), cot_gather.blocks(), w_gate, w_up, w_down)
        back_sum = RowSum(act_back(1, own[1], own[2], w_gate, w_up, BF16))
        even_back = act_back(0, own[1], own[2], w_gate, w_up, BF16, (own[0],))
        back_sum.add_pairs(even_back)
        mlp_odd = terms(own[0], w_down, 1, False, back_sum.sent)
        grad_gate = grow(0, [own], None, mlp_odd)
        grad_up = grow(1, [own], None, grad_gate)
        grad_up, mlp_odd, *back_sum.moving = together(grad_up, mlp_odd, *back_sum.moving)
        hidden_one_back, branch = norm_two_back(back_sum.terms(), hidden_one)

        branch_gather = RowGather(branch)
        mlp_sum = RowSum(after(mlp_odd, branch))
        mlp_even = terms(own[0], w_down, 0, False, (branch,))
        grad_down = grow(2, [own], None, mlp_even)
        grad_down, mlp_even, *moving = together(
            grad_down, mlp_even, *branch_gather.moving, *mlp_sum.moving
        )
        branch_gather.moving, mlp_sum.moving = moving[:2], moving[2:]

        branch_gather.forward()
        branch_gather.cores()
        mlp_even, *branch_gather.moving = together(mlp_even, *branch_gather.moving)
        mixed_back, grad_out_terms = attend_back(branch_gather.blocks())
        grad_mixed = weight_grad([act_one], [mixed_back], 512, columns, (), None, BF16)
        mixed_sum, grad_out = lax.psum((grad_mixed, grad_out_terms), "dp")
        one_odd = terms(mixed_back, w_projections, 1, True, (grad_mixed,))
        one_sum = RowSum(one_odd)
        one_even = terms(mixed_back, w_projections, 0, True, (one_odd,))
        mlp_sum.add_pairs(after(mlp_even, one_even))
        others = ffn_others(which, both, w_gate, w_up, w_down, mlp_sum.sent)
        *others, one_even, got, one, two, three = together(
            *others, one_even, *one_sum.moving, *mlp_sum.moving
        )
        one_sum.moving, mlp_sum.moving = [got], [one, two, three]

        one_sum.add_pairs(one_even)
        grad_gate, grad_up = grad_pair(
            which,
            both,
            others[1],
            others[2],
            grad_gate,
            grad_up,
            256,
            one_sum.sent,
        )
        (layer_out,) = small_call(
            layer_out_body, (rows_bf16,), after(hidden_one, grad_gate), *mlp_sum.terms()
        )
        beside = after(hidden_one_back, layer_out)
        grad_tokens = norm_one_back(one_sum.terms(), beside, len(one_sum.moving))
        mixed_sum, grad_out, grad_tokens = together(mixed_sum, grad_out, grad_tokens)
        mixed_rows = to_rows(mixed_sum)
        grad_down = grad_others(
            which, both, 1, others[0], grad_down, 1024, 512, (mixed_sum,)
        )
        waits = (grad_down,)
    else:
        waits = ()
        w_projections = w_local[:, :part_rows, :].reshape(width, columns)
        act_one, mixed, out_rel, log_sums, out_even, out_odd = attend(gather_rel(tokens), w_local)
        hidden_one, act_two, _ = norm_two((scatter_rel(out_even, out_odd),))
        act_blocks, cot_blocks, half = gather_rel(act_two), gather_rel(cotangent), shards // 2
        own = [
            jnp.concatenate(parts, axis=0)
            for parts in zip(
                ffn(act_blocks[:half], cot_blocks[:half], w_gate, w_up, w_down),
                ffn(act_blocks[half:], cot_blocks[half:], w_gate, w_up, w_down),
                strict=True,
            )
        ]
        act_two_back = scatter_rel(
            act_back(0, own[1], own[2], w_gate, w_up, BF16),
            act_back(1, own[1], own[2], w_gate, w_up, BF16),
        )
        hidden_one_back, branch = norm_two_back((act_two_back,), hidden_one)
        mixed_back, grad_out_terms = attend_back(gather_rel(branch))
        act_one_back = scatter_rel(
            terms(mixed_back, w_projections, 0, True), terms(mixed_back, w_projections, 1, True)
        )
        mixed_rows = to_rows(lax.psum(contract(act_one, mixed_back, 0, 0).astype(BF16), "dp"))
        mlp_out = scatter_rel(terms(own[0], w_down, 0), terms(own[0], w_down, 1))
        layer_out = (hidden_one + mlp_out).astype(BF16)
        grad_tokens = norm_one_back((act_one_back,), hidden_one_back)
        grad_out, grad_gate, grad_up, grad_down = (
            lax.psum(grad.astype(BF16), "dp").astype(F32)
            for grad in (grad_out_terms, *(grow(kind, [own], None) for kind in range(3)))
        )
    grad_gain_mlp = lax.dynamic_slice(
        grad_out, (q_cols, seq_rank * part_rows), (1, part_rows)
    ).astype(F32)[0]
    if copies == 1:
        grad_query, grad_key, grad_value, products, grad_out = unpack_grads(
            mixed_rows[None], grad_out, (w_query, w_key, w_value), q_cols, waits
        )
        products = products.reshape(part_rows)
    else:
        grad_out = grad_out[:q_cols].astype(F32)
        parts = jnp.transpose(mixed_rows.astype(F32), (1, 0, 2))
        grad_query = parts[:, :, :q_cols].reshape(part_rows, shards * q_cols)
        grad_key, grad_value = (
            parts[:, :, first : first + HD]
            .reshape(part_rows, kv_total, copies, HD)
            .sum(axis=2)
            .reshape(part_rows, -1)
            for first in (q_cols, q_cols + HD)
        )
        products = sum(
            jnp.sum(weight.astype(F32) * grad, axis=1)
            for weight, grad in (
                (w_query, grad_query),
                (w_key, grad_key),
                (w_value, grad_value),
            )
        )
    grad_gain_attn = products / gain_attn.astype(F32)
    return (
        layer_out,
        grad_tokens,
        grad_query,
        grad_key,
        grad_value,
        grad_out,
        grad_gain_attn,
        grad_gain_mlp,
        grad_gate,
        grad_up,
        grad_down,
    )


def solution(mesh):
    placed = (
        P(("dp", "sp"), None),
        P("dp", None),
        P("sp", None),
        P("sp", None),
        P("sp", None),
        P("sp", None),
        P("sp"),
        P("sp"),
        P(None, "sp"),
        P(None, "sp"),
        P("sp", None),
        P(("dp", "sp"), None),
    )
    return jax.shard_map(
        on_device,
        mesh=mesh,
        in_specs=placed,
        out_specs=(
            P(("dp", "sp"), None),
            P(("dp", "sp"), None),
            P("sp", None),
            P("sp", None),
            P("sp", None),
            P("sp", None),
            P("sp"),
            P("sp"),
            P(None, "sp"),
            P(None, "sp"),
            P("sp", None),
        ),
        check_vma=False,
    )
```
